32 devices in a mesh: dp: 8 (over y, x, core), tensor: 4 (over z).
Axes of the slice: x: 2, y: 2, z: 4, core: 2. Of those that a mesh axis runs over, the one named last changes fastest.
Arguments:
- tokens: bfloat16 [11664, 1152], P('dp', 'tensor'), may hold values from -6 to 6
- cotangent: bfloat16 [11664, 1152], P('dp', 'tensor'), may hold values from -6 to 6
- adapter_index: int32 [16], P('dp'), may hold values from 0 to 7
- valid_image: int32 [16], P('dp'), may hold values 0 or 1
- first_gain: bfloat16 [1152], replicated, may hold values from 0.5 to 1.5
- first_shift: bfloat16 [1152], replicated, may hold values from -1.5 to 1.5
- triple_weight: bfloat16 [3, 1152, 1152], P(None, None, 'tensor'), may hold values from -0.1875 to 0.1875
- triple_bias: bfloat16 [3, 1152], P(None, 'tensor'), may hold values from -1.5 to 1.5
- triple_down: bfloat16 [3, 8, 1152, 16], replicated, may hold values from -0.1875 to 0.1875
- triple_up: bfloat16 [3, 8, 16, 1152], P(None, None, None, 'tensor'), may hold values from -1.5 to 1.5
- merge_weight: bfloat16 [1152, 1152], P('tensor'), may hold values from -0.75 to 0.75
- merge_bias: bfloat16 [1152], replicated, may hold values from -1.5 to 1.5
- merge_down: bfloat16 [8, 1152, 16], P(None, 'tensor'), may hold values from -0.75 to 0.75
- merge_up: bfloat16 [8, 16, 1152], replicated, may hold values from -1.5 to 1.5
- second_gain: bfloat16 [1152], replicated, may hold values from 0.4 to 8.5
- second_shift: bfloat16 [1152], replicated, may hold values from -1.5 to 1.5
- expand_weight: bfloat16 [1152, 4304], P(None, 'tensor'), may hold values from -0.1875 to 0.1875
- expand_bias: bfloat16 [4304], P('tensor'), may hold values from -1.5 to 1.5
- expand_down: bfloat16 [8, 1152, 16], replicated, may hold values from -0.1875 to 0.1875
- expand_up: bfloat16 [8, 16, 4304], P(None, None, 'tensor'), may hold values from -1.5 to 1.5
- reduce_weight: bfloat16 [4304, 1152], P('tensor'), may hold values from -0.09375 to 0.09375
- reduce_bias: bfloat16 [1152], replicated, may hold values from -1.5 to 1.5
- reduce_down: bfloat16 [8, 4304, 16], P(None, 'tensor'), may hold values from -0.09375 to 0.09375
- reduce_up: bfloat16 [8, 16, 1152], replicated, may hold values from -1.5 to 1.5
Outputs:
- layer_out: bfloat16 [11664, 1152], P('dp', 'tensor')
- tokens_grad: float32 [11664, 1152], P('dp', 'tensor')
- triple_down_grad: float32 [3, 8, 1152, 16], replicated
- triple_up_grad: float32 [3, 8, 16, 1152], P(None, None, None, 'tensor')
- merge_down_grad: float32 [8, 1152, 16], P(None, 'tensor')
- merge_up_grad: float32 [8, 16, 1152], replicated
- expand_down_grad: float32 [8, 1152, 16], replicated
- expand_up_grad: float32 [8, 16, 4304], P(None, None, 'tensor')
- reduce_down_grad: float32 [8, 4304, 16], P(None, 'tensor')
- reduce_up_grad: float32 [8, 16, 1152], replicated
The draws below stay inside these ranges and needn't reach their ends.
Inputs may be any that keep to these rules, and one draw needn't show every extreme that they name: `valid_image`: padding images carry 0.
All inputs are finite; a program needn't handle non-finite values. No bound on the sum of `valid_image` on one device may be relied on, other than what follows from the above.
Results may differ from the reference program's by a relative error of at most 0.017.
Values may be sent and summed in bfloat16 or wider, within the bound.
No kernel may reach another device: no remote copies, remote signals or barrier semaphores. Data moves between devices by JAX's collectives and lax.ppermute only.
A program may use at most 256 MiB of HBM per device.

```python
import math
import jax
import jax.numpy as jnp
from jax import lax

D = 1152
FF = 4304
HEADS = 16
HEAD_DIM = 72
RANK = 16
ADAPTERS = 8
SEQ = 729
IMAGES = 16
TOKENS = 11664


def draw_second_gain(key, part):
    key = jax.random.fold_in(key, 11)
    place = jnp.arange(D, dtype=jnp.float32) / (D - 1)
    rough = jax.random.uniform(key, (D,), jnp.float32, 0.7, 1.4)
    ramp = jnp.exp(place * jnp.log(4.0))
    return (0.7 * ramp * rough).astype(jnp.bfloat16)


def with_ends(array, key, smallest, top_value):
    spot = [jax.random.randint(jax.random.fold_in(key, axis), (), 0, length) for axis, length in enumerate(array.shape)]
    main_axis = array.shape.index(max(array.shape))
    beside = spot[:main_axis] + [(spot[main_axis] + 1) % array.shape[main_axis]] + spot[main_axis + 1:]
    return array.at[tuple(spot)].set(smallest).at[tuple(beside)].set(top_value)


def level_of(stream_key, extent, cuts, low, largest):
    factor_of, own = 1.0, jax.random.fold_in(stream_key, 6)
    for position, shards_of in cuts:
        steps = jnp.exp(jax.random.uniform(jax.random.fold_in(own, position), (shards_of,), jnp.float32, low / len(cuts), largest / len(cuts)))
        factor_of = factor_of * jnp.repeat(steps, extent[position] // shards_of).reshape([-1 if axis == position else 1 for axis in range(len(extent))])
    return factor_of


def gaussian(rng, shape, scale, limit, cuts=(), kind=jnp.bfloat16):
    level = level_of(rng, shape, cuts, -0.22, 0.18) if cuts else 1.0
    entries = jax.random.normal(rng, shape, jnp.float32) * scale * level
    return jnp.minimum(jnp.maximum(entries, -limit), limit).astype(kind)


def setup_inputs(seed: int = 0) -> dict:
    key_of = jax.random.split(jax.random.key(seed), 25)
    return {
        "tokens": gaussian(key_of[0], (TOKENS, D), 1.0, 6.0, ((0, 8), (1, 4))),
        "cotangent": gaussian(key_of[1], (TOKENS, D), 1.0, 6.0, ((0, 8), (1, 4))),
        "adapter_index": with_ends(jax.random.randint(key_of[2], (IMAGES,), 0, ADAPTERS), jax.random.fold_in(key_of[2], 1), 0, ADAPTERS - 1).astype(jnp.int32),
        "valid_image": with_ends((jax.random.randint(key_of[3], (IMAGES,), 0, 4) < 3).astype(jnp.int32), jax.random.fold_in(key_of[3], 1), 0, 1),
        "first_gain": jnp.clip(1.0 + 0.1 * jax.random.normal(key_of[4], (D,), jnp.float32), 0.5, 1.5).astype(jnp.bfloat16),
        "first_shift": gaussian(key_of[5], (D,), 0.3, 1.5),
        "triple_weight": gaussian(key_of[6], (3, D, D), D ** -0.5, 0.1875, ((2, 4),)),
        "triple_bias": gaussian(key_of[7], (3, D), 0.3, 1.5, ((1, 4),)),
        "triple_down": gaussian(key_of[8], (3, ADAPTERS, D, RANK), D ** -0.5, 0.1875),
        "triple_up": gaussian(key_of[9], (3, ADAPTERS, RANK, D), RANK ** -0.5, 1.5, ((3, 4),)),
        "merge_weight": gaussian(key_of[10], (D, D), (D // 16) ** -0.5, 0.75, ((0, 4),)),
        "merge_bias": gaussian(key_of[11], (D,), 0.3, 1.5),
        "merge_down": gaussian(key_of[12], (ADAPTERS, D, RANK), (D // 16) ** -0.5, 0.75, ((1, 4),)),
        "merge_up": gaussian(key_of[13], (ADAPTERS, RANK, D), RANK ** -0.5, 1.5),
        "second_gain": draw_second_gain(jax.random.fold_in(key_of[24], 71), 0),
        "second_shift": gaussian(key_of[15], (D,), 0.3, 1.5),
        "expand_weight": gaussian(key_of[16], (D, FF), D ** -0.5, 0.1875, ((1, 4),)),
        "expand_bias": gaussian(key_of[17], (FF,), 0.3, 1.5, ((0, 4),)),
        "expand_down": gaussian(key_of[18], (ADAPTERS, D, RANK), D ** -0.5, 0.1875),
        "expand_up": gaussian(key_of[19], (ADAPTERS, RANK, FF), RANK ** -0.5, 1.5, ((2, 4),)),
        "reduce_weight": gaussian(key_of[20], (FF, D), FF ** -0.5, 0.09375, ((0, 4),)),
        "reduce_bias": gaussian(key_of[21], (D,), 0.3, 1.5),
        "reduce_down": gaussian(key_of[22], (ADAPTERS, FF, RANK), FF ** -0.5, 0.09375, ((1, 4),)),
        "reduce_up": gaussian(key_of[23], (ADAPTERS, RANK, D), RANK ** -0.5, 1.5),
    }


@jax.custom_vjp
def low(v):
    return lax.optimization_barrier(v.astype(jnp.bfloat16)).astype(jnp.float32)

@jax.custom_vjp
def low_back(v):
    return v

def low_keep(v):
    return (low(v), None)

def low_pass(kept, grad):
    return (grad,)

def back_keep(v):
    return (v, None)

def back_low(kept, grad):
    return (low(grad),)
low.defvjp(low_keep, low_pass)
low_back.defvjp(back_keep, back_low)
eps = 1e-06
adapter_scale = 0.5
highest = lax.Precision.HIGHEST

def product(left, right):
    return jnp.dot(left, right, precision=highest)

def norm_rows(rows, gain, shift):
    center = rows - lax.optimization_barrier(jnp.mean(rows, -1, keepdims=True))
    scaled = lax.rsqrt(lax.optimization_barrier(jnp.mean(center * center, -1, keepdims=True)) + eps)
    return center * scaled * gain + shift

def adapted(inputs, weight, down_map, up_map):
    return product(inputs, weight) + adapter_scale * product(product(inputs, down_map), up_map)

def image_layer(frozen, adapters, image, index):
    first_gain, first_shift, triple_weight, triple_bias, merge_weight, merge_bias, second_gain, second_shift, expand_weight, expand_bias, reduce_weight, reduce_bias = frozen
    triple_down, triple_up, merge_down, merge_up, expand_down, expand_up, reduce_down, reduce_up = adapters
    normed = low(norm_rows(image, first_gain, first_shift))
    pieces = []
    for which in range(3):
        value = adapted(normed, triple_weight[which], triple_down[which, index], triple_up[which, index]) + triple_bias[which]
        pieces.append(low(low_back(value)).reshape(SEQ, HEADS, HEAD_DIM))
    scores = low_back(jnp.einsum('qhd,khd->hqk', pieces[0], pieces[1], precision=highest) / math.sqrt(HEAD_DIM))
    attn_weights = low(jax.nn.softmax(scores, axis=-1))
    heads = low_back(low(jnp.einsum('hqk,khd->qhd', attn_weights, pieces[2], precision=highest))).reshape(SEQ, D)
    hidden = image + low_back(adapted(heads, merge_weight, merge_down[index], merge_up[index]) + merge_bias)
    normed_two = low(norm_rows(hidden, second_gain, second_shift))
    pre_act = low_back(adapted(normed_two, expand_weight, expand_down[index], expand_up[index]) + expand_bias)
    activated = low(jax.nn.gelu(pre_act, approximate=True))
    return hidden + low_back(adapted(activated, reduce_weight, reduce_down[index], reduce_up[index]) + reduce_bias)

def reference(tokens, cotangent, adapter_index, valid_image, first_gain, first_shift, triple_weight, triple_bias, triple_down, triple_up, merge_weight, merge_bias, merge_down, merge_up, second_gain, second_shift, expand_weight, expand_bias, expand_down, expand_up, reduce_weight, reduce_bias, reduce_down, reduce_up):
    frozen = tuple((entry.astype(jnp.float32) for entry in (first_gain, first_shift, triple_weight, triple_bias, merge_weight, merge_bias, second_gain, second_shift, expand_weight, expand_bias, reduce_weight, reduce_bias)))
    adapters = tuple((entry.astype(jnp.float32) for entry in (triple_down, triple_up, merge_down, merge_up, expand_down, expand_up, reduce_down, reduce_up)))
    images = tokens.astype(jnp.float32).reshape(IMAGES, SEQ, D)

    def forward(images, adapters):

        def single(element):
            return image_layer(frozen, adapters, element[0], element[1])
        return lax.map(jax.checkpoint(single), (images, adapter_index))
    result, pullback = jax.vjp(forward, images, adapters)
    weight = valid_image.astype(jnp.float32)[:, None, None]
    start_grad = cotangent.astype(jnp.float32).reshape(IMAGES, SEQ, D) * weight
    grad_images, grads = pullback(start_grad)
    return (result.reshape(TOKENS, D).astype(jnp.bfloat16), grad_images.reshape(TOKENS, D), grads[0], grads[1], grads[2], grads[3], grads[4], grads[5], grads[6], grads[7])
```

```python
import math
from functools import partial

import jax
import jax.numpy as jnp
from jax import lax
from jax.experimental import pallas as pl
from jax.experimental.pallas import tpu as pltpu
from jax.sharding import PartitionSpec as P

HEAD_DIM = 72
HEAD_PAD = 80
LANES = 128
CHUNK = 256
EPS = 1e-06
BF = jnp.bfloat16
F32 = jnp.float32
SCALE = 1.0 / math.sqrt(HEAD_DIM)
LOG2E = 1.4426950408889634
MIB = 1024 * 1024

NN = (((1,), (0,)), ((), ()))
NT = (((1,), (1,)), ((), ()))
TN = (((0,), (0,)), ((), ()))


def mm(a, b, dims=NN):
    return lax.dot_general(a, b, dims, preferred_element_type=F32)


def up_to(value, step):
    return -(-value // step) * step


def attend_kernel(seq, slots, groups, tok_ref, norm_ref, down_ref, upx_ref, *rest):
    weights = rest[:slots]
    qkv_ref, n1_ref, stats_ref, lse_ref, inner_ref, heads_ref, rows_ref = rest[slots : slots + 7]
    (scr,) = rest[slots + 7 :]
    parts, width, span = tok_ref.shape
    dim = parts * width
    head_rows = upx_ref.shape[2] // 3
    heads_here = head_rows // HEAD_DIM
    block = span // groups

    def norm_step(c, carry):
        cols = pl.ds(pl.multiple_of(c * LANES, LANES), LANES)
        x = tok_ref[:, :, cols].reshape(dim, LANES).astype(F32)
        mean = jnp.mean(x, 0, keepdims=True)
        center = x - mean
        rstd = lax.rsqrt(jnp.mean(center * center, 0, keepdims=True) + EPS)
        n1 = center * rstd * norm_ref[:, 0:1] + norm_ref[:, 1:2]
        n1_ref[:, cols] = n1.astype(BF)
        stats_ref[0:1, cols] = mean
        stats_ref[1:2, cols] = rstd
        return carry

    lax.fori_loop(0, span // LANES, norm_step, 0)
    stats_ref[2:8, :] = jnp.zeros((6, span), F32)

    def proj_step(c, carry):
        start = pl.multiple_of(c * CHUNK, CHUNK)
        cols = pl.ds(start, CHUNK)
        n1 = n1_ref[:, cols]
        rank = down_ref.shape[0]
        inner = mm(down_ref[...], n1)
        line = lax.broadcasted_iota(jnp.int32, (rank, CHUNK), 0)
        inner_x = jnp.where(line == 48, 1.0, 0.5 * inner).astype(BF)
        inner_ref[:, cols] = inner_x
        spot = lax.broadcasted_iota(jnp.int32, (HEAD_PAD - HEAD_DIM, CHUNK), 0)
        place = start + lax.broadcasted_iota(jnp.int32, (HEAD_PAD - HEAD_DIM, CHUNK), 1)
        tails = (
            jnp.where(spot == 0, 1.0, 0.0),
            jnp.where((spot == 0) & (place >= seq), -1e30, 0.0),
            jnp.zeros((HEAD_PAD - HEAD_DIM, CHUNK), F32),
        )
        for k in range(slots):
            proj = mm(weights[k][0 : 3 * head_rows, :], n1) + mm(upx_ref[k], inner_x, TN)
            for j in range(3):
                for h in range(heads_here):
                    at = j * head_rows + h * HEAD_DIM
                    piece = jnp.concatenate([proj[at : at + HEAD_DIM, :], tails[j]], 0)
                    qkv_ref[j, k * heads_here + h, :, cols] = piece.astype(BF)
        return carry

    lax.fori_loop(0, span // CHUNK, proj_step, 0)

    def head_step(h, carry):
        keys = qkv_ref[1, h].T
        vals = qkv_ref[2, h]
        row = pl.multiple_of(h * HEAD_DIM, 8)
        for c in range(span // CHUNK):
            cols = slice(c * CHUNK, (c + 1) * CHUNK)
            scores = mm(keys, qkv_ref[0, h, :, cols]) * (SCALE * LOG2E)
            top = jnp.max(scores, 0, keepdims=True)
            raised = jnp.exp2(scores - top)
            total = jnp.sum(raised, 0, keepdims=True)
            out = mm(vals, raised.astype(BF)) / total
            scr[pl.ds(row, HEAD_DIM), cols] = out[0:HEAD_DIM, :]
            lse_ref[pl.ds(h, 1), 0:1, cols] = (top + jnp.log2(total)).reshape(1, 1, CHUNK)
        return carry

    lax.fori_loop(0, slots * heads_here, head_step, 0)
    for g in range(groups):
        cols = slice(g * block, (g + 1) * block)
        rows_ref[g] = tok_ref[:, :, cols].reshape(dim, block)
        for k in range(slots):
            heads_ref[g, k] = scr[k * head_rows : (k + 1) * head_rows, cols].astype(BF)


def attend(seq, groups, tok, norm, down, upx, weights):
    parts, width, span = tok.shape
    slots = len(weights)
    head_rows = upx.shape[2] // 3
    heads = slots * head_rows // HEAD_DIM
    dim = parts * width
    out = (
        jax.ShapeDtypeStruct((3, heads, HEAD_PAD, span), BF),
        jax.ShapeDtypeStruct((dim, span), BF),
        jax.ShapeDtypeStruct((8, span), F32),
        jax.ShapeDtypeStruct((heads, 1, span), F32),
        jax.ShapeDtypeStruct((down.shape[0], span), BF),
        jax.ShapeDtypeStruct((groups, slots, head_rows, span // groups), BF),
        jax.ShapeDtypeStruct((groups, dim, span // groups), BF),
    )
    return pl.pallas_call(
        partial(attend_kernel, seq, slots, groups),
        out_shape=out,
        in_specs=[pl.BlockSpec(memory_space=pltpu.VMEM)] * (4 + slots),
        out_specs=tuple(pl.BlockSpec(memory_space=pltpu.VMEM) for _ in out),
        scratch_shapes=[pltpu.VMEM((slots * head_rows, span), F32)],
        compiler_params=pltpu.CompilerParams(vmem_limit_bytes=48 * MIB),
        cost_estimate=pl.CostEstimate(flops=8 * 10**9, bytes_accessed=16 * 10**6, transcendentals=5 * 10**6),
        name="attend",
    )(tok, norm, down, upx, *weights)


def middle_kernel(
    sc,
    heads_ref,
    rows_ref,
    cot_ref,
    fac_ref,
    vec_ref,
    tab_ref,
    merge_hbm,
    mlp_hbm,
    pair_ref,
    back_ref,
    gm_ref,
    we,
    wr,
    wm,
    heads_in,
    acc_out,
    acc_back,
    n2x,
    gx,
    eug,
    rdg,
    sem,
):
    groups, slots, head_rows, block = heads_ref.shape
    parts = cot_ref.shape[0]
    dim = parts * head_rows
    hidden_rows = fac_ref.shape[3]
    full = parts * hidden_rows
    tail = slice(dim, dim + LANES)
    mine, member, valid = sc[0], sc[1], sc[2]

    copies = []
    for t in range(parts):
        copies.append(
            pltpu.make_async_copy(
                merge_hbm.at[t, pl.ds(0, head_rows), :],
                wm.at[pl.ds(t * head_rows, head_rows), pl.ds(0, dim)],
                sem.at[0, t],
            )
        )
    for t in range(parts):
        for which, dest in ((0, we), (1, wr)):
            copies.append(
                pltpu.make_async_copy(
                    mlp_hbm.at[t, pl.ds(which * hidden_rows, hidden_rows), :],
                    dest.at[pl.ds(t * hidden_rows, hidden_rows), pl.ds(0, dim)],
                    sem.at[1 + which, t],
                )
            )
    for copy in copies:
        copy.start()

    for s in range(groups):
        for k in range(slots):
            heads_in[s + groups * lax.rem(mine + k, slots)] = heads_ref[s, k]
    heads_t = heads_in[...].reshape(dim, block)
    heads = heads_t.T
    grads = cot_ref[...].reshape(dim, block).T * valid.astype(F32).astype(BF)

    for t in range(parts):
        fac = fac_ref[t, mine]
        spread = jnp.concatenate(
            [fac[0:16, :], fac[48:64, :], jnp.zeros((LANES - 32, hidden_rows), BF)], 0
        )
        we[t * hidden_rows : (t + 1) * hidden_rows, tail] = spread.T
        spread = jnp.concatenate([fac[16:32, :], jnp.zeros((LANES - 16, hidden_rows), BF)], 0)
        wr[t * hidden_rows : (t + 1) * hidden_rows, tail] = spread.T
        spread = jnp.concatenate(
            [fac[32:48, 0:head_rows], jnp.zeros((LANES - 16, head_rows), BF)], 0
        )
        wm[t * head_rows : (t + 1) * head_rows, tail] = spread.T

    for copy in copies[:parts]:
        copy.wait()
    merged = mm(heads, wm[...])
    inner_m = (0.5 * merged[:, tail]).astype(BF)
    x = rows_ref[member].T.astype(F32)
    hidden = x + merged[:, :dim] + mm(inner_m, tab_ref[0]) + vec_ref[0:1, :]
    mean = jnp.mean(hidden, 1, keepdims=True)
    center = hidden - mean
    rstd = lax.rsqrt(jnp.mean(center * center, 1, keepdims=True) + EPS)
    unit = center * rstd
    n2 = (unit * vec_ref[2:3, :] + vec_ref[3:4, :]).astype(BF)
    n2x[:, 0:dim] = n2
    lane = lax.broadcasted_iota(jnp.int32, (block, LANES), 1)
    inner_e = jnp.where(lane == 16, 1.0, 0.5 * mm(n2, tab_ref[1], NT)).astype(BF)
    n2x[:, tail] = inner_e
    gx[:, 0:dim] = grads
    thr_r = (0.5 * mm(grads, tab_ref[2], NT)).astype(BF)
    gx[:, tail] = thr_r
    inner_et = inner_e.T
    thr_rt = thr_r.T
    acc_out[...] = jnp.zeros_like(acc_out)
    acc_back[...] = jnp.zeros_like(acc_back)
    for copy in copies[parts:]:
        copy.wait()

    def step(c, carry):
        at = pl.ds(pl.multiple_of(c * CHUNK, CHUNK), CHUNK)
        we_c = we[at, :]
        wr_c = wr[at, :]
        pre = mm(n2x[...], we_c, NT)
        grad_act = mm(gx[...], wr_c, NT)
        square = pre * pre
        th = jnp.tanh(pre * (0.7978845608028654 + 0.035677408136300125 * square))
        half = 0.5 * (1.0 + th)
        act = (pre * half).astype(BF)
        slope = half + pre * (0.5 * (1.0 - th * th)) * (
            0.7978845608028654 + 0.10703222440890037 * square
        )
        grad_pre = (grad_act * slope).astype(BF)
        acc_out[...] += mm(act, wr_c)
        acc_back[...] += mm(grad_pre, we_c)
        eug[:, at] = mm(inner_et[0:16, :], grad_pre)
        rdg[:, at] = mm(thr_rt[0:16, :], act)
        return carry

    lax.fori_loop(0, full // CHUNK, step, 0)

    inner_r = (0.5 * acc_out[:, tail]).astype(BF)
    layer = hidden + acc_out[:, 0:dim] + mm(inner_r, tab_ref[2]) + vec_ref[1:2, :]
    thr_e = (0.5 * acc_back[:, tail]).astype(BF)
    scaled = (acc_back[:, 0:dim] + mm(thr_e, tab_ref[1])) * vec_ref[2:3, :]
    first = jnp.mean(scaled, 1, keepdims=True)
    second = jnp.mean(scaled * unit, 1, keepdims=True)
    grad_hidden = grads.astype(F32) + rstd * (scaled - first - unit * second)
    branch = grad_hidden.astype(BF)
    thr_m = (0.5 * mm(branch, tab_ref[0], NT)).astype(BF)
    grad_heads = mm(branch, wm[:, 0:dim], NT) + mm(thr_m, wm[:, tail], NT)
    grad_heads_t = grad_heads.T.astype(BF)
    layer_t = layer.T.astype(BF)
    hidden_t = grad_hidden.T.astype(BF)
    for t in range(parts):
        at = slice(t * head_rows, (t + 1) * head_rows)
        pair_ref[t, 0] = layer_t[at, :]
        pair_ref[t, 1] = hidden_t[at, :]
        back_ref[t % groups, lax.rem(t // groups - mine + slots, slots)] = grad_heads_t[at, :]

    whole = (
        mm(thr_m, heads, TN)[0:16, :],
        mm(inner_m, branch, TN)[0:16, :],
        mm(thr_e, n2, TN)[0:16, :],
        mm(inner_r, grads, TN)[0:16, :],
    )
    for t in range(parts):
        at = slice(t * hidden_rows, (t + 1) * hidden_rows)
        gm_ref[t, :, 0:hidden_rows] = eug[:, at].astype(BF)
        gm_ref[t, :, hidden_rows : 2 * hidden_rows] = rdg[:, at].astype(BF)
        for n in range(4):
            off = 2 * hidden_rows + n * head_rows
            gm_ref[t, :, off : off + head_rows] = whole[n][
                :, t * head_rows : (t + 1) * head_rows
            ].astype(BF)


def middle(scalars, heads, rows, cot, fac, vec, tab, merge, mlp):
    groups, slots, head_rows, block = heads.shape
    parts = cot.shape[0]
    dim = parts * head_rows
    hidden_rows = fac.shape[3]
    full = parts * hidden_rows
    out = (
        jax.ShapeDtypeStruct((parts, 2, head_rows, block), BF),
        jax.ShapeDtypeStruct((groups, slots, head_rows, block), BF),
        jax.ShapeDtypeStruct((parts, 16, 2 * hidden_rows + 4 * head_rows), BF),
    )
    vmem = pl.BlockSpec(memory_space=pltpu.VMEM)
    return pl.pallas_call(
        middle_kernel,
        out_shape=out,
        in_specs=[pl.BlockSpec(memory_space=pltpu.SMEM)]
        + [vmem] * 6
        + [pl.BlockSpec(memory_space=pl.ANY)] * 2,
        out_specs=tuple(vmem for _ in out),
        scratch_shapes=[
            pltpu.VMEM((full, dim + LANES), BF),
            pltpu.VMEM((full, dim + LANES), BF),
            pltpu.VMEM((dim, dim + LANES), BF),
            pltpu.VMEM((parts, head_rows, block), BF),
            pltpu.VMEM((block, dim + LANES), F32),
            pltpu.VMEM((block, dim + LANES), F32),
            pltpu.VMEM((block, dim + LANES), BF),
            pltpu.VMEM((block, dim + LANES), BF),
            pltpu.VMEM((16, full), F32),
            pltpu.VMEM((16, full), F32),
            pltpu.SemaphoreType.DMA((3, parts)),
        ],
        compiler_params=pltpu.CompilerParams(vmem_limit_bytes=60 * MIB),
        cost_estimate=pl.CostEstimate(flops=20 * 10**9, bytes_accessed=30 * 10**6, transcendentals=2 * 10**6),
        name="middle",
    )(scalars, heads, rows, cot, fac, vec, tab, merge, mlp)


def back_kernel(
    slots, sc, tok_ref, norm_ref, down_ref, upx_ref, qkv_ref, n1_ref, stats_ref, lse_ref,
    inner_ref, dout_ref, *rest,
):
    weights = rest[:slots]
    (out_ref,) = rest[slots : slots + 1]
    dot_scr, grad_scr, gb_scr, e1_scr, tu_scr = rest[slots + 1 :]
    parts, width, span = tok_ref.shape
    dim = parts * width
    groups, _, head_rows, block = dout_ref.shape
    heads_here = head_rows // HEAD_DIM
    mine, member = sc[0], sc[1]
    rank = down_ref.shape[0]

    pad = jnp.zeros((HEAD_PAD - HEAD_DIM, block), F32)
    for g in range(groups):
        cols = slice(g * block, (g + 1) * block)
        for k in range(slots):
            piece = dout_ref[g, k].astype(F32)
            for h in range(heads_here):
                one = jnp.concatenate([piece[h * HEAD_DIM : (h + 1) * HEAD_DIM, :], pad], 0)
                dot_scr[k * heads_here + h, :, cols] = one.astype(BF)

    def head_step(h, carry):
        query_t = qkv_ref[0, h]
        keys_t = qkv_ref[1, h]
        query = query_t.T
        keys = keys_t.T
        vals = qkv_ref[2, h].T
        dout_t = dot_scr[h]
        dout = dout_t.T
        dvals = jnp.zeros((span, HEAD_PAD), F32)
        dkeys = jnp.zeros((span, HEAD_PAD), F32)
        slot = h // heads_here
        row = pl.multiple_of(lax.rem(h, heads_here) * HEAD_DIM, 8)
        for c in range(span // CHUNK):
            cols = slice(c * CHUNK, (c + 1) * CHUNK)
            scores = mm(keys, query_t[:, cols]) * (SCALE * LOG2E)
            probs = jnp.exp2(scores - lse_ref[h, 0:1, cols])
            dprobs = mm(vals, dout_t[:, cols])
            delta = jnp.sum(probs * dprobs, 0, keepdims=True)
            dscores = (probs * (dprobs - delta)).astype(BF)
            dvals += mm(probs.astype(BF), dout[cols, :])
            dkeys += mm(dscores, query[cols, :])
            dquery = mm(keys_t, dscores) * SCALE
            grad_scr[slot, pl.ds(row, HEAD_DIM), cols] = dquery[0:HEAD_DIM, :]
        row = pl.multiple_of(row + head_rows, 8)
        grad_scr[slot, pl.ds(row, HEAD_DIM), :] = (dkeys * SCALE).T[0:HEAD_DIM, :]
        row = pl.multiple_of(row + head_rows, 8)
        grad_scr[slot, pl.ds(row, HEAD_DIM), :] = dvals.T[0:HEAD_DIM, :]
        return carry

    lax.fori_loop(0, slots * heads_here, head_step, 0)

    thr = jnp.zeros((rank, span), F32)
    spread = 3 * head_rows
    row_of = lax.broadcasted_iota(jnp.int32, (rank, spread), 0) // 16
    part_of = lax.broadcasted_iota(jnp.int32, (rank, spread), 1) // head_rows
    for k in range(slots):
        gb_scr[k] = grad_scr[k].astype(BF)
        thr = thr + mm(upx_ref[k], gb_scr[k])
        ups = mm(inner_ref[...], gb_scr[k], NT)
        ups = jnp.where(row_of == part_of, ups, 0.0)
        tu_scr[k] = ups[0:16, :] + ups[16:32, :] + ups[32:48, :]
    line = lax.broadcasted_iota(jnp.int32, (rank, span), 0)
    thr_b = jnp.where(line < 48, 0.5 * thr, 0.0).astype(BF)
    downs = mm(thr_b, n1_ref[...], NT)

    def final_step(c, carry):
        cols = pl.ds(pl.multiple_of(c * CHUNK, CHUNK), CHUNK)
        total = mm(weights[0][0:spread, :], gb_scr[0, :, cols], TN)
        for k in range(1, slots):
            total = total + mm(weights[k][0:spread, :], gb_scr[k, :, cols], TN)
        e1_scr[:, cols] = total
        return carry

    lax.fori_loop(0, span // CHUNK, final_step, 0)
    e1 = (e1_scr[...] + mm(down_ref[...], thr_b, TN)) * norm_ref[:, 0:1]
    first = jnp.sum(e1, 0, keepdims=True)
    mean, rstd = stats_ref[0:1, :], stats_ref[1:2, :]
    unit = (tok_ref[...].reshape(dim, span).astype(F32) - mean) * rstd
    second = jnp.sum(e1 * unit, 0, keepdims=True)
    lines = []
    for value in (first, second, mean, rstd):
        high = value.astype(BF).astype(F32)
        lines += [high, value - high]
    lines = jnp.concatenate(lines + [jnp.zeros((8, span), F32)], 0).astype(BF)
    for t in range(parts):
        out_ref[t, 0:width, :] = e1[t * width : (t + 1) * width, :].astype(BF)
        out_ref[t, width : width + 16, :] = lines
        own = jnp.where(member == t % groups, 1.0, 0.0)
        ups = tu_scr[lax.rem(t // groups - mine + slots, slots)] * own
        ups = jnp.concatenate([ups[:, j * head_rows : (j + 1) * head_rows] for j in range(3)], 0)
        down_part = downs[0:48, t * width : (t + 1) * width]
        rest_cols = span - width - head_rows
        out_ref[t, width + 16 : width + 64, :] = jnp.concatenate(
            [down_part, ups, jnp.zeros((48, rest_cols), F32)], 1
        ).astype(BF)


def attend_back(scalars, tok, norm, down, upx, qkv, n1, stats, lse, inner, dout, weights):
    parts, width, span = tok.shape
    slots = len(weights)
    head_rows = upx.shape[2] // 3
    heads = slots * head_rows // HEAD_DIM
    dim = parts * width
    return pl.pallas_call(
        partial(back_kernel, slots),
        out_shape=jax.ShapeDtypeStruct((parts, width + 64, span), BF),
        in_specs=[pl.BlockSpec(memory_space=pltpu.SMEM)]
        + [pl.BlockSpec(memory_space=pltpu.VMEM)] * (10 + slots),
        out_specs=pl.BlockSpec(memory_space=pltpu.VMEM),
        scratch_shapes=[
            pltpu.VMEM((heads, HEAD_PAD, span), BF),
            pltpu.VMEM((slots, 3 * head_rows, span), F32),
            pltpu.VMEM((slots, 3 * head_rows, span), BF),
            pltpu.VMEM((dim, span), F32),
            pltpu.VMEM((slots, 16, 3 * head_rows), F32),
        ],
        compiler_params=pltpu.CompilerParams(vmem_limit_bytes=56 * MIB),
        cost_estimate=pl.CostEstimate(flops=12 * 10**9, bytes_accessed=20 * 10**6, transcendentals=5 * 10**6),
        name="attend_back",
    )(scalars, tok, norm, down, upx, qkv, n1, stats, lse, inner, dout, *weights)


def shards(
    tokens,
    cotangent,
    adapter_index,
    valid_image,
    first_gain,
    first_shift,
    triple_weight,
    triple_bias,
    triple_down,
    triple_up,
    merge_weight,
    merge_bias,
    merge_down,
    merge_up,
    second_gain,
    second_shift,
    expand_weight,
    expand_bias,
    expand_down,
    expand_up,
    reduce_weight,
    reduce_bias,
    reduce_down,
    reduce_up,
    *,
    parts,
    copies,
):
    slots = adapter_index.shape[0]
    groups = parts // slots
    seq = tokens.shape[0] // slots
    width = tokens.shape[1]
    dim = width * parts
    head_rows = triple_weight.shape[2]
    adapters = triple_down.shape[1]
    span = up_to(seq, CHUNK)
    block = span // groups
    place = lax.axis_index("tensor")
    row = lax.axis_index("dp")
    mine, member = place // groups, place % groups
    index = lax.dynamic_index_in_dim(adapter_index, mine, 0, False)
    valid = lax.dynamic_index_in_dim(valid_image, mine, 0, False)
    all_index = lax.all_gather(adapter_index, "dp", tiled=True)
    scalars = jnp.stack([mine, member, valid]).astype(jnp.int32)

    def hop(x, step):
        return lax.ppermute(x, "tensor", [(s, (s + step) % parts) for s in range(parts)])

    def swap(x):
        pieces = [lax.dynamic_index_in_dim(x, place, 0, False)]
        for k in range(1, parts):
            pieces.append(hop(lax.dynamic_index_in_dim(x, (place + k) % parts, 0, False), k))
        stacked = jnp.stack(pieces)
        return jnp.stack(
            [lax.dynamic_index_in_dim(stacked, (place - s) % parts, 0, False) for s in range(parts)]
        )

    def images_of(x):
        flat = x.T
        return jnp.stack(
            [
                jnp.pad(flat[:, n * seq : (n + 1) * seq], ((0, 0), (0, span - seq)))
                for n in range(slots)
            ]
        )

    def pick(table, axis=0):
        return lax.dynamic_index_in_dim(table, index, axis, False)

    tok = lax.all_to_all(jnp.repeat(images_of(tokens), groups, 0), "tensor", 0, 0)

    flat_triple = triple_weight.transpose(0, 2, 1).reshape(3 * head_rows, dim)
    piece_rows = up_to(3 * head_rows, 16 * copies) // copies
    padded = jnp.pad(flat_triple, ((0, piece_rows * copies - 3 * head_rows), (0, 0)))
    my_piece = lax.dynamic_slice_in_dim(padded, row * piece_rows, piece_rows, 0)
    weights = [flat_triple]
    for k in range(1, slots):
        got = hop(my_piece, -groups * k)
        weights.append(lax.all_gather(got, "dp", tiled=True))

    def up_pack(which):
        table = lax.dynamic_index_in_dim(triple_up, which, 1, False)
        lines = [
            jnp.pad(table[j], ((0, 0), (j * head_rows, (2 - j) * head_rows))) for j in range(3)
        ]
        bias = jnp.pad(triple_bias.reshape(1, 3 * head_rows), ((0, 15), (0, 0)))
        return jnp.concatenate(lines + [bias], 0)

    ups = [up_pack(index)]
    for k in range(1, slots):
        there = lax.dynamic_index_in_dim(adapter_index, (mine - k) % slots, 0, False)
        ups.append(hop(up_pack(there), -groups * k))
    upx = jnp.stack(ups)
    down = jnp.pad(pick(triple_down, 1).transpose(0, 2, 1).reshape(48, dim), ((0, 16), (0, 0)))
    norm = jnp.pad(jnp.stack([first_gain, first_shift], 1).astype(F32), ((0, 0), (0, 6)))

    merge_rows = up_to(width, 16 * copies) // copies
    merge_piece = lax.dynamic_slice_in_dim(
        jnp.pad(merge_weight, ((0, merge_rows * copies - width), (0, 0))), row * merge_rows, merge_rows, 0
    )
    merge_all = lax.all_gather(merge_piece, ("tensor", "dp")).reshape(parts, merge_rows * copies, dim)
    hidden_here = reduce_weight.shape[0]
    hidden_rows = up_to(hidden_here, 8 * copies)
    extra = ((0, hidden_rows - hidden_here), (0, 0))
    both = jnp.concatenate([jnp.pad(expand_weight.T, extra), jnp.pad(reduce_weight, extra)], 0)
    mlp_rows = 2 * hidden_rows // copies
    mlp_piece = lax.dynamic_slice_in_dim(both, row * mlp_rows, mlp_rows, 0)
    mlp_all = lax.all_gather(mlp_piece, ("tensor", "dp")).reshape(parts, 2 * hidden_rows, dim)

    def factor_pack(which):
        def lanes(x):
            return jnp.pad(x, ((0, 16 - x.shape[0]), (0, hidden_rows - x.shape[1])))

        return jnp.concatenate(
            [
                lanes(lax.dynamic_index_in_dim(expand_up, which, 0, False)),
                lanes(lax.dynamic_index_in_dim(reduce_down, which, 0, False).T),
                lanes(lax.dynamic_index_in_dim(merge_down, which, 0, False).T),
                lanes(expand_bias[None, :]),
            ],
            0,
        )

    fac = lax.all_gather(jnp.stack([factor_pack(adapter_index[n]) for n in range(slots)]), "tensor")
    tab = jnp.stack(
        [
            jnp.pad(x, ((0, LANES - 16), (0, 0)))
            for x in (pick(merge_up), pick(expand_down).T, pick(reduce_up))
        ]
    )
    vec = jnp.pad(
        jnp.stack([merge_bias, reduce_bias, second_gain, second_shift]).astype(F32), ((0, 4), (0, 0))
    )

    cot = images_of(cotangent).reshape(slots, width, groups, block).transpose(0, 2, 1, 3)
    cot = swap(cot.reshape(parts, width, block))

    group_list = [[n * groups + g for g in range(groups)] for n in range(slots)]

    def trade(x):
        return lax.all_to_all(x, "tensor", 0, 0, axis_index_groups=group_list)

    qkv, n1, stats, lse, inner, heads, rows = attend(seq, groups, tok, norm, down, upx, weights)
    heads = trade(heads)
    pair, back, gm = middle(scalars, heads, rows, cot, fac, vec, tab, merge_all, mlp_all)
    dout = trade(back)
    pair = swap(pair)
    gm = swap(gm)
    last = attend_back(scalars, tok, norm, down, upx, qkv, n1, stats, lse, inner, dout, weights)
    last = lax.all_to_all(last, "tensor", 0, 0)

    def to_rows(image_parts):
        return jnp.concatenate([x[:, :seq] for x in image_parts], 1).T

    def whole_image(x):
        return x.reshape(slots, groups, width, block).transpose(0, 2, 1, 3).reshape(slots, width, span)

    layer = to_rows(whole_image(pair[:, 0])).astype(BF)
    residual = whole_image(pair[:, 1]).astype(F32)
    last = last.reshape(slots, groups, width + 64, span).astype(F32)
    summed = jnp.sum(last, 1)
    mine_t = images_of(tokens).astype(F32)
    one = last[:, 0]

    def line(source, n):
        at = width + 2 * n
        return source[:, at : at + 1, :] + source[:, at + 1 : at + 2, :]

    first, second = line(summed, 0), line(summed, 1)
    mean, rstd = line(one, 2), line(one, 3)
    unit = (mine_t - mean) * rstd
    grad = residual + rstd * (summed[:, :width] - first / dim - unit * (second / dim))
    tokens_grad = to_rows(grad)

    one_hot = (all_index[:, None] == jnp.arange(adapters, dtype=jnp.int32)[None, :]).astype(BF)

    def by_adapter(terms):
        gathered = lax.all_gather(terms.astype(BF), "dp", tiled=True)
        flat = gathered.reshape(gathered.shape[0], -1)
        summed = lax.dot_general(one_hot, flat, TN, preferred_element_type=F32)
        return summed.reshape((adapters,) + terms.shape[1:])

    gm = jnp.sum(gm.reshape(slots, groups, 16, gm.shape[2]).astype(F32), 1)
    gm = by_adapter(gm)
    off = 2 * hidden_rows
    expand_up_grad = gm[:, :, :hidden_here]
    reduce_down_grad = gm[:, :, hidden_rows : hidden_rows + hidden_here].transpose(0, 2, 1)
    merge_down_grad = gm[:, :, off : off + width].transpose(0, 2, 1)
    held = lax.all_gather(gm[:, :, off + width :].astype(BF), "tensor").astype(F32)
    held = held.reshape(parts, adapters, 16, 3, width).transpose(3, 1, 2, 0, 4)
    held = held.reshape(3, adapters, 16, dim)
    merge_up_grad = held[0]
    expand_down_grad = held[1].transpose(0, 2, 1)
    reduce_up_grad = held[2]

    gt = by_adapter(summed[:, width + 16 : width + 64, : width + head_rows])
    triple_up_grad = gt[:, :, width:].reshape(adapters, 3, 16, head_rows).transpose(1, 0, 2, 3)
    held = lax.all_gather(gt[:, :, :width].astype(BF), "tensor").astype(F32)
    held = held.reshape(parts, adapters, 3, 16, width).transpose(2, 1, 0, 4, 3)
    triple_down_grad = held.reshape(3, adapters, dim, 16)

    return (
        layer,
        tokens_grad,
        triple_down_grad,
        triple_up_grad,
        merge_down_grad,
        merge_up_grad,
        expand_down_grad,
        expand_up_grad,
        reduce_down_grad,
        reduce_up_grad,
    )


def solution(mesh):
    in_specs = (
        P("dp", "tensor"),
        P("dp", "tensor"),
        P("dp"),
        P("dp"),
        P(),
        P(),
        P(None, None, "tensor"),
        P(None, "tensor"),
        P(),
        P(None, None, None, "tensor"),
        P("tensor", None),
        P(),
        P(None, "tensor", None),
        P(),
        P(),
        P(),
        P(None, "tensor"),
        P("tensor"),
        P(),
        P(None, None, "tensor"),
        P("tensor", None),
        P(),
        P(None, "tensor", None),
        P(),
    )
    out_specs = (
        P("dp", "tensor"),
        P("dp", "tensor"),
        P(),
        P(None, None, None, "tensor"),
        P(None, "tensor", None),
        P(),
        P(),
        P(None, None, "tensor"),
        P(None, "tensor", None),
        P(),
    )
    return jax.shard_map(
        partial(shards, parts=mesh.shape["tensor"], copies=mesh.shape["dp"]),
        mesh=mesh,
        in_specs=in_specs,
        out_specs=out_specs,
        check_vma=False,
    )
```

```python
import math
from functools import partial

import jax
import jax.numpy as jnp
from jax import lax
from jax.experimental import pallas as pl
from jax.experimental.pallas import tpu as pltpu
from jax.sharding import PartitionSpec as P

HEAD_DIM = 72
HEAD_PAD = 80
LANES = 128
CHUNK = 256
EPS = 1e-06
BF = jnp.bfloat16
F32 = jnp.float32
SCALE = 1.0 / math.sqrt(HEAD_DIM)
LOG2E = 1.4426950408889634
MIB = 1024 * 1024

NN = (((1,), (0,)), ((), ()))
NT = (((1,), (1,)), ((), ()))
TN = (((0,), (0,)), ((), ()))


def mm(a, b, dims=NN):
    return lax.dot_general(a, b, dims, preferred_element_type=F32)


def up_to(value, step):
    return -(-value // step) * step


def vmem():
    return pl.BlockSpec(memory_space=pltpu.VMEM)


def anywhere():
    return pl.BlockSpec(memory_space=pl.ANY)


def smem():
    return pl.BlockSpec(memory_space=pltpu.SMEM)


class Shape:
    def __init__(self, parts, slots, copies):
        self.parts, self.slots, self.copies = parts, slots, copies
        self.groups = parts // slots
        self.pairs = [(k, g) for k in range(slots) for g in range(self.groups)]
        self.bits = []
        bit = copies // 2
        while bit:
            self.bits.append(bit)
            bit //= 2
        self.orders = (self.bits, self.bits[1::-1] + self.bits[2:])
        self.batches = (
            [(0, g) for g in range(1, self.groups)],
            [(k, 0) for k in range(1, slots)],
            [(k, g) for k, g in self.pairs if k > 0 and g > 0],
        )

    def source(self, mine, member, k, g):
        return lax.rem(mine - k + self.slots, self.slots) * self.groups + lax.rem(
            member - g + self.groups, self.groups
        )

    def mask(self, spot, order=0):
        return sum(bit for n, bit in enumerate(self.orders[order]) if (spot >> n) & 1)


def run_all(copies):
    for copy in copies:
        copy.start()
    for copy in copies:
        copy.wait()


def weight_copies(shape, row, own, foreign, dest, sems):
    rows = own.shape[0]
    copies = [pltpu.make_async_copy(own, dest.at[0, pl.ds(0, rows), :], sems.at[0])]
    for k in range(1, shape.slots):
        near, far = foreign[2 * (k - 1) : 2 * k]
        half, size, _ = near.shape
        for spot in range(shape.copies):
            piece = near.at[spot] if spot < half else far.at[spot - half]
            at = pl.multiple_of(jnp.bitwise_xor(row, shape.mask(spot)) * size, 16)
            copies.append(
                pltpu.make_async_copy(
                    piece,
                    dest.at[k, pl.ds(at, size), :],
                    sems.at[1 + (k - 1) * shape.copies + spot],
                )
            )
    return copies


def project_kernel(shape, seq, sc, norm_ref, down_ref, upx_ref, own_tok, own_w, *rest):
    slots, groups, parts = shape.slots, shape.groups, shape.parts
    toks = rest[: parts - 1]
    foreign = rest[parts - 1 : parts - 1 + 2 * (slots - 1)]
    rest = rest[parts - 1 + 2 * (slots - 1) :]
    qkv_ref, n1_ref, stats_ref, inner_ref, rows_ref = rest[:5]
    tok_ref, weights, tok_sem, weight_sem = rest[5:]
    _, width, span = tok_ref.shape
    dim = parts * width
    head_rows = upx_ref.shape[2] // 3
    heads_here = head_rows // HEAD_DIM
    block = span // groups
    mine, member, row = sc[0], sc[1], sc[3]

    tok_copies = []
    for n, (k, g) in enumerate(shape.pairs):
        source = own_tok.at[mine] if n == 0 else toks[n - 1]
        tok_copies.append(
            pltpu.make_async_copy(
                source, tok_ref.at[shape.source(mine, member, k, g)], tok_sem.at[n]
            )
        )
    weight_list = weight_copies(shape, row, own_w, foreign, weights, weight_sem)
    for copy in tok_copies + weight_list:
        copy.start()
    for copy in tok_copies:
        copy.wait()

    def norm_step(c, carry):
        cols = pl.ds(pl.multiple_of(c * LANES, LANES), LANES)
        x = tok_ref[:, :, cols].reshape(dim, LANES).astype(F32)
        mean = jnp.mean(x, 0, keepdims=True)
        center = x - mean
        rstd = lax.rsqrt(jnp.mean(center * center, 0, keepdims=True) + EPS)
        n1 = center * rstd * norm_ref[:, 0:1] + norm_ref[:, 1:2]
        n1_ref[:, cols] = n1.astype(BF)
        stats_ref[0:1, cols] = mean
        stats_ref[1:2, cols] = rstd
        return carry

    lax.fori_loop(0, span // LANES, norm_step, 0)
    stats_ref[2:8, :] = jnp.zeros((6, span), F32)
    for copy in weight_list:
        copy.wait()

    def proj_step(c, carry):
        start = pl.multiple_of(c * CHUNK, CHUNK)
        cols = pl.ds(start, CHUNK)
        n1 = n1_ref[:, cols]
        rank = down_ref.shape[0]
        inner = mm(down_ref[...], n1)
        line = lax.broadcasted_iota(jnp.int32, (rank, CHUNK), 0)
        inner_x = jnp.where(line == 48, 1.0, 0.5 * inner).astype(BF)
        inner_ref[:, cols] = inner_x
        spot = lax.broadcasted_iota(jnp.int32, (HEAD_PAD - HEAD_DIM, CHUNK), 0)
        place = start + lax.broadcasted_iota(jnp.int32, (HEAD_PAD - HEAD_DIM, CHUNK), 1)
        tails = (
            jnp.where(spot == 0, 1.0, 0.0),
            jnp.where((spot == 0) & (place >= seq), -1e30, 0.0),
            jnp.zeros((HEAD_PAD - HEAD_DIM, CHUNK), F32),
        )
        for k in range(slots):
            proj = mm(weights[k, 0 : 3 * head_rows, :], n1) + mm(upx_ref[k], inner_x, TN)
            for j in range(3):
                for h in range(heads_here):
                    at = j * head_rows + h * HEAD_DIM
                    piece = jnp.concatenate([proj[at : at + HEAD_DIM, :], tails[j]], 0)
                    qkv_ref[j, k * heads_here + h, :, cols] = piece.astype(BF)
        return carry

    lax.fori_loop(0, span // CHUNK, proj_step, 0)

    for g in range(groups):
        rows_ref[g] = tok_ref[:, :, g * block : (g + 1) * block].reshape(dim, block)


def project(shape, seq, scalars, norm, down, upx, own_tok, toks, own_w, foreign):
    slots, groups, parts = shape.slots, shape.groups, shape.parts
    _, width, span = own_tok.shape
    head_rows = upx.shape[2] // 3
    heads = slots * head_rows // HEAD_DIM
    dim = parts * width
    weight_rows = max([own_w.shape[0]] + [w.shape[1] * shape.copies for w in foreign])
    out = (
        jax.ShapeDtypeStruct((3, heads, HEAD_PAD, span), BF),
        jax.ShapeDtypeStruct((dim, span), BF),
        jax.ShapeDtypeStruct((8, span), F32),
        jax.ShapeDtypeStruct((down.shape[0], span), BF),
        jax.ShapeDtypeStruct((groups, dim, span // groups), BF),
    )
    return pl.pallas_call(
        partial(project_kernel, shape, seq),
        out_shape=out,
        in_specs=[smem()] + [vmem()] * 3 + [anywhere()] * (2 + len(toks) + len(foreign)),
        out_specs=tuple(vmem() for _ in out),
        scratch_shapes=[
            pltpu.VMEM((parts, width, span), BF),
            pltpu.VMEM((slots, weight_rows, dim), BF),
            pltpu.SemaphoreType.DMA((parts,)),
            pltpu.SemaphoreType.DMA((1 + (slots - 1) * shape.copies,)),
        ],
        compiler_params=pltpu.CompilerParams(vmem_limit_bytes=48 * MIB),
        cost_estimate=pl.CostEstimate(flops=4 * 10**9, bytes_accessed=40 * 10**6, transcendentals=10**6),
        name="project",
    )(scalars, norm, down, upx, own_tok, own_w, *toks, *foreign)


def attend_kernel(slots, groups, sc, qkv_ref, lse_ref, heads_ref, scr):
    span = scr.shape[1]
    head_rows = scr.shape[0] // slots
    block = span // groups
    h = pl.program_id(0)
    keys = qkv_ref[1, 0].T
    vals = qkv_ref[2, 0]
    at = pl.multiple_of(h * HEAD_DIM, 8)
    for c in range(span // CHUNK):
        cols = slice(c * CHUNK, (c + 1) * CHUNK)
        scores = mm(keys, qkv_ref[0, 0, :, cols]) * (SCALE * LOG2E)
        top = jnp.max(scores, 0, keepdims=True)
        raised = jnp.exp2(scores - top)
        total = jnp.sum(raised, 0, keepdims=True)
        out = mm(vals, raised.astype(BF)) / total
        scr[pl.ds(at, HEAD_DIM), cols] = out[0:HEAD_DIM, :]
        lse_ref[0, 0:1, cols] = top + jnp.log2(total)

    @pl.when(h == pl.num_programs(0) - 1)
    def _():
        for g in range(groups):
            cols = slice(g * block, (g + 1) * block)
            for k in range(slots):
                heads_ref[g, k] = scr[k * head_rows : (k + 1) * head_rows, cols].astype(BF)


def attend(shape, scalars, qkv):
    slots, groups = shape.slots, shape.groups
    _, heads, _, span = qkv.shape
    head_rows = heads * HEAD_DIM // slots
    out = (
        jax.ShapeDtypeStruct((heads, 1, span), F32),
        jax.ShapeDtypeStruct((groups, slots, head_rows, span // groups), BF),
    )
    return pl.pallas_call(
        partial(attend_kernel, slots, groups),
        grid=(heads,),
        out_shape=out,
        in_specs=[smem(), pl.BlockSpec((3, 1, HEAD_PAD, span), lambda h: (0, h, 0, 0))],
        out_specs=(
            pl.BlockSpec((1, 1, span), lambda h: (h, 0, 0)),
            pl.BlockSpec(out[1].shape, lambda h: (0, 0, 0, 0)),
        ),
        scratch_shapes=[pltpu.VMEM((slots * head_rows, span), F32)],
        compiler_params=pltpu.CompilerParams(vmem_limit_bytes=40 * MIB),
        cost_estimate=pl.CostEstimate(flops=4 * 10**9, bytes_accessed=60 * 10**6, transcendentals=5 * 10**6),
        name="attend",
    )(scalars, qkv)


def middle_kernel(
    shape, sizes, sc, vec_ref, tab_ref, rows_hbm, own_heads, own_expand, own_reduce, own_merge, *rest
):
    slots, groups, parts = shape.slots, shape.groups, shape.parts
    piece, merge_rows = sizes
    gathered, rest = rest[:12], rest[12:]
    heads_hbm = (own_heads,) + rest[: groups - 1]
    cots = rest[groups - 1 : groups - 1 + parts]
    facs = rest[groups - 1 + parts : groups - 1 + 2 * parts]
    rest = rest[groups - 1 + 2 * parts :]
    layer_ref, resid_ref, back_ref, gm_ref = rest[:4]
    both, wm, heads_rel, heads_in, rows_in, cot_in, fac_in = rest[4:11]
    acc_out, acc_back, n2x, gx, eug, rdg, sem, own_sem, w_sem = rest[11:]
    _, head_rows, block = heads_in.shape
    dim = parts * head_rows
    hidden_rows = fac_in.shape[2]
    full = parts * hidden_rows
    tail = slice(dim, dim + LANES)
    mine, member, valid, row, ident = sc[0], sc[1], sc[2], sc[3], sc[4]
    here = mine * groups + member

    small = [pltpu.make_async_copy(own_heads.at[member], heads_rel.at[0], sem.at[0])]
    for g in range(1, groups):
        small.append(pltpu.make_async_copy(heads_hbm[g], heads_rel.at[g], sem.at[g]))
    small.append(pltpu.make_async_copy(rows_hbm.at[member], rows_in, sem.at[groups]))
    for n, (k, g) in enumerate(shape.pairs):
        spot = shape.source(mine, member, k, g)
        at = groups + 1 + 2 * n
        small.append(pltpu.make_async_copy(cots[n], cot_in.at[spot], sem.at[at]))
        small.append(pltpu.make_async_copy(facs[n], fac_in.at[spot], sem.at[at + 1]))
    merges, mlps = [], []
    cols = pl.ds(0, dim)
    start = pl.multiple_of(here * hidden_rows, 16)
    for n, source in enumerate((own_expand, own_reduce)):
        mlps.append(
            pltpu.make_async_copy(
                source, both.at[n, pl.ds(start, hidden_rows), cols], own_sem.at[n]
            )
        )
    start = pl.multiple_of(here * head_rows, 16)
    merges.append(
        pltpu.make_async_copy(own_merge, wm.at[pl.ds(start, head_rows), cols], own_sem.at[2])
    )
    lines = (piece + merge_rows) // 2
    real = head_rows // merge_rows
    spare = shape.copies - real
    half = shape.copies // 2
    done = 0
    for batch in range(3):
        for order in range(2):
            near, far = gathered[4 * batch + 2 * order : 4 * batch + 2 * order + 2]
            for spot in range(shape.copies):
                origin = jnp.bitwise_xor(row, shape.mask(spot, order))
                for n, (k, g) in enumerate(shape.batches[batch]):
                    shard = shape.source(mine, member, k, g)
                    source = near.at[spot, n] if spot < half else far.at[spot - half, n]
                    first = order * lines
                    count = min(lines, piece - first)
                    index = (done + n) * 2 * shape.copies
                    index = index + 2 * spot + order
                    base = shard * hidden_rows + lax.rem(origin, half) * piece + first
                    mlps.append(
                        pltpu.make_async_copy(
                            source.at[pl.ds(0, count), :],
                            both.at[origin // half, pl.ds(pl.multiple_of(base, 16), count), cols],
                            w_sem.at[0, index],
                        )
                    )
                    if count < lines:
                        base = jnp.where(
                            origin < real,
                            shard * head_rows + origin * merge_rows,
                            dim + (shard * spare + origin - real) * merge_rows,
                        )
                        merges.append(
                            pltpu.make_async_copy(
                                source.at[pl.ds(count, merge_rows), :],
                                wm.at[pl.ds(pl.multiple_of(base, 16), merge_rows), cols],
                                w_sem.at[1, index],
                            )
                        )
        done += len(shape.batches[batch])
    for copy in small + merges + mlps:
        copy.start()
    for copy in small:
        copy.wait()

    for g in range(groups):
        for k in range(slots):
            spot = lax.rem(member - g + groups, groups) + groups * lax.rem(mine + k, slots)
            heads_in[spot] = heads_rel[g, k]
    heads = heads_in[...].reshape(dim, block).T
    grads = cot_in[...].reshape(dim, block).T * valid.astype(F32).astype(BF)

    for t in range(parts):
        fac = fac_in[t]
        spread = jnp.concatenate(
            [fac[0:16, :], fac[48:64, :], jnp.zeros((LANES - 32, hidden_rows), BF)], 0
        )
        both[0, t * hidden_rows : (t + 1) * hidden_rows, tail] = spread.T
        spread = jnp.concatenate([fac[16:32, :], jnp.zeros((LANES - 16, hidden_rows), BF)], 0)
        both[1, t * hidden_rows : (t + 1) * hidden_rows, tail] = spread.T
        spread = jnp.concatenate(
            [fac[32:48, 0:head_rows], jnp.zeros((LANES - 16, head_rows), BF)], 0
        )
        wm[t * head_rows : (t + 1) * head_rows, tail] = spread.T

    for copy in merges:
        copy.wait()
    merged = mm(heads, wm[0:dim, :])
    inner_m = (0.5 * merged[:, tail]).astype(BF)
    x = rows_in[...].T.astype(F32)
    hidden = x + merged[:, :dim] + mm(inner_m, tab_ref[0]) + vec_ref[0:1, :]
    mean = jnp.mean(hidden, 1, keepdims=True)
    center = hidden - mean
    rstd = lax.rsqrt(jnp.mean(center * center, 1, keepdims=True) + EPS)
    unit = center * rstd
    n2 = (unit * vec_ref[2:3, :] + vec_ref[3:4, :]).astype(BF)
    n2x[:, 0:dim] = n2
    lane = lax.broadcasted_iota(jnp.int32, (block, LANES), 1)
    inner_e = jnp.where(lane == 16, 1.0, 0.5 * mm(n2, tab_ref[1], NT)).astype(BF)
    n2x[:, tail] = inner_e
    gx[:, 0:dim] = grads
    thr_r = (0.5 * mm(grads, tab_ref[2], NT)).astype(BF)
    gx[:, tail] = thr_r
    inner_et = inner_e.T
    thr_rt = thr_r.T
    acc_out[...] = jnp.zeros_like(acc_out)
    acc_back[...] = jnp.zeros_like(acc_back)
    for copy in mlps:
        copy.wait()

    def step(c, carry):
        at = pl.ds(pl.multiple_of(c * CHUNK, CHUNK), CHUNK)
        we_c = both[0, at, :]
        wr_c = both[1, at, :]
        pre = mm(n2x[...], we_c, NT)
        grad_act = mm(gx[...], wr_c, NT)
        square = pre * pre
        th = jnp.tanh(pre * (0.7978845608028654 + 0.035677408136300125 * square))
        half = 0.5 * (1.0 + th)
        act = (pre * half).astype(BF)
        slope = half + pre * (0.5 * (1.0 - th * th)) * (
            0.7978845608028654 + 0.10703222440890037 * square
        )
        grad_pre = (grad_act * slope).astype(BF)
        acc_out[...] += mm(act, wr_c)
        acc_back[...] += mm(grad_pre, we_c)
        eug[:, at] = mm(inner_et[0:16, :], grad_pre)
        rdg[:, at] = mm(thr_rt[0:16, :], act)
        return carry

    lax.fori_loop(0, full // CHUNK, step, 0)

    inner_r = (0.5 * acc_out[:, tail]).astype(BF)
    layer = hidden + acc_out[:, 0:dim] + mm(inner_r, tab_ref[2]) + vec_ref[1:2, :]
    thr_e = (0.5 * acc_back[:, tail]).astype(BF)
    scaled = (acc_back[:, 0:dim] + mm(thr_e, tab_ref[1])) * vec_ref[2:3, :]
    first = jnp.mean(scaled, 1, keepdims=True)
    second = jnp.mean(scaled * unit, 1, keepdims=True)
    grad_hidden = grads.astype(F32) + rstd * (scaled - first - unit * second)
    branch = grad_hidden.astype(BF)
    thr_m = (0.5 * mm(branch, tab_ref[0], NT)).astype(BF)
    grad_heads = mm(branch, wm[0:dim, 0:dim], NT) + mm(thr_m, wm[0:dim, tail], NT)
    grad_heads_t = grad_heads.T.astype(BF)
    layer_t = layer.T.astype(BF)
    resid_ref[...] = grad_hidden.T
    for t in range(parts):
        at = slice(t * head_rows, (t + 1) * head_rows)
        layer_ref[t] = layer_t[at, :]
        back_ref[t % groups, lax.rem(t // groups - mine + slots, slots)] = grad_heads_t[at, :]

    whole = (
        mm(thr_m, heads, TN)[0:16, :],
        mm(inner_m, branch, TN)[0:16, :],
        mm(thr_e, n2, TN)[0:16, :],
        mm(inner_r, grads, TN)[0:16, :],
    )
    for t in range(parts):
        at = slice(t * hidden_rows, (t + 1) * hidden_rows)
        gm_ref[t, :, 0:hidden_rows] = eug[:, at].astype(BF)
        gm_ref[t, :, hidden_rows : 2 * hidden_rows] = rdg[:, at].astype(BF)
        for n in range(4):
            off = 2 * hidden_rows + n * head_rows
            gm_ref[t, :, off : off + head_rows] = whole[n][
                :, t * head_rows : (t + 1) * head_rows
            ].astype(BF)
        off = 2 * hidden_rows + 4 * head_rows
        gm_ref[t, :, off:] = jnp.full((16, gm_ref.shape[2] - off), ident, jnp.int32).astype(F32).astype(BF)


def middle(shape, sizes, scalars, vec, tab, rows, heads, own_w, gathered, cots, facs):
    slots, groups, parts = shape.slots, shape.groups, shape.parts
    own_heads, others = heads
    _, _, head_rows, block = own_heads.shape
    dim = parts * head_rows
    hidden_rows = facs[0].shape[1]
    full = parts * hidden_rows
    cols = up_to(2 * hidden_rows + 4 * head_rows + 1, LANES)
    spare = parts * (shape.copies - head_rows // sizes[1]) * sizes[1]
    out = (
        jax.ShapeDtypeStruct((parts, head_rows, block), BF),
        jax.ShapeDtypeStruct((dim, block), F32),
        jax.ShapeDtypeStruct((groups, slots, head_rows, block), BF),
        jax.ShapeDtypeStruct((parts, 16, cols), BF),
    )
    return pl.pallas_call(
        partial(middle_kernel, shape, sizes),
        out_shape=out,
        in_specs=[smem()] + [vmem()] * 2 + [anywhere()] * (5 + len(gathered) + len(others) + 2 * parts),
        out_specs=tuple(vmem() for _ in out),
        scratch_shapes=[
            pltpu.VMEM((2, full, dim + LANES), BF),
            pltpu.VMEM((dim + spare, dim + LANES), BF),
            pltpu.VMEM((groups, slots, head_rows, block), BF),
            pltpu.VMEM((parts, head_rows, block), BF),
            pltpu.VMEM((dim, block), BF),
            pltpu.VMEM((parts, head_rows, block), BF),
            pltpu.VMEM((parts, 64, hidden_rows), BF),
            pltpu.VMEM((block, dim + LANES), F32),
            pltpu.VMEM((block, dim + LANES), F32),
            pltpu.VMEM((block, dim + LANES), BF),
            pltpu.VMEM((block, dim + LANES), BF),
            pltpu.VMEM((16, full), F32),
            pltpu.VMEM((16, full), F32),
            pltpu.SemaphoreType.DMA((groups + 1 + 2 * parts,)),
            pltpu.SemaphoreType.DMA((3,)),
            pltpu.SemaphoreType.DMA((2, 2 * parts * shape.copies)),
        ],
        compiler_params=pltpu.CompilerParams(vmem_limit_bytes=60 * MIB),
        cost_estimate=pl.CostEstimate(flops=20 * 10**9, bytes_accessed=100 * 10**6, transcendentals=2 * 10**6),
        name="middle",
    )(scalars, vec, tab, rows, own_heads, *own_w, *gathered, *others, *cots, *facs)


def heads_back_kernel(shape, slot, sc, qkv_ref, lse_ref, own_dout, *rest):
    groups = shape.groups
    douts = (own_dout,) + rest[: groups - 1]
    out_ref, dout_rel, dot_scr, grad_scr, sem = rest[groups - 1 :]
    _, head_rows, block = dout_rel.shape
    span = groups * block
    heads_here = head_rows // HEAD_DIM
    member = sc[1]
    h = pl.program_id(0)

    @pl.when(h == 0)
    def _():
        copies = []
        for g in range(groups):
            source = own_dout.at[member, slot] if g == 0 else douts[g].at[slot]
            spot = lax.rem(member - g + groups, groups)
            copies.append(pltpu.make_async_copy(source, dout_rel.at[spot], sem.at[g]))
        run_all(copies)
        pad = jnp.zeros((HEAD_PAD - HEAD_DIM, block), F32)
        for g in range(groups):
            piece = dout_rel[g].astype(F32)
            for n in range(heads_here):
                one = jnp.concatenate([piece[n * HEAD_DIM : (n + 1) * HEAD_DIM, :], pad], 0)
                dot_scr[n, :, g * block : (g + 1) * block] = one.astype(BF)

    query_t = qkv_ref[0, 0]
    keys_t = qkv_ref[1, 0]
    query = query_t.T
    keys = keys_t.T
    vals = qkv_ref[2, 0].T
    dout_t = dot_scr[h]
    dout = dout_t.T
    dvals = jnp.zeros((span, HEAD_PAD), F32)
    dkeys = jnp.zeros((span, HEAD_PAD), F32)
    row = pl.multiple_of(h * HEAD_DIM, 8)
    for c in range(span // CHUNK):
        cols = slice(c * CHUNK, (c + 1) * CHUNK)
        scores = mm(keys, query_t[:, cols]) * (SCALE * LOG2E)
        probs = jnp.exp2(scores - lse_ref[0, 0:1, cols])
        dprobs = mm(vals, dout_t[:, cols])
        delta = jnp.sum(probs * dprobs, 0, keepdims=True)
        dscores = (probs * (dprobs - delta)).astype(BF)
        dvals += mm(probs.astype(BF), dout[cols, :])
        dkeys += mm(dscores, query[cols, :])
        dquery = mm(keys_t, dscores) * SCALE
        grad_scr[pl.ds(row, HEAD_DIM), cols] = dquery[0:HEAD_DIM, :]
    row = pl.multiple_of(row + head_rows, 8)
    grad_scr[pl.ds(row, HEAD_DIM), :] = (dkeys * SCALE).T[0:HEAD_DIM, :]
    row = pl.multiple_of(row + head_rows, 8)
    grad_scr[pl.ds(row, HEAD_DIM), :] = dvals.T[0:HEAD_DIM, :]

    @pl.when(h == heads_here - 1)
    def _():
        out_ref[...] = grad_scr[...].astype(BF)


def heads_back(shape, slot, scalars, qkv, lse, dout):
    own, others = dout
    groups, _, head_rows, block = own.shape
    span = groups * block
    heads_here = head_rows // HEAD_DIM
    return pl.pallas_call(
        partial(heads_back_kernel, shape, slot),
        grid=(heads_here,),
        out_shape=jax.ShapeDtypeStruct((3 * head_rows, span), BF),
        in_specs=[
            smem(),
            pl.BlockSpec((3, 1, HEAD_PAD, span), lambda h: (0, slot * heads_here + h, 0, 0)),
            pl.BlockSpec((1, 1, span), lambda h: (slot * heads_here + h, 0, 0)),
            anywhere(),
        ]
        + [anywhere()] * len(others),
        out_specs=pl.BlockSpec((3 * head_rows, span), lambda h: (0, 0)),
        scratch_shapes=[
            pltpu.VMEM((groups, head_rows, block), BF),
            pltpu.VMEM((heads_here, HEAD_PAD, span), BF),
            pltpu.VMEM((3 * head_rows, span), F32),
            pltpu.SemaphoreType.DMA((groups,)),
        ],
        compiler_params=pltpu.CompilerParams(vmem_limit_bytes=40 * MIB),
        cost_estimate=pl.CostEstimate(flops=4 * 10**9, bytes_accessed=40 * 10**6, transcendentals=3 * 10**6),
        name="heads_back",
    )(scalars, qkv, lse, own, *others)


def rank_back_kernel(shape, sc, down_ref, upx_ref, n1_ref, inner_ref, *rest):
    slots, groups, parts = shape.slots, shape.groups, shape.parts
    grads = rest[:slots]
    td_ref, thr_ref, tu_scr = rest[slots:]
    dim, span = n1_ref.shape
    width = dim // parts
    head_rows = upx_ref.shape[2] // 3
    mine, member, ident = sc[0], sc[1], sc[4]
    rank = down_ref.shape[0]
    spread = 3 * head_rows
    thr = jnp.zeros((rank, span), F32)
    row_of = lax.broadcasted_iota(jnp.int32, (rank, spread), 0) // 16
    part_of = lax.broadcasted_iota(jnp.int32, (rank, spread), 1) // head_rows
    for k in range(slots):
        thr = thr + mm(upx_ref[k], grads[k][...])
        ups = mm(inner_ref[...], grads[k][...], NT)
        ups = jnp.where(row_of == part_of, ups, 0.0)
        tu_scr[k] = ups[0:16, :] + ups[16:32, :] + ups[32:48, :]
    line = lax.broadcasted_iota(jnp.int32, (rank, span), 0)
    thr_b = jnp.where(line < 48, 0.5 * thr, 0.0).astype(BF)
    thr_ref[...] = thr_b
    downs = mm(thr_b, n1_ref[...], NT)
    rest_cols = td_ref.shape[2] - width - head_rows
    ids = jnp.full((48, rest_cols), ident, jnp.int32).astype(F32)
    for t in range(parts):
        own = jnp.where(member == t % groups, 1.0, 0.0)
        ups = tu_scr[lax.rem(t // groups - mine + slots, slots)] * own
        ups = jnp.concatenate([ups[:, j * head_rows : (j + 1) * head_rows] for j in range(3)], 0)
        down_part = downs[0:48, t * width : (t + 1) * width]
        td_ref[t] = jnp.concatenate([down_part, ups, ids], 1).astype(BF)


def rank_back(shape, scalars, down, upx, n1, inner, grads):
    slots, parts = shape.slots, shape.parts
    dim, span = n1.shape
    head_rows = upx.shape[2] // 3
    cols = up_to(dim // parts + head_rows + 1, LANES)
    out = (
        jax.ShapeDtypeStruct((parts, 48, cols), BF),
        jax.ShapeDtypeStruct((down.shape[0], span), BF),
    )
    return pl.pallas_call(
        partial(rank_back_kernel, shape),
        out_shape=out,
        in_specs=[smem()] + [vmem()] * (4 + slots),
        out_specs=(vmem(), vmem()),
        scratch_shapes=[pltpu.VMEM((slots, 16, 3 * head_rows), F32)],
        compiler_params=pltpu.CompilerParams(vmem_limit_bytes=40 * MIB),
        cost_estimate=pl.CostEstimate(flops=10**9, bytes_accessed=10 * 10**6, transcendentals=0),
        name="rank_back",
    )(scalars, down, upx, n1, inner, *grads)


def norm_back_kernel(shape, sc, norm_ref, down_ref, thr_ref, stats_ref, rows_ref, resid_ref, own_w, *rest):
    slots, groups, parts = shape.slots, shape.groups, shape.parts
    foreign = rest[: 2 * (slots - 1)]
    rest = rest[2 * (slots - 1) :]
    grads = rest[:slots]
    out_ref, weights, e1_scr, sem = rest[slots:]
    _, dim, block = rows_ref.shape
    span = groups * block
    width = dim // parts
    spread = own_w.shape[0]
    member, row = sc[1], sc[3]
    run_all(weight_copies(shape, row, own_w, foreign, weights, sem))

    def final_step(c, carry):
        cols = pl.ds(pl.multiple_of(c * CHUNK, CHUNK), CHUNK)
        total = mm(down_ref[...], thr_ref[:, cols], TN)
        for k in range(slots):
            total = total + mm(weights[k, 0:spread, :], grads[k][:, cols], TN)
        e1_scr[:, cols] = total * norm_ref[:, 0:1]
        return carry

    lax.fori_loop(0, span // CHUNK, final_step, 0)
    for g in range(groups):
        cols = slice(g * block, (g + 1) * block)
        e1 = e1_scr[:, cols]
        first = jnp.sum(e1, 0, keepdims=True)
        mean, rstd = stats_ref[0:1, cols], stats_ref[1:2, cols]
        unit = (rows_ref[g].astype(F32) - mean) * rstd
        second = jnp.sum(e1 * unit, 0, keepdims=True)
        lines = []
        for value in (first, second, mean, rstd):
            high = value.astype(BF).astype(F32)
            lines += [high, value - high]
        lines = jnp.concatenate(lines + [jnp.zeros((8, block), F32)], 0).astype(BF)
        e1 = e1 + resid_ref[...] * (jnp.where(member == g, 1.0, 0.0) / rstd)
        for t in range(parts):
            out_ref[t, 0:width, cols] = e1[t * width : (t + 1) * width, :].astype(BF)
            out_ref[t, width : width + 16, cols] = lines


def norm_back(shape, scalars, norm, down, thr, stats, rows, resid, own_w, foreign, grads):
    slots, parts = shape.slots, shape.parts
    groups, dim, block = rows.shape
    span = groups * block
    weight_rows = max([own_w.shape[0]] + [w.shape[1] * shape.copies for w in foreign])
    return pl.pallas_call(
        partial(norm_back_kernel, shape),
        out_shape=jax.ShapeDtypeStruct((parts, dim // parts + 16, span), BF),
        in_specs=[smem()] + [vmem()] * 6 + [anywhere()] * (1 + len(foreign)) + [vmem()] * slots,
        out_specs=vmem(),
        scratch_shapes=[
            pltpu.VMEM((slots, weight_rows, dim), BF),
            pltpu.VMEM((dim, span), F32),
            pltpu.SemaphoreType.DMA((1 + (slots - 1) * shape.copies,)),
        ],
        compiler_params=pltpu.CompilerParams(vmem_limit_bytes=48 * MIB),
        cost_estimate=pl.CostEstimate(flops=3 * 10**9, bytes_accessed=20 * 10**6, transcendentals=0),
        name="norm_back",
    )(scalars, norm, down, thr, stats, rows, resid, own_w, *foreign, *grads)


def tokens_kernel(shape, seq, sc, img_ref, own, *rest):
    slots, groups, parts = shape.slots, shape.groups, shape.parts
    out_ref, held, sem = rest[parts - 1 :]
    mine, member, place = sc[0], sc[1], sc[5]
    _, width, span = img_ref.shape
    dim = parts * width
    copies = []
    for n, (k, g) in enumerate(shape.pairs):
        source = own.at[place] if n == 0 else rest[n - 1]
        copies.append(
            pltpu.make_async_copy(source, held.at[shape.source(mine, member, k, g)], sem.at[n])
        )
    run_all(copies)
    for n in range(slots):
        total = held[n * groups].astype(F32)
        lines = total[width : width + 16, :]
        mean = lines[4:5, :] + lines[5:6, :]
        rstd = lines[6:7, :] + lines[7:8, :]
        for g in range(1, groups):
            total = total + held[n * groups + g].astype(F32)
        first = (total[width : width + 1, :] + total[width + 1 : width + 2, :]) / dim
        second = (total[width + 2 : width + 3, :] + total[width + 3 : width + 4, :]) / dim
        unit = (img_ref[n].astype(F32) - mean) * rstd
        grad = rstd * (total[0:width, :] - first - unit * second)
        out_ref[:, n * seq : (n + 1) * seq] = grad[:, 0:seq]


def tokens_result(shape, seq, scalars, images, own, others):
    slots, parts = shape.slots, shape.parts
    _, width, span = images.shape
    return pl.pallas_call(
        partial(tokens_kernel, shape, seq),
        out_shape=jax.ShapeDtypeStruct((width, slots * seq), F32),
        in_specs=[smem(), vmem()] + [anywhere()] * parts,
        out_specs=vmem(),
        scratch_shapes=[
            pltpu.VMEM((parts, width + 16, span), BF),
            pltpu.SemaphoreType.DMA((parts,)),
        ],
        compiler_params=pltpu.CompilerParams(vmem_limit_bytes=40 * MIB),
        cost_estimate=pl.CostEstimate(flops=10**7, bytes_accessed=6 * 10**6, transcendentals=0),
        name="tokens_result",
    )(scalars, images, own, *others)


def layer_kernel(shape, seq, sc, own, *rest):
    slots, groups, parts = shape.slots, shape.groups, shape.parts
    out_ref, held, sem = rest[parts - 1 :]
    mine, member, place = sc[0], sc[1], sc[5]
    copies = []
    for n, (k, g) in enumerate(shape.pairs):
        source = own.at[place] if n == 0 else rest[n - 1]
        copies.append(
            pltpu.make_async_copy(source, held.at[shape.source(mine, member, k, g)], sem.at[n])
        )
    run_all(copies)
    for n in range(slots):
        image = jnp.concatenate([held[n * groups + g].astype(F32) for g in range(groups)], 1)
        out_ref[:, n * seq : (n + 1) * seq] = image[:, 0:seq].astype(BF)


def layer_result(shape, seq, scalars, own, others):
    slots, parts = shape.slots, shape.parts
    _, width, block = own.shape
    return pl.pallas_call(
        partial(layer_kernel, shape, seq),
        out_shape=jax.ShapeDtypeStruct((width, slots * seq), BF),
        in_specs=[smem()] + [anywhere()] * parts,
        out_specs=vmem(),
        scratch_shapes=[
            pltpu.VMEM((parts, width, block), BF),
            pltpu.SemaphoreType.DMA((parts,)),
        ],
        compiler_params=pltpu.CompilerParams(vmem_limit_bytes=40 * MIB),
        cost_estimate=pl.CostEstimate(flops=10**7, bytes_accessed=3 * 10**6, transcendentals=0),
        name="layer_result",
    )(scalars, own, *others)


def tables_kernel(shape, sc, downs, held, downs_ref, merge_ref, expand_ref, reduce_ref, downs_in, held_in, sem):
    mine, member = sc[0], sc[1]
    copies = []
    for n, (k, g) in enumerate(shape.pairs):
        spot = shape.source(mine, member, k, g)
        copies.append(pltpu.make_async_copy(downs.at[:, n], downs_in.at[:, spot], sem.at[0, n]))
        copies.append(pltpu.make_async_copy(held.at[:, n], held_in.at[:, spot], sem.at[1, n]))
    run_all(copies)
    adapters = downs_ref.shape[1]
    width = downs_in.shape[3]
    for t in range(shape.parts):
        lanes = slice(t * width, (t + 1) * width)
        rows = downs_in[:, t].astype(F32).reshape(adapters * 48, width)
        for a in range(adapters):
            for j in range(3):
                downs_ref[j, a, :, lanes] = rows[48 * a + 16 * j : 48 * a + 16 * j + 16, :]
        rows = held_in[:, t].astype(F32).reshape(adapters, 16, 3 * width)
        for n, ref in enumerate((merge_ref, expand_ref, reduce_ref)):
            ref[:, :, lanes] = rows[:, :, n * width : (n + 1) * width]


def whole_tables(shape, scalars, downs, held):
    copies, parts, rows, width = downs.shape
    adapters = copies * rows // 48
    dim = parts * width
    out = (jax.ShapeDtypeStruct((3, adapters, 16, dim), F32),) + (
        jax.ShapeDtypeStruct((adapters, 16, dim), F32),
    ) * 3
    result = pl.pallas_call(
        partial(tables_kernel, shape),
        out_shape=out,
        in_specs=[smem(), anywhere(), anywhere()],
        out_specs=tuple(vmem() for _ in out),
        scratch_shapes=[
            pltpu.VMEM(downs.shape, BF),
            pltpu.VMEM(held.shape, BF),
            pltpu.SemaphoreType.DMA((2, parts)),
        ],
        compiler_params=pltpu.CompilerParams(vmem_limit_bytes=40 * MIB),
        cost_estimate=pl.CostEstimate(flops=10**7, bytes_accessed=6 * 10**6, transcendentals=0),
        name="whole_tables",
    )(scalars, downs, held)
    return result[0], result[1:]


def by_adapter_kernel(parts_of, adapters, count, terms_ref, *outs):
    images, rows, cols = terms_ref.shape
    for spot, (first, size) in enumerate(parts_of):
        for a in range(adapters):
            total = jnp.zeros((rows, size), F32)
            for e in range(images):
                which = terms_ref[e, 0:1, cols - 1 : cols].astype(F32)
                chosen = jnp.where(jnp.abs(which - a * count) < 0.5, 1.0, 0.0)
                total = total + terms_ref[e, :, first : first + size].astype(F32) * chosen
            outs[spot][a] = total.astype(outs[spot].dtype)


def by_adapter(terms, adapters, count, parts_of, types):
    images, rows, cols = terms.shape
    out = tuple(
        jax.ShapeDtypeStruct((adapters, rows, size), kind)
        for (_, size), kind in zip(parts_of, types, strict=True)
    )
    return pl.pallas_call(
        partial(by_adapter_kernel, parts_of, adapters, count),
        out_shape=out,
        in_specs=[vmem()],
        out_specs=tuple(vmem() for _ in out),
        compiler_params=pltpu.CompilerParams(vmem_limit_bytes=40 * MIB),
        cost_estimate=pl.CostEstimate(flops=10**7, bytes_accessed=5 * 10**6, transcendentals=0),
        name="by_adapter",
    )(terms)


def shards(
    tokens,
    cotangent,
    adapter_index,
    valid_image,
    first_gain,
    first_shift,
    triple_weight,
    triple_bias,
    triple_down,
    triple_up,
    merge_weight,
    merge_bias,
    merge_down,
    merge_up,
    second_gain,
    second_shift,
    expand_weight,
    expand_bias,
    expand_down,
    expand_up,
    reduce_weight,
    reduce_bias,
    reduce_down,
    reduce_up,
    *,
    parts,
    copies,
):
    slots = adapter_index.shape[0]
    shape = Shape(parts, slots, copies)
    groups = shape.groups
    seq = tokens.shape[0] // slots
    width = tokens.shape[1]
    dim = width * parts
    head_rows = triple_weight.shape[2]
    adapters = triple_down.shape[1]
    span = up_to(seq, CHUNK)
    block = span // groups
    place = lax.axis_index("tensor")
    row = lax.axis_index("dp")
    mine, member = place // groups, place % groups

    def at(x, n, axis=0):
        return lax.dynamic_index_in_dim(x, n, axis, False)

    index = at(adapter_index, mine)
    valid = at(valid_image, mine)
    scalars = jnp.stack([mine, member, valid, row, index, place]).astype(jnp.int32)

    def jump(x, k, g):
        perm = [
            (s, ((s // groups + k) % slots) * groups + (s % groups + g) % groups)
            for s in range(parts)
        ]
        return lax.ppermute(x, "tensor", perm)

    def swap(pick):
        return [
            jump(pick((mine + k) % slots, (member + g) % groups), k, g)
            for k, g in shape.pairs[1:]
        ]

    def spread_images(x):
        first = [at(x, mine)] + [jump(at(x, (mine + k) % slots), k, 0) for k in range(1, slots)]
        out = []
        for x_k in first:
            out.append(x_k)
            out += [jump(x_k, 0, g) for g in range(1, groups)]
        return out

    def cross(x, bit):
        return lax.ppermute(x, "dp", [(d, d ^ bit) for d in range(copies)])

    def widen(near, bits):
        for bit in bits:
            near = jnp.concatenate([near, cross(near, bit)], 0)
        return near

    def hyper(near, order):
        near = widen(near, order[:-1])
        return [near, cross(near, order[-1])]

    def after(x, *others):
        return lax.optimization_barrier((x, *others))[0]

    def images_of(x):
        flat = x.T
        return jnp.stack(
            [
                jnp.pad(flat[:, n * seq : (n + 1) * seq], ((0, 0), (0, span - seq)))
                for n in range(slots)
            ]
        )

    images = images_of(tokens)
    toks = spread_images(images)[1:]
    ready = toks[groups - 1]

    flat_triple = triple_weight.transpose(0, 2, 1).reshape(3 * head_rows, dim)
    piece_rows = up_to(3 * head_rows, 16 * copies) // copies
    padded = jnp.pad(flat_triple, ((0, piece_rows * copies - 3 * head_rows), (0, 0)))
    my_piece = lax.dynamic_slice_in_dim(padded, row * piece_rows, piece_rows, 0)
    foreign = []
    for k in range(1, slots):
        foreign += hyper(jump(my_piece, -k, 0)[None], shape.bits)

    merge_rows = up_to(width, 16 * copies) // copies
    merge_piece = lax.dynamic_slice_in_dim(
        jnp.pad(merge_weight, ((0, merge_rows * copies - width), (0, 0))), row * merge_rows, merge_rows, 0
    )
    hidden_here = reduce_weight.shape[0]
    hidden_rows = up_to(hidden_here, 8 * copies)
    extra = ((0, hidden_rows - hidden_here), (0, 0))
    mlp_rows = 2 * hidden_rows // copies
    half = copies // 2

    def mlp_part(x):
        return lax.dynamic_slice_in_dim(jnp.pad(x, extra), (row % half) * mlp_rows, mlp_rows, 0)

    mlp_piece = jnp.where(row < half, mlp_part(expand_weight.T), mlp_part(reduce_weight))
    my_w = jnp.concatenate([mlp_piece, merge_piece], 0)
    lines = my_w.shape[0] // 2

    def halves(pieces):
        return [
            jnp.stack([x[order * lines : (order + 1) * lines] for x in pieces])[None]
            for order in range(2)
        ]

    def step(pieces, first, last=None):
        return [widen(x, order[first:last]) for x, order in zip(pieces, shape.orders)]

    def cores(pieces):
        out = []
        for x in pieces:
            out += [x, cross(x, shape.bits[-1])]
        return out

    pair_w = halves([jump(my_w, 0, g) for _, g in shape.batches[0]])
    late_w = after(my_w, ready)
    cross_w = [jump(late_w, k, 0) for k, _ in shape.batches[1]]
    pair_w = step(pair_w, 0, -1)
    gathered = cores(pair_w)
    own_expand = jnp.pad(after(expand_weight.T, ready), extra)
    own_reduce = jnp.pad(after(reduce_weight, ready), extra)

    def up_pack(which):
        table = at(triple_up, which, 1)
        lines = [
            jnp.pad(table[j], ((0, 0), (j * head_rows, (2 - j) * head_rows))) for j in range(3)
        ]
        bias = jnp.pad(triple_bias.reshape(1, 3 * head_rows), ((0, 15), (0, 0)))
        return jnp.concatenate(lines + [bias], 0)

    ups = [up_pack(index)]
    for k in range(1, slots):
        ups.append(jump(up_pack(at(adapter_index, (mine - k) % slots)), -k, 0))
    upx = jnp.stack(ups)
    down = jnp.pad(at(triple_down, index, 1).transpose(0, 2, 1).reshape(48, dim), ((0, 16), (0, 0)))
    norm = jnp.pad(jnp.stack([first_gain, first_shift], 1).astype(F32), ((0, 0), (0, 6)))

    late_index = after(adapter_index, ready)

    def factor_pack(which):
        def lanes(x):
            return jnp.pad(x, ((0, 16 - x.shape[0]), (0, hidden_rows - x.shape[1])))

        return jnp.concatenate(
            [
                lanes(at(expand_up, which)),
                lanes(at(reduce_down, which).T),
                lanes(at(merge_down, which).T),
                lanes(expand_bias[None, :]),
            ],
            0,
        )

    fac_parts = jnp.stack([factor_pack(late_index[n]) for n in range(slots)])
    late = after(index, ready)
    tab = jnp.stack(
        [
            jnp.pad(x, ((0, LANES - 16), (0, 0)))
            for x in (at(merge_up, late), at(expand_down, late).T, at(reduce_up, late))
        ]
    )
    vec = jnp.pad(
        jnp.stack([merge_bias, reduce_bias, second_gain, second_shift]).astype(F32), ((0, 4), (0, 0))
    )

    cot_images = images_of(after(cotangent, ready))

    def trade(x):
        return x, [jump(at(x, (member + g) % groups), 0, g) for g in range(1, groups)]

    begin = after(scalars, own_expand, own_reduce, tab, vec, fac_parts, cot_images, *pair_w)
    qkv, n1, stats, inner, rows = project(
        shape, seq, begin, norm, down, upx, images, toks, flat_triple, foreign
    )
    cross_w = [after(x, stats) for x in cross_w]
    far_w = halves([jump(cross_w[k - 1], 0, g) for k, g in shape.batches[2]])
    cross_w = halves(cross_w)
    late_starts = cross_w
    cross_w = step(cross_w, 0, 1)
    late_cot = after(cot_images, stats)

    def cot_part(i, m):
        return lax.dynamic_slice(late_cot, (i, 0, m * block), (1, width, block))[0]

    cots = [cot_part(mine, member)] + swap(cot_part)
    facs = spread_images(after(fac_parts, stats))
    lse, heads = attend(shape, after(scalars, late_cot, *late_starts), qkv)
    heads = trade(heads)
    cross_w = step([after(x, lse) for x in cross_w], 1, -1)
    far_w = step([after(x, lse) for x in far_w], 0, 1)
    gathered += cores([after(x, *heads[1]) for x in cross_w])
    gathered += cores(step([after(x, *heads[1]) for x in far_w], 1, -1))
    layer, resid, back, gm = middle(
        shape,
        (mlp_rows, merge_rows),
        scalars,
        vec,
        tab,
        rows,
        heads,
        (own_expand, own_reduce, merge_weight),
        gathered,
        cots,
        facs,
    )
    dout = trade(back)

    def spread_rows(x):
        share = x.shape[0] // copies
        own = lax.dynamic_slice_in_dim(x, row * share, share, 0)
        return jnp.stack([own] + [jump(own, k, g) for k, g in shape.pairs[1:]])

    def by_place(x):
        return lambda i, m: at(x, i * groups + m)

    def sum_members(own, others):
        pieces = [at(own, place)] + others
        sums = []
        for k in range(slots):
            total = pieces[k * groups].astype(F32)
            for g in range(1, groups):
                total = total + pieces[k * groups + g].astype(F32)
            sums.append(total.astype(BF))
        return jnp.stack(sums)

    gm_own, gm_others = gm, swap(by_place(gm))
    layers = swap(by_place(layer))
    grads = [heads_back(shape, 0, scalars, qkv, lse, dout)]
    gm = sum_members(after(gm_own, grads[0]), gm_others)
    near = [gm] + [cross(gm, d) for d in range(2, copies, 2)]
    for k in range(1, slots):
        grads.append(heads_back(shape, k, after(scalars, gm), qkv, lse, dout))
    near = after(jnp.concatenate(near, 0), grads[-1])
    gm = jnp.concatenate([near, cross(near, 1)], 0)
    td, thr = rank_back(shape, scalars, down, upx, n1, inner, grads)
    td_own, td_others = td, swap(by_place(td))
    last = norm_back(shape, scalars, norm, down, thr, stats, rows, resid, flat_triple, foreign, grads)
    lasts = swap(by_place(last))
    td = sum_members(after(td_own, last), td_others)
    td = lax.all_gather(td, "dp", tiled=True)
    down_terms, up_terms = by_adapter(
        td, adapters, groups, ((0, width), (width, head_rows)), (BF, F32)
    )
    downs = spread_rows(down_terms.reshape(adapters * 48, width))
    off = 2 * hidden_rows
    expand_up_grad, reduce_down_grad, merge_down_grad, held = by_adapter(
        after(gm, last),
        adapters,
        groups,
        ((0, hidden_here), (hidden_rows, hidden_here), (off, width), (off + width, 3 * width)),
        (F32, F32, F32, BF),
    )
    held = spread_rows(held.reshape(adapters * 16, 3 * width))
    layer_out = layer_result(shape, seq, after(scalars, last), layer, layers).T
    downs, held = whole_tables(shape, scalars, lax.all_gather(downs, "dp"), lax.all_gather(held, "dp"))
    tokens_grad = tokens_result(shape, seq, after(scalars, downs), images, last, lasts).T
    triple_up_grad = up_terms.reshape(adapters, 3, 16, head_rows).transpose(1, 0, 2, 3)

    return (
        layer_out,
        tokens_grad,
        downs.transpose(0, 1, 3, 2),
        triple_up_grad,
        merge_down_grad.transpose(0, 2, 1),
        held[0],
        held[1].transpose(0, 2, 1),
        expand_up_grad,
        reduce_down_grad.transpose(0, 2, 1),
        held[2],
    )


def solution(mesh):
    in_specs = (
        P("dp", "tensor"),
        P("dp", "tensor"),
        P("dp"),
        P("dp"),
        P(),
        P(),
        P(None, None, "tensor"),
        P(None, "tensor"),
        P(),
        P(None, None, None, "tensor"),
        P("tensor", None),
        P(),
        P(None, "tensor", None),
        P(),
        P(),
        P(),
        P(None, "tensor"),
        P("tensor"),
        P(),
        P(None, None, "tensor"),
        P("tensor", None),
        P(),
        P(None, "tensor", None),
        P(),
    )
    out_specs = (
        P("dp", "tensor"),
        P("dp", "tensor"),
        P(),
        P(None, None, None, "tensor"),
        P(None, "tensor", None),
        P(),
        P(),
        P(None, None, "tensor"),
        P(None, "tensor", None),
        P(),
    )
    return jax.shard_map(
        partial(shards, parts=mesh.shape["tensor"], copies=mesh.shape["dp"]),
        mesh=mesh,
        in_specs=in_specs,
        out_specs=out_specs,
        check_vma=False,
    )
```

```python
import math
from functools import partial

import jax
import jax.numpy as jnp
from jax import lax
from jax.experimental import pallas as pl
from jax.experimental.pallas import tpu as pltpu
from jax.sharding import PartitionSpec as P

HEAD_DIM = 72
HEAD_PAD = 80
LANES = 128
CHUNK = 256
UNITS = 512
EPS = 1e-06
BF = jnp.bfloat16
F32 = jnp.float32
SCALE = 1.0 / math.sqrt(HEAD_DIM)
LOG2E = 1.4426950408889634
MIB = 1024 * 1024

NN = (((1,), (0,)), ((), ()))
NT = (((1,), (1,)), ((), ()))
TN = (((0,), (0,)), ((), ()))


def mm(a, b, dims=NN):
    return lax.dot_general(a, b, dims, preferred_element_type=F32)


def up_to(value, step):
    return -(-value // step) * step


def vmem():
    return pl.BlockSpec(memory_space=pltpu.VMEM)


def anywhere():
    return pl.BlockSpec(memory_space=pl.ANY)


def smem():
    return pl.BlockSpec(memory_space=pltpu.SMEM)


class Shape:
    def __init__(self, parts, slots, copies):
        self.parts, self.slots, self.copies = parts, slots, copies
        self.groups = parts // slots
        self.pairs = [(k, g) for k in range(slots) for g in range(self.groups)]
        self.far = [(0, g) for g in range(1, self.groups)]
        self.far += [(k, 0) for k in range(1, slots)]
        self.far += [(k, g) for k in range(1, slots) for g in range(1, self.groups)]
        self.order = [(0, 0)] + self.far
        self.bits = []
        bit = copies // 2
        while bit:
            self.bits.append(bit)
            bit //= 2

    def source(self, mine, member, k, g):
        return lax.rem(mine - k + self.slots, self.slots) * self.groups + lax.rem(
            member - g + self.groups, self.groups
        )

    def mask(self, spot):
        return sum(bit for n, bit in enumerate(self.bits) if (spot >> n) & 1)


def run_all(copies):
    for copy in copies:
        copy.start()
    for copy in copies:
        copy.wait()


def weight_copies(shape, row, own, foreign, dest, sems):
    rows = own.shape[0]
    copies = [pltpu.make_async_copy(own, dest.at[0, pl.ds(0, rows), :], sems.at[0])]
    for k in range(1, shape.slots):
        near, far = foreign[2 * (k - 1) : 2 * k]
        half, size, _ = near.shape
        for spot in range(shape.copies):
            piece = near.at[spot] if spot < half else far.at[spot - half]
            at = pl.multiple_of(jnp.bitwise_xor(row, shape.mask(spot)) * size, 16)
            copies.append(
                pltpu.make_async_copy(
                    piece,
                    dest.at[k, pl.ds(at, size), :],
                    sems.at[1 + (k - 1) * shape.copies + spot],
                )
            )
    return copies


def project_kernel(shape, seq, sc, norm_ref, down_ref, ups_ref, own_tok, own_w, *rest):
    slots, groups, parts = shape.slots, shape.groups, shape.parts
    toks = rest[: parts - 1]
    foreign = rest[parts - 1 : parts - 1 + 2 * (slots - 1)]
    rest = rest[parts - 1 + 2 * (slots - 1) :]
    qkv_ref, n1_ref, stats_ref, inner_ref, rows_ref, upx_ref = rest[:6]
    tok_ref, weights, tok_sem, weight_sem = rest[6:]
    _, width, span = tok_ref.shape
    dim = parts * width
    head_rows = upx_ref.shape[2] // 3
    heads_here = head_rows // HEAD_DIM
    block = span // groups
    mine, member, row = sc[0], sc[1], sc[3]

    tok_copies = []
    for n, (k, g) in enumerate(shape.pairs):
        source = own_tok.at[mine] if n == 0 else toks[n - 1]
        tok_copies.append(
            pltpu.make_async_copy(
                source, tok_ref.at[shape.source(mine, member, k, g)], tok_sem.at[n]
            )
        )
    weight_list = weight_copies(shape, row, own_w, foreign, weights, weight_sem)
    for copy in tok_copies + weight_list:
        copy.start()
    for copy in tok_copies:
        copy.wait()

    def norm_step(c, carry):
        cols = pl.ds(pl.multiple_of(c * LANES, LANES), LANES)
        x = tok_ref[:, :, cols].reshape(dim, LANES).astype(F32)
        mean = jnp.mean(x, 0, keepdims=True)
        center = x - mean
        rstd = lax.rsqrt(jnp.mean(center * center, 0, keepdims=True) + EPS)
        n1 = center * rstd * norm_ref[:, 0:1] + norm_ref[:, 1:2]
        n1_ref[:, cols] = n1.astype(BF)
        stats_ref[0:1, cols] = mean
        stats_ref[1:2, cols] = rstd
        return carry

    lax.fori_loop(0, span // LANES, norm_step, 0)
    stats_ref[2:8, :] = jnp.zeros((6, span), F32)
    part_of = lax.broadcasted_iota(jnp.int32, (16, 3 * head_rows), 1) // head_rows
    for k in range(slots):
        up = ups_ref[k, 0:16, 0 : 3 * head_rows]
        lines = [jnp.where(part_of == j, up, jnp.zeros_like(up)) for j in range(3)]
        upx_ref[k] = jnp.concatenate(lines + [ups_ref[k, 16:32, 0 : 3 * head_rows]], 0)
    for copy in weight_list:
        copy.wait()

    def proj_step(c, carry):
        start = pl.multiple_of(c * CHUNK, CHUNK)
        cols = pl.ds(start, CHUNK)
        n1 = n1_ref[:, cols]
        rank = down_ref.shape[0]
        inner = mm(down_ref[...], n1)
        line = lax.broadcasted_iota(jnp.int32, (rank, CHUNK), 0)
        inner_x = jnp.where(line == 48, 1.0, 0.5 * inner).astype(BF)
        inner_ref[:, cols] = inner_x
        spot = lax.broadcasted_iota(jnp.int32, (HEAD_PAD - HEAD_DIM, CHUNK), 0)
        place = start + lax.broadcasted_iota(jnp.int32, (HEAD_PAD - HEAD_DIM, CHUNK), 1)
        tails = (
            jnp.where(spot == 0, 1.0, 0.0),
            jnp.where((spot == 0) & (place >= seq), -1e30, 0.0),
            jnp.zeros((HEAD_PAD - HEAD_DIM, CHUNK), F32),
        )
        for k in range(slots):
            proj = mm(weights[k, 0 : 3 * head_rows, :], n1) + mm(upx_ref[k], inner_x, TN)
            for j in range(3):
                for h in range(heads_here):
                    at = j * head_rows + h * HEAD_DIM
                    piece = jnp.concatenate([proj[at : at + HEAD_DIM, :], tails[j]], 0)
                    qkv_ref[j, k * heads_here + h, :, cols] = piece.astype(BF)
        return carry

    lax.fori_loop(0, span // CHUNK, proj_step, 0)

    for g in range(groups):
        rows_ref[g] = tok_ref[:, :, g * block : (g + 1) * block].reshape(dim, block)


def project(shape, seq, scalars, norm, down, ups, own_tok, toks, own_w, foreign):
    slots, groups, parts = shape.slots, shape.groups, shape.parts
    _, width, span = own_tok.shape
    head_rows = own_w.shape[0] // 3
    heads = slots * head_rows // HEAD_DIM
    dim = parts * width
    weight_rows = max([own_w.shape[0]] + [w.shape[1] * shape.copies for w in foreign])
    out = (
        jax.ShapeDtypeStruct((3, heads, HEAD_PAD, span), BF),
        jax.ShapeDtypeStruct((dim, span), BF),
        jax.ShapeDtypeStruct((8, span), F32),
        jax.ShapeDtypeStruct((down.shape[0], span), BF),
        jax.ShapeDtypeStruct((groups, dim, span // groups), BF),
        jax.ShapeDtypeStruct((slots, 64, 3 * head_rows), BF),
    )
    return pl.pallas_call(
        partial(project_kernel, shape, seq),
        out_shape=out,
        in_specs=[smem()] + [vmem()] * 3 + [anywhere()] * (2 + len(toks) + len(foreign)),
        out_specs=tuple(vmem() for _ in out),
        scratch_shapes=[
            pltpu.VMEM((parts, width, span), BF),
            pltpu.VMEM((slots, weight_rows, dim), BF),
            pltpu.SemaphoreType.DMA((parts,)),
            pltpu.SemaphoreType.DMA((1 + (slots - 1) * shape.copies,)),
        ],
        compiler_params=pltpu.CompilerParams(vmem_limit_bytes=48 * MIB),
        cost_estimate=pl.CostEstimate(flops=4 * 10**9, bytes_accessed=40 * 10**6, transcendentals=10**6),
        name="project",
    )(scalars, norm, down, ups, own_tok, own_w, *toks, *foreign)


def attend_kernel(slots, sc, qkv_ref, lse_ref, heads_ref, scr):
    span = scr.shape[1]
    head_rows = scr.shape[0] // slots
    h = pl.program_id(0)
    keys = qkv_ref[1, 0].T
    vals = qkv_ref[2, 0]
    at = pl.multiple_of(h * HEAD_DIM, 8)
    for c in range(span // CHUNK):
        cols = slice(c * CHUNK, (c + 1) * CHUNK)
        scores = mm(keys, qkv_ref[0, 0, :, cols]) * (SCALE * LOG2E)
        top = jnp.max(scores, 0, keepdims=True)
        raised = jnp.exp2(scores - top)
        total = jnp.sum(raised, 0, keepdims=True)
        out = mm(vals, raised.astype(BF)) / total
        scr[pl.ds(at, HEAD_DIM), cols] = out[0:HEAD_DIM, :]
        lse_ref[0, 0:1, cols] = top + jnp.log2(total)

    @pl.when(h == pl.num_programs(0) - 1)
    def _():
        for k in range(slots):
            heads_ref[k] = scr[k * head_rows : (k + 1) * head_rows, :].astype(BF)


def attend(shape, scalars, qkv):
    slots = shape.slots
    _, heads, _, span = qkv.shape
    head_rows = heads * HEAD_DIM // slots
    out = (
        jax.ShapeDtypeStruct((heads, 1, span), F32),
        jax.ShapeDtypeStruct((slots, head_rows, span), BF),
    )
    return pl.pallas_call(
        partial(attend_kernel, slots),
        grid=(heads,),
        out_shape=out,
        in_specs=[smem(), pl.BlockSpec((3, 1, HEAD_PAD, span), lambda h: (0, h, 0, 0))],
        out_specs=(
            pl.BlockSpec((1, 1, span), lambda h: (h, 0, 0)),
            pl.BlockSpec(out[1].shape, lambda h: (0, 0, 0)),
        ),
        scratch_shapes=[pltpu.VMEM((slots * head_rows, span), F32)],
        compiler_params=pltpu.CompilerParams(vmem_limit_bytes=40 * MIB),
        cost_estimate=pl.CostEstimate(flops=4 * 10**9, bytes_accessed=60 * 10**6, transcendentals=5 * 10**6),
        name="attend",
    )(scalars, qkv)


def load_factors(fac, both, base, hidden_rows, tail):
    blank = jnp.zeros((LANES - 32, hidden_rows), BF)
    both[0, base : base + hidden_rows, tail] = jnp.concatenate([fac[0:32, :], blank], 0).T
    spread = jnp.concatenate([fac[32:48, :], jnp.zeros((16, hidden_rows), BF), blank], 0)
    both[1, base : base + hidden_rows, tail] = spread.T


def hidden_units(both, n2x, gx, acc_out, acc_back, eug, rdg, tail):
    rows = both.shape[1]
    inner_t = n2x[:, tail].T
    thr_t = gx[:, tail].T

    def units(at):
        we_c = both[0, at, :]
        wr_c = both[1, at, :]
        pre = mm(n2x[...], we_c, NT)
        grad_act = mm(gx[...], wr_c, NT)
        square = pre * pre
        th = jnp.tanh(pre * (0.7978845608028654 + 0.035677408136300125 * square))
        half = 0.5 * (1.0 + th)
        act = (pre * half).astype(BF)
        slope = half + pre * (0.5 * (1.0 - th * th)) * (
            0.7978845608028654 + 0.10703222440890037 * square
        )
        grad_pre = (grad_act * slope).astype(BF)
        acc_out[...] += mm(act, wr_c)
        acc_back[...] += mm(grad_pre, we_c)
        eug[:, at] = mm(inner_t[0:16, :], grad_pre)
        rdg[:, at] = mm(thr_t[0:16, :], act)

    def step(c, carry):
        units(pl.ds(pl.multiple_of(c * UNITS, UNITS), UNITS))
        return carry

    lax.fori_loop(0, rows // UNITS, step, 0)
    if rows % UNITS:
        units(slice(rows // UNITS * UNITS, rows))


def normalise(hidden):
    mean = jnp.mean(hidden, 1, keepdims=True)
    center = hidden - mean
    rstd = lax.rsqrt(jnp.mean(center * center, 1, keepdims=True) + EPS)
    return center * rstd, rstd


def merge_copies(parts, merge_hbm, wm, dim, sems):
    rows = dim // parts
    return [
        pltpu.make_async_copy(
            merge_hbm.at[t, pl.ds(0, rows), :], wm.at[pl.ds(t * rows, rows), pl.ds(0, dim)], sems.at[t]
        )
        for t in range(parts)
    ]


def pick_block(parts, which):
    out = parts[0]
    for n in range(1, len(parts)):
        out = jnp.where(which == n, parts[n], out)
    return out


def hidden_kernel(
    shape, turn, sc, vec_ref, tab_ref, fac_ref, rows_ref, own_expand, own_reduce, merge_hbm, own_cot, own_heads, *rest
):
    slots, groups, parts = shape.slots, shape.groups, shape.parts
    cots, rest = rest[: parts - 1], rest[parts - 1 :]
    heads_hbm, rest = (own_heads,) + rest[: groups - 1], rest[groups - 1 :]
    pieces, rest = rest[: slots - 1], rest[slots - 1 :]
    layer_ref, back_ref, gm_ref, gw_ref = rest[:4]
    kept, rest = (rest[4:9], rest[9:]) if turn == 0 else (None, rest[4:])
    both, wm, heads_in, cot_in, n2x, gx, acc_out, acc_back, eug, rdg = rest[:10]
    heads_sem, cot_sem, own_sem, merge_sem, w_sem = rest[10:]
    _, head_rows, span = heads_in.shape
    block = span // groups
    dim = parts * head_rows
    hidden_rows = both.shape[1] // slots
    size = 2 * hidden_rows // shape.copies
    half = shape.copies // 2
    tail = slice(dim, dim + LANES)
    cols = pl.ds(0, dim)
    mine, member, valid, ident = sc[0], sc[1], sc[2], sc[4]

    small = []
    for n, (k, g) in enumerate(shape.pairs):
        source = own_cot.at[mine] if n == 0 else cots[n - 1]
        spot = shape.source(mine, member, k, g)
        small.append(pltpu.make_async_copy(source, cot_in.at[spot], cot_sem.at[n]))
    for g in range(groups):
        for k in range(slots):
            spot = lax.rem(member - g + groups, groups) + groups * lax.rem(mine + k, slots)
            small.append(
                pltpu.make_async_copy(heads_hbm[g].at[k], heads_in.at[spot], heads_sem.at[g, k])
            )
    merges = merge_copies(parts, merge_hbm, wm, dim, merge_sem)
    mlps = [
        pltpu.make_async_copy(source, both.at[n, pl.ds(0, hidden_rows), cols], own_sem.at[n])
        for n, source in enumerate((own_expand, own_reduce))
    ]
    for k in range(1, slots):
        for d in range(shape.copies):
            start = k * hidden_rows + d % half * size
            mlps.append(
                pltpu.make_async_copy(
                    pieces[k - 1].at[d],
                    both.at[d // half, pl.ds(start, size), cols],
                    w_sem.at[k, d],
                )
            )
    for copy in small + merges + mlps:
        copy.start()
    for k in range(slots):
        load_factors(fac_ref[k], both, k * hidden_rows, hidden_rows, tail)
    acc_out[...] = jnp.zeros_like(acc_out)
    acc_back[...] = jnp.zeros_like(acc_back)
    for copy in small:
        copy.wait()
    for t in range(parts):
        lines = cot_in[t, head_rows : head_rows + 16, 0:head_rows]
        lines = jnp.concatenate([lines, jnp.zeros((LANES - 16, head_rows), BF)], 0).T
        wm[t * head_rows : (t + 1) * head_rows, tail] = lines
    which = lax.rem(member + turn, groups)
    blocks = [slice(g * block, (g + 1) * block) for g in range(groups)]
    cot = pick_block([cot_in[:, 0:head_rows, at] for at in blocks], which)
    grads = cot.reshape(dim, block).T * valid.astype(F32).astype(BF)
    gx[:, 0:dim] = grads
    gx[:, tail] = (0.5 * mm(grads, tab_ref[2], NT)).astype(BF)
    heads = pick_block([heads_in[:, :, at] for at in blocks], which).reshape(dim, block).T
    for copy in merges:
        copy.wait()
    lane = lax.broadcasted_iota(jnp.int32, (block, LANES), 1)
    merged = mm(heads, wm[...])
    inner_m = (0.5 * merged[:, tail]).astype(BF)
    hidden = rows_ref[which].T.astype(F32) + merged[:, :dim] + mm(inner_m, tab_ref[0]) + vec_ref[0:1, :]
    unit, _ = normalise(hidden)
    n2 = (unit * vec_ref[2:3, :] + vec_ref[3:4, :]).astype(BF)
    n2x[:, 0:dim] = n2
    n2x[:, tail] = jnp.where(lane == 16, 1.0, 0.5 * mm(n2, tab_ref[1], NT)).astype(BF)
    if kept:
        for ref, value in zip(kept, (hidden, heads, inner_m, grads, wm[:, tail]), strict=True):
            ref[...] = value
    for copy in mlps:
        copy.wait()
    hidden_units(both, n2x, gx, acc_out, acc_back, eug, rdg, tail)

    inner_r = (0.5 * acc_out[:, tail]).astype(BF)
    thr_e = (0.5 * acc_back[:, tail]).astype(BF)
    layer = acc_out[:, 0:dim] + mm(inner_r, tab_ref[2])
    if kept:
        layer = layer + kept[0][...] + vec_ref[1:2, :]
    layer = layer.T.astype(BF)
    for t in range(parts):
        layer_ref[t] = layer[t * head_rows : (t + 1) * head_rows, :]
    back_ref[...] = (acc_back[:, 0:dim] + mm(thr_e, tab_ref[1])).astype(back_ref.dtype)
    whole = (
        mm(thr_e, n2x[:, 0:dim], TN)[0:16, :],
        mm(inner_r, gx[:, 0:dim], TN)[0:16, :],
    )
    ids = jnp.full((32, LANES), ident, jnp.int32).astype(F32)
    if turn:
        ids = jnp.zeros_like(ids)
    gw_ref[...] = jnp.concatenate([jnp.concatenate(whole, 0), ids], 1).astype(BF)
    blank = jnp.zeros((16, 2 * (dim + LANES) - 2 * hidden_rows), F32)
    for k in range(slots):
        at = slice(k * hidden_rows, (k + 1) * hidden_rows)
        line = jnp.concatenate([eug[:, at], rdg[:, at], blank], 1)
        gm_ref[k, 0:16, :] = line[:, 0 : dim + LANES].astype(BF)
        gm_ref[k, 16:32, :] = line[:, dim + LANES :].astype(BF)


def hidden_part(shape, turn, scalars, vec, tab, fac, rows, own_w, merge, own_cot, cots, heads, pieces):
    slots, groups, parts = shape.slots, shape.groups, shape.parts
    own_heads, others = heads
    _, head_rows, span = own_heads.shape
    block = span // groups
    dim = parts * head_rows
    hidden_rows = fac.shape[2]
    count = slots * hidden_rows
    out = (
        jax.ShapeDtypeStruct((parts, head_rows, block), BF),
        jax.ShapeDtypeStruct((block, dim), BF if turn else F32),
        jax.ShapeDtypeStruct((slots, 32, dim + LANES), BF),
        jax.ShapeDtypeStruct((32, dim + LANES), BF),
    )
    if turn == 0:
        out += (
            jax.ShapeDtypeStruct((block, dim), F32),
            jax.ShapeDtypeStruct((block, dim), BF),
            jax.ShapeDtypeStruct((block, LANES), BF),
            jax.ShapeDtypeStruct((block, dim), BF),
            jax.ShapeDtypeStruct((dim, LANES), BF),
        )
    inputs = 5 + len(cots) + len(others) + len(pieces)
    return pl.pallas_call(
        partial(hidden_kernel, shape, turn),
        out_shape=out,
        in_specs=[smem()] + [vmem()] * 4 + [anywhere()] * inputs,
        out_specs=tuple(vmem() for _ in out),
        scratch_shapes=[
            pltpu.VMEM((2, count, dim + LANES), BF),
            pltpu.VMEM((dim, dim + LANES), BF),
            pltpu.VMEM((parts, head_rows, span), BF),
            pltpu.VMEM((parts,) + own_cot.shape[1:], BF),
            pltpu.VMEM((block, dim + LANES), BF),
            pltpu.VMEM((block, dim + LANES), BF),
            pltpu.VMEM((block, dim + LANES), F32),
            pltpu.VMEM((block, dim + LANES), F32),
            pltpu.VMEM((16, count), F32),
            pltpu.VMEM((16, count), F32),
            pltpu.SemaphoreType.DMA((groups, slots)),
            pltpu.SemaphoreType.DMA((parts,)),
            pltpu.SemaphoreType.DMA((2,)),
            pltpu.SemaphoreType.DMA((parts,)),
            pltpu.SemaphoreType.DMA((slots, shape.copies)),
        ],
        compiler_params=pltpu.CompilerParams(vmem_limit_bytes=62 * MIB),
        cost_estimate=pl.CostEstimate(flops=10 * 10**9, bytes_accessed=60 * 10**6, transcendentals=10**6),
        name="hidden_part",
    )(scalars, vec, tab, fac, rows, *own_w, merge, own_cot, own_heads, *cots, *others, *pieces)


def branch_kernel(shape, sc, vec_ref, tab_ref, merge_hbm, *rest):
    slots, groups, parts = shape.slots, shape.groups, shape.parts
    inputs, rest = rest[: groups + 5], rest[groups + 5 :]
    resid_ref, back_ref, gw_ref, wm, sem, in_sem = rest[:6]
    held = rest[6:]
    own_back, hidden_ref, heads_ref, inner_ref, grads_ref, tails_ref = held[:6]
    others = held[6:]
    _, dim = hidden_ref.shape
    head_rows = dim // parts
    mine, ident = sc[0], sc[4]
    merges = merge_copies(parts, merge_hbm, wm, dim, sem)
    loads = [
        pltpu.make_async_copy(source, dest, in_sem.at[n])
        for n, (source, dest) in enumerate(zip(inputs, held, strict=True))
    ]
    for copy in loads + merges:
        copy.start()
    for copy in loads:
        copy.wait()
    total = own_back[...]
    for other in others:
        total = total + other[...].astype(F32)
    scaled = total * vec_ref[2:3, :]
    unit, rstd = normalise(hidden_ref[...])
    first = jnp.mean(scaled, 1, keepdims=True)
    second = jnp.mean(scaled * unit, 1, keepdims=True)
    grad_hidden = grads_ref[...].astype(F32) + rstd * (scaled - first - unit * second)
    branch = grad_hidden.astype(BF)
    thr_m = (0.5 * mm(branch, tab_ref[0], NT)).astype(BF)
    resid_ref[...] = grad_hidden.T
    whole = (
        mm(inner_ref[...], branch, TN)[0:16, :],
        mm(thr_m, heads_ref[...], TN)[0:16, :],
    )
    ids = jnp.full((32, LANES), ident, jnp.int32).astype(F32)
    gw_ref[...] = jnp.concatenate([jnp.concatenate(whole, 0), ids], 1).astype(BF)
    for copy in merges:
        copy.wait()
    grad_heads = (mm(branch, wm[...], NT) + mm(thr_m, tails_ref[...], NT)).T.astype(BF)
    for t in range(parts):
        at = slice(t * head_rows, (t + 1) * head_rows)
        back_ref[t % groups, lax.rem(t // groups - mine + slots, slots)] = grad_heads[at, :]


def branch_part(shape, scalars, vec, tab, kept, merge, others):
    slots, groups, parts = shape.slots, shape.groups, shape.parts
    block, dim = kept[0].shape
    out = (
        jax.ShapeDtypeStruct((dim, block), F32),
        jax.ShapeDtypeStruct((groups, slots, dim // parts, block), BF),
        jax.ShapeDtypeStruct((32, dim + LANES), BF),
    )
    return pl.pallas_call(
        partial(branch_kernel, shape),
        out_shape=out,
        in_specs=[smem()] + [vmem()] * 2 + [anywhere()] * (1 + len(kept) + len(others)),
        out_specs=tuple(vmem() for _ in out),
        scratch_shapes=[
            pltpu.VMEM((dim, dim), BF),
            pltpu.SemaphoreType.DMA((parts,)),
            pltpu.SemaphoreType.DMA((len(kept) + len(others),)),
        ]
        + [pltpu.VMEM(x.shape, x.dtype) for x in (*kept, *others)],
        compiler_params=pltpu.CompilerParams(vmem_limit_bytes=48 * MIB),
        cost_estimate=pl.CostEstimate(flops=2 * 10**9, bytes_accessed=10**7, transcendentals=0),
        name="branch_part",
    )(scalars, vec, tab, merge, *kept, *others)


def heads_back_kernel(shape, slot, sc, qkv_ref, lse_ref, own_dout, *rest):
    groups = shape.groups
    douts = (own_dout,) + rest[: groups - 1]
    out_ref, dout_rel, dot_scr, grad_scr, sem = rest[groups - 1 :]
    _, head_rows, block = dout_rel.shape
    span = groups * block
    heads_here = head_rows // HEAD_DIM
    member = sc[1]
    h = pl.program_id(0)

    @pl.when(h == 0)
    def _():
        copies = []
        for g in range(groups):
            source = own_dout.at[member, slot] if g == 0 else douts[g].at[slot]
            spot = lax.rem(member - g + groups, groups)
            copies.append(pltpu.make_async_copy(source, dout_rel.at[spot], sem.at[g]))
        run_all(copies)
        pad = jnp.zeros((HEAD_PAD - HEAD_DIM, block), F32)
        for g in range(groups):
            piece = dout_rel[g].astype(F32)
            for n in range(heads_here):
                one = jnp.concatenate([piece[n * HEAD_DIM : (n + 1) * HEAD_DIM, :], pad], 0)
                dot_scr[n, :, g * block : (g + 1) * block] = one.astype(BF)

    query_t = qkv_ref[0, 0]
    keys_t = qkv_ref[1, 0]
    query = query_t.T
    keys = keys_t.T
    vals = qkv_ref[2, 0].T
    dout_t = dot_scr[h]
    dout = dout_t.T
    dvals = jnp.zeros((span, HEAD_PAD), F32)
    dkeys = jnp.zeros((span, HEAD_PAD), F32)
    row = pl.multiple_of(h * HEAD_DIM, 8)
    for c in range(span // CHUNK):
        cols = slice(c * CHUNK, (c + 1) * CHUNK)
        scores = mm(keys, query_t[:, cols]) * (SCALE * LOG2E)
        probs = jnp.exp2(scores - lse_ref[0, 0:1, cols])
        dprobs = mm(vals, dout_t[:, cols])
        delta = jnp.sum(probs * dprobs, 0, keepdims=True)
        dscores = (probs * (dprobs - delta)).astype(BF)
        dvals += mm(probs.astype(BF), dout[cols, :])
        dkeys += mm(dscores, query[cols, :])
        dquery = mm(keys_t, dscores) * SCALE
        grad_scr[pl.ds(row, HEAD_DIM), cols] = dquery[0:HEAD_DIM, :]
    row = pl.multiple_of(row + head_rows, 8)
    grad_scr[pl.ds(row, HEAD_DIM), :] = (dkeys * SCALE).T[0:HEAD_DIM, :]
    row = pl.multiple_of(row + head_rows, 8)
    grad_scr[pl.ds(row, HEAD_DIM), :] = dvals.T[0:HEAD_DIM, :]

    @pl.when(h == heads_here - 1)
    def _():
        out_ref[...] = grad_scr[...].astype(BF)


def heads_back(shape, slot, scalars, qkv, lse, dout):
    own, others = dout
    groups, _, head_rows, block = own.shape
    span = groups * block
    heads_here = head_rows // HEAD_DIM
    return pl.pallas_call(
        partial(heads_back_kernel, shape, slot),
        grid=(heads_here,),
        out_shape=jax.ShapeDtypeStruct((3 * head_rows, span), BF),
        in_specs=[
            smem(),
            pl.BlockSpec((3, 1, HEAD_PAD, span), lambda h: (0, slot * heads_here + h, 0, 0)),
            pl.BlockSpec((1, 1, span), lambda h: (slot * heads_here + h, 0, 0)),
            anywhere(),
        ]
        + [anywhere()] * len(others),
        out_specs=pl.BlockSpec((3 * head_rows, span), lambda h: (0, 0)),
        scratch_shapes=[
            pltpu.VMEM((groups, head_rows, block), BF),
            pltpu.VMEM((heads_here, HEAD_PAD, span), BF),
            pltpu.VMEM((3 * head_rows, span), F32),
            pltpu.SemaphoreType.DMA((groups,)),
        ],
        compiler_params=pltpu.CompilerParams(vmem_limit_bytes=40 * MIB),
        cost_estimate=pl.CostEstimate(flops=10**9, bytes_accessed=40 * 10**6, transcendentals=0),
        name="heads_back",
    )(scalars, qkv, lse, own, *others)


def rank_back_kernel(shape, sc, down_ref, upx_ref, n1_ref, inner_ref, *rest):
    slots = shape.slots
    grads = rest[:slots]
    td_ref, tu_ref, thr_ref = rest[slots:]
    dim, span = n1_ref.shape
    head_rows = upx_ref.shape[2] // 3
    ident = sc[4]
    rank = down_ref.shape[0]
    spread = 3 * head_rows
    thr = jnp.zeros((rank, span), F32)
    row_of = lax.broadcasted_iota(jnp.int32, (rank, spread), 0) // 16
    part_of = lax.broadcasted_iota(jnp.int32, (rank, spread), 1) // head_rows
    for k in range(slots):
        thr = thr + mm(upx_ref[k], grads[k][...])
        ups = mm(inner_ref[...], grads[k][...], NT)
        ups = jnp.where(row_of == part_of, ups, 0.0)
        ups = ups[0:16, :] + ups[16:32, :] + ups[32:48, :]
        blank = jnp.zeros((16, dim + LANES - spread), F32)
        tu_ref[k] = jnp.concatenate([ups, blank], 1).astype(BF)
    line = lax.broadcasted_iota(jnp.int32, (rank, span), 0)
    thr_b = jnp.where(line < 48, 0.5 * thr, 0.0).astype(BF)
    thr_ref[...] = thr_b
    downs = mm(thr_b, n1_ref[...], NT)
    ids = jnp.full((48, LANES), ident, jnp.int32).astype(F32)
    td_ref[...] = jnp.concatenate([downs[0:48, :], ids], 1).astype(BF)


def rank_back(shape, scalars, down, upx, n1, inner, grads):
    slots = shape.slots
    dim, span = n1.shape
    out = (
        jax.ShapeDtypeStruct((48, dim + LANES), BF),
        jax.ShapeDtypeStruct((slots, 16, dim + LANES), BF),
        jax.ShapeDtypeStruct((down.shape[0], span), BF),
    )
    return pl.pallas_call(
        partial(rank_back_kernel, shape),
        out_shape=out,
        in_specs=[smem()] + [vmem()] * (4 + slots),
        out_specs=(vmem(), vmem(), vmem()),
        compiler_params=pltpu.CompilerParams(vmem_limit_bytes=40 * MIB),
        cost_estimate=pl.CostEstimate(flops=10**9, bytes_accessed=40 * 10**6, transcendentals=0),
        name="rank_back",
    )(scalars, down, upx, n1, inner, *grads)


def norm_back_kernel(shape, sc, norm_ref, down_ref, thr_ref, stats_ref, rows_ref, resid_ref, own_w, *rest):
    slots, groups, parts = shape.slots, shape.groups, shape.parts
    foreign = rest[: 2 * (slots - 1)]
    rest = rest[2 * (slots - 1) :]
    grads = rest[:slots]
    out_ref, weights, e1_scr, sem = rest[slots:]
    _, dim, block = rows_ref.shape
    span = groups * block
    width = dim // parts
    spread = own_w.shape[0]
    member, row = sc[1], sc[3]
    run_all(weight_copies(shape, row, own_w, foreign, weights, sem))

    def final_step(c, carry):
        cols = pl.ds(pl.multiple_of(c * CHUNK, CHUNK), CHUNK)
        total = mm(down_ref[...], thr_ref[:, cols], TN)
        for k in range(slots):
            total = total + mm(weights[k, 0:spread, :], grads[k][:, cols], TN)
        e1_scr[:, cols] = total * norm_ref[:, 0:1]
        return carry

    lax.fori_loop(0, span // CHUNK, final_step, 0)
    for g in range(groups):
        cols = slice(g * block, (g + 1) * block)
        e1 = e1_scr[:, cols]
        first = jnp.sum(e1, 0, keepdims=True)
        mean, rstd = stats_ref[0:1, cols], stats_ref[1:2, cols]
        unit = (rows_ref[g].astype(F32) - mean) * rstd
        second = jnp.sum(e1 * unit, 0, keepdims=True)
        lines = []
        for value in (first, second, mean, rstd):
            high = value.astype(BF).astype(F32)
            lines += [high, value - high]
        lines = jnp.concatenate(lines + [jnp.zeros((8, block), F32)], 0).astype(BF)
        e1 = e1 + resid_ref[...] * (jnp.where(member == g, 1.0, 0.0) / rstd)
        for t in range(parts):
            out_ref[t, 0:width, cols] = e1[t * width : (t + 1) * width, :].astype(BF)
            out_ref[t, width : width + 16, cols] = lines


def norm_back(shape, scalars, norm, down, thr, stats, rows, resid, own_w, foreign, grads):
    slots, parts = shape.slots, shape.parts
    groups, dim, block = rows.shape
    span = groups * block
    weight_rows = max([own_w.shape[0]] + [w.shape[1] * shape.copies for w in foreign])
    return pl.pallas_call(
        partial(norm_back_kernel, shape),
        out_shape=jax.ShapeDtypeStruct((parts, dim // parts + 16, span), BF),
        in_specs=[smem()] + [vmem()] * 6 + [anywhere()] * (1 + len(foreign)) + [vmem()] * slots,
        out_specs=vmem(),
        scratch_shapes=[
            pltpu.VMEM((slots, weight_rows, dim), BF),
            pltpu.VMEM((dim, span), F32),
            pltpu.SemaphoreType.DMA((1 + (slots - 1) * shape.copies,)),
        ],
        compiler_params=pltpu.CompilerParams(vmem_limit_bytes=48 * MIB),
        cost_estimate=pl.CostEstimate(flops=10**9, bytes_accessed=40 * 10**6, transcendentals=0),
        name="norm_back",
    )(scalars, norm, down, thr, stats, rows, resid, own_w, *foreign, *grads)


def tokens_kernel(shape, seq, img_ref, held, out_ref):
    slots, groups, parts = shape.slots, shape.groups, shape.parts
    _, width, span = img_ref.shape
    dim = parts * width
    for n in range(slots):
        total = held[n * groups].astype(F32)
        lines = total[width : width + 16, :]
        mean = lines[4:5, :] + lines[5:6, :]
        rstd = lines[6:7, :] + lines[7:8, :]
        for g in range(1, groups):
            total = total + held[n * groups + g].astype(F32)
        first = (total[width : width + 1, :] + total[width + 1 : width + 2, :]) / dim
        second = (total[width + 2 : width + 3, :] + total[width + 3 : width + 4, :]) / dim
        unit = (img_ref[n].astype(F32) - mean) * rstd
        grad = rstd * (total[0:width, :] - first - unit * second)
        out_ref[:, n * seq : (n + 1) * seq] = grad[:, 0:seq]


def tokens_result(shape, seq, images, last):
    _, width, _ = images.shape
    return pl.pallas_call(
        partial(tokens_kernel, shape, seq),
        out_shape=jax.ShapeDtypeStruct((width, shape.slots * seq), F32),
        in_specs=[vmem(), vmem()],
        out_specs=vmem(),
        compiler_params=pltpu.CompilerParams(vmem_limit_bytes=40 * MIB),
        cost_estimate=pl.CostEstimate(flops=10**5, bytes_accessed=10**5, transcendentals=0),
        name="tokens_result",
    )(images, last)


def layer_kernel(shape, seq, sc, *rest):
    groups = shape.groups
    turns, out_ref = rest[:groups], rest[groups]
    for n in range(shape.slots):
        blocks = []
        for at in range(groups):
            total = turns[0][n * groups + at].astype(F32)
            for g in range(1, groups):
                total = total + turns[g][n * groups + (at - g) % groups].astype(F32)
            blocks.append(total)
        image = jnp.concatenate(blocks, 1)
        out_ref[:, n * seq : (n + 1) * seq] = image[:, 0:seq].astype(BF)


def layer_result(shape, seq, scalars, layers):
    _, width, _ = layers[0].shape
    return pl.pallas_call(
        partial(layer_kernel, shape, seq),
        out_shape=jax.ShapeDtypeStruct((width, shape.slots * seq), BF),
        in_specs=[smem()] + [vmem()] * len(layers),
        out_specs=vmem(),
        compiler_params=pltpu.CompilerParams(vmem_limit_bytes=40 * MIB),
        cost_estimate=pl.CostEstimate(flops=10**5, bytes_accessed=10**5, transcendentals=0),
        name="layer_result",
    )(scalars, *layers)


def summed(terms_ref, first, rows, adapter, count):
    images, _, cols = terms_ref.shape
    lines = slice(first, first + rows)
    total = jnp.zeros((rows, cols), F32)
    for e in range(images):
        which = terms_ref[e, 0:1, cols - 1 : cols].astype(F32)
        chosen = jnp.where(jnp.abs(which - adapter * count) < 0.5, 1.0, 0.0)
        total = total + terms_ref[e, lines, :].astype(F32) * chosen
    return total


def block_terms_kernel(count, padded, terms_ref, merge_ref, expand_ref, reduce_ref, eu_ref, rd_ref, md_ref):
    adapters, _, dim = merge_ref.shape
    hidden = eu_ref.shape[2]
    for a in range(adapters):
        whole = summed(terms_ref, 0, 64, a, count)
        for n, ref in enumerate((merge_ref, expand_ref, reduce_ref, md_ref)):
            ref[a] = whole[16 * n : 16 * n + 16, 0:dim]
        parts = summed(terms_ref, 64, 32, a, count)
        parts = jnp.concatenate([parts[0:16, :], parts[16:32, :]], 1)
        eu_ref[a] = parts[:, 0:hidden]
        rd_ref[a] = parts[:, padded : padded + hidden]


def triple_terms_kernel(count, terms_ref, down_ref, up_ref):
    _, adapters, _, dim = down_ref.shape
    rows = up_ref.shape[3]
    for a in range(adapters):
        downs = summed(terms_ref, 0, 48, a, count)
        ups = summed(terms_ref, 48, 16, a, count)
        for j in range(3):
            down_ref[j, a] = downs[16 * j : 16 * j + 16, 0:dim]
            up_ref[j, a] = ups[:, j * rows : (j + 1) * rows]


def by_adapter(kernel, terms, shapes, name):
    out = tuple(jax.ShapeDtypeStruct(one, F32) for one in shapes)
    return pl.pallas_call(
        kernel,
        out_shape=out,
        in_specs=[vmem()],
        out_specs=tuple(vmem() for _ in out),
        compiler_params=pltpu.CompilerParams(vmem_limit_bytes=40 * MIB),
        cost_estimate=pl.CostEstimate(flops=10**5, bytes_accessed=10**5, transcendentals=0),
        name=name,
    )(terms)


def shards(
    tokens,
    cotangent,
    adapter_index,
    valid_image,
    first_gain,
    first_shift,
    triple_weight,
    triple_bias,
    triple_down,
    triple_up,
    merge_weight,
    merge_bias,
    merge_down,
    merge_up,
    second_gain,
    second_shift,
    expand_weight,
    expand_bias,
    expand_down,
    expand_up,
    reduce_weight,
    reduce_bias,
    reduce_down,
    reduce_up,
    *,
    parts,
    copies,
):
    slots = adapter_index.shape[0]
    shape = Shape(parts, slots, copies)
    groups = shape.groups
    seq = tokens.shape[0] // slots
    width = tokens.shape[1]
    dim = width * parts
    head_rows = triple_weight.shape[2]
    adapters = triple_down.shape[1]
    span = up_to(seq, CHUNK)
    block = span // groups
    place = lax.axis_index("tensor")
    row = lax.axis_index("dp")
    mine, member = place // groups, place % groups

    def at(x, n, axis=0):
        return lax.dynamic_index_in_dim(x, n, axis, False)

    def jump(x, k, g):
        perm = [
            (s, ((s // groups + k) % slots) * groups + (s % groups + g) % groups)
            for s in range(parts)
        ]
        return lax.ppermute(x, "tensor", perm)

    def swap(x):
        return lax.all_to_all(x, "tensor", 0, 0)

    def spread_images(x):
        first = [at(x, mine)] + [jump(at(x, (mine + k) % slots), k, 0) for k in range(1, slots)]
        out = []
        for x_k in first:
            out.append(x_k)
            out += [jump(x_k, 0, g) for g in range(1, groups)]
        return out

    def cross(x, bit):
        return lax.ppermute(x, "dp", [(d, d ^ bit) for d in range(copies)])

    def widen(near, bits):
        for bit in bits:
            near = jnp.concatenate([near, cross(near, bit)], 0)
        return near

    def hyper(near, order):
        near = widen(near, order[:-1])
        return [near, cross(near, order[-1])]

    def after(x, *others):
        return lax.optimization_barrier((x, *others))[0]

    def images_of(x):
        flat = x.T
        return jnp.stack(
            [
                jnp.pad(flat[:, n * seq : (n + 1) * seq], ((0, 0), (0, span - seq)))
                for n in range(slots)
            ]
        )

    images = images_of(tokens)
    tok_first = [at(images, (mine + k) % slots) for k in range(slots)]
    tok_first, adapter_index, triple_weight, valid_image, expand_weight, reduce_weight = (
        lax.optimization_barrier(
            (tok_first, adapter_index, triple_weight, valid_image, expand_weight, reduce_weight)
        )
    )
    toks = [tok_first[0]] + [jump(tok_first[k], k, 0) for k in range(1, slots)]
    ready = toks[slots - 1]
    toks = [x if g == 0 else jump(x, 0, g) for x in toks for g in range(groups)][1:]

    index = at(adapter_index, mine)
    valid = at(valid_image, mine)
    scalars = jnp.stack([mine, member, valid, row, index, place]).astype(jnp.int32)

    flat_triple = triple_weight.transpose(0, 2, 1).reshape(3 * head_rows, dim)
    piece_rows = up_to(3 * head_rows, 16 * copies) // copies
    padded = jnp.pad(flat_triple, ((0, piece_rows * copies - 3 * head_rows), (0, 0)))
    my_piece = lax.dynamic_slice_in_dim(padded, row * piece_rows, piece_rows, 0)

    def up_pack(which):
        table = at(triple_up, which, 1).transpose(1, 0, 2).reshape(16, 3 * head_rows)
        bias = jnp.pad(triple_bias.reshape(1, 3 * head_rows), ((0, 15), (0, 0)))
        return jnp.pad(jnp.concatenate([table, bias], 0), ((0, 0), (0, dim - 3 * head_rows)))

    foreign, ups, arrived = [], [up_pack(index)], [ready]
    for k in range(1, slots):
        packed = up_pack(at(adapter_index, (mine - k) % slots))
        got = jump(jnp.concatenate([my_piece, packed], 0), -k, 0)
        arrived.append(got)
        ups.append(got[piece_rows:])
        foreign += hyper(got[None, :piece_rows], shape.bits)
    ups = jnp.stack(ups)
    ready = after(*arrived, toks[-1])

    merge_rows = up_to(width, 16 * copies) // copies
    merge_piece = lax.dynamic_slice_in_dim(
        jnp.pad(merge_weight, ((0, merge_rows * copies - width), (0, 0))), row * merge_rows, merge_rows, 0
    )
    hidden_here = reduce_weight.shape[0]
    hidden_rows = up_to(hidden_here, 8 * copies)
    extra = ((0, hidden_rows - hidden_here), (0, 0))
    mlp_rows = 2 * hidden_rows // copies
    half = copies // 2

    def mlp_part(x):
        return lax.dynamic_slice_in_dim(jnp.pad(x, extra), (row % half) * mlp_rows, mlp_rows, 0)

    my_w = jnp.where(row < half, mlp_part(expand_weight.T), mlp_part(reduce_weight))
    natural = ((1, 0, None),)
    near_masks = list(range(0, copies, 2))
    merge_all = lax.all_gather(merge_piece, ("tensor", "dp")).reshape(parts, merge_rows * copies, dim)
    late_w = after(my_w, ready)
    pieces = [jump(late_w, -k, 0) for k in range(1, slots)]
    own_expand = jnp.pad(after(expand_weight.T, ready), extra)
    own_reduce = jnp.pad(after(reduce_weight, ready), extra)

    down = jnp.pad(at(triple_down, index, 1).transpose(0, 2, 1).reshape(48, dim), ((0, 16), (0, 0)))
    norm = jnp.pad(jnp.stack([first_gain, first_shift], 1).astype(F32), ((0, 0), (0, 6)))

    late_index = after(adapter_index, ready)

    def factor_pack(which):
        def lanes(x):
            return jnp.pad(x, ((0, 16 - x.shape[0]), (0, hidden_rows - x.shape[1])))

        return jnp.concatenate(
            [lanes(at(expand_up, which)), lanes(expand_bias[None, :]), lanes(at(reduce_down, which).T)], 0
        )

    packs = [factor_pack(at(late_index, (mine - k) % slots)) for k in range(slots)]
    late = after(index, ready)
    tab = jnp.stack(
        [
            jnp.pad(x, ((0, LANES - 16), (0, 0)))
            for x in (at(merge_up, late), at(expand_down, late).T, at(reduce_up, late))
        ]
    )
    vec = jnp.pad(
        jnp.stack([merge_bias, reduce_bias, second_gain, second_shift]).astype(F32), ((0, 4), (0, 0))
    )

    merge_lines = [at(merge_down, late_index[n]).T for n in range(slots)]
    merge_lines = jnp.pad(jnp.stack(merge_lines), ((0, 0), (0, 0), (0, span - width)))
    cot_parts = jnp.concatenate([images_of(after(cotangent, ready)), merge_lines], 1)

    def trade(x):
        return x, [jump(at(x, (member + g) % groups), 0, g) for g in range(1, groups)]

    begin = after(scalars, own_expand, own_reduce, tab, vec, cot_parts, *packs)
    qkv, n1, stats, inner, rows, upx = project(
        shape, seq, begin, norm, down, ups, images, toks, flat_triple, foreign
    )
    fac = [packs[0]] + [jump(packs[k], -k, 0) for k in range(1, slots)]
    cots = {(k, 0): jump(at(cot_parts, (mine + k) % slots), k, 0) for k in range(1, slots)}
    own_cot = at(cot_parts, mine)
    cots.update({(0, g): jump(own_cot, 0, g) for g in range(1, groups)})
    pieces, cots = lax.optimization_barrier((pieces, cots, stats))[:2]
    pieces = [lax.all_gather(x, "dp") for x in pieces]
    begin = after(scalars, *cots.values())
    cots.update({(k, g): jump(cots[k, 0], 0, g) for k in range(1, slots) for g in range(1, groups)})
    lse, heads = attend(shape, begin, qkv)
    heads, cots, fac = lax.optimization_barrier((heads, cots, fac))
    heads = (heads, [jump(heads, 0, g) for g in range(1, groups)])
    fac = jnp.stack(fac)
    cots = [cots[pair] for pair in shape.pairs[1:]]
    layers, near, gms, gws = [None] * groups, [], [], []
    for turn in list(range(1, groups)) + [0]:
        begin = scalars
        layers[turn], back, gm, gw, *kept = hidden_part(
            shape,
            turn,
            begin,
            vec,
            tab,
            fac,
            rows,
            (own_expand, own_reduce),
            merge_all,
            cot_parts,
            cots,
            heads,
            pieces,
        )
        gms.append(gm)
        gws.append(gw)
        if turn:
            near.append(jump(back, 0, turn))
            scalars = after(scalars, back)
    near, layers[1:], kept = lax.optimization_barrier((near, layers[1:], kept))
    layers[1:] = [swap(x) for x in layers[1:]]
    resid, back, gw_branch = branch_part(
        shape, scalars, vec, tab, [back] + kept, merge_all, near
    )
    dout = trade(back)

    def spread_rows(x):
        share = x.shape[0] // copies
        own = lax.dynamic_slice_in_dim(x, row * share, share, 0)
        return jnp.stack([own] + [jump(own, k, g) for k, g in shape.pairs[1:]])

    def members_sum(x, beside):
        out, rows = [], x.shape[0]
        for k in range(slots):
            both = jnp.concatenate([x, beside[k]], 0)
            both = jump(both, k, 0) if k else both
            total = both[:rows].astype(F32)
            for g in range(1, groups):
                total = total + jump(x, k, g).astype(F32)
            out.append(jnp.concatenate([total.astype(BF), both[rows:]], 0))
        return jnp.stack(out)

    layers[0] = swap(layers[0])
    grads = [heads_back(shape, 0, after(scalars, *layers[1:]), qkv, lse, dout)]
    gms, gws, gw_branch, begin = lax.optimization_barrier((gms, gws, gw_branch, scalars, grads[0]))[:4]
    gm = sum(x.astype(F32) for x in gms).astype(BF)
    gw = sum(x.astype(F32) for x in gws).astype(BF)
    gm = members_sum(jnp.concatenate([gw_branch[0:16], gw, gw_branch[16:32]], 0), gm)
    for k in range(1, slots):
        grads.append(heads_back(shape, k, after(begin, layers[0]), qkv, lse, dout))
    gm = after(gm, grads[-1])
    td, tu, thr = rank_back(shape, after(scalars, gm), down, upx, n1, inner, grads)
    td = members_sum(td, tu)
    last = norm_back(shape, scalars, norm, down, thr, stats, rows, resid, flat_triple, foreign, grads)
    last, td = lax.optimization_barrier((last, td))
    last = swap(last)
    gm = lax.all_gather(gm, "dp", tiled=True)
    near = jnp.concatenate([td] + [cross(td, mask) for mask in near_masks[1:]], 0)
    merge_up_grad, expand_down_grad, reduce_up_grad, expand_up_grad, reduce_down_grad, merge_down_grad = by_adapter(
        partial(block_terms_kernel, groups, hidden_rows),
        gm,
        ((adapters, 16, dim),) * 3 + ((adapters, 16, hidden_here),) * 2 + ((adapters, 16, dim),),
        "block_terms",
    )
    merge_down_grad = lax.dynamic_slice_in_dim(merge_down_grad, place * width, width, 2)
    td = jnp.concatenate([near, cross(near, 1)], 0)
    layer_out = layer_result(shape, seq, after(scalars, gm), layers).T
    downs, triple_up_grad = by_adapter(
        partial(triple_terms_kernel, groups),
        td,
        ((3, adapters, 16, dim), (3, adapters, 16, head_rows)),
        "triple_terms",
    )
    tokens_grad = tokens_result(shape, seq, after(images, downs), last).T

    return (
        layer_out,
        tokens_grad,
        downs.transpose(0, 1, 3, 2),
        triple_up_grad,
        merge_down_grad.transpose(0, 2, 1),
        merge_up_grad,
        expand_down_grad.transpose(0, 2, 1),
        expand_up_grad,
        reduce_down_grad.transpose(0, 2, 1),
        reduce_up_grad,
    )


def solution(mesh):
    in_specs = (
        P("dp", "tensor"),
        P("dp", "tensor"),
        P("dp"),
        P("dp"),
        P(),
        P(),
        P(None, None, "tensor"),
        P(None, "tensor"),
        P(),
        P(None, None, None, "tensor"),
        P("tensor", None),
        P(),
        P(None, "tensor", None),
        P(),
        P(),
        P(),
        P(None, "tensor"),
        P("tensor"),
        P(),
        P(None, None, "tensor"),
        P("tensor", None),
        P(),
        P(None, "tensor", None),
        P(),
    )
    out_specs = (
        P("dp", "tensor"),
        P("dp", "tensor"),
        P(),
        P(None, None, None, "tensor"),
        P(None, "tensor", None),
        P(),
        P(),
        P(None, None, "tensor"),
        P(None, "tensor", None),
        P(),
    )
    return jax.shard_map(
        partial(shards, parts=mesh.shape["tensor"], copies=mesh.shape["dp"]),
        mesh=mesh,
        in_specs=in_specs,
        out_specs=out_specs,
        check_vma=False,
    )
```

```python
import math
from functools import partial

import jax
import jax.numpy as jnp
from jax import lax
from jax.experimental import pallas as pl
from jax.experimental.pallas import tpu as pltpu
from jax.sharding import PartitionSpec as P

HEAD_DIM = 72
HEAD_PAD = 80
LANES = 128
CHUNK = 256
UNITS = 512
EPS = 1e-06
BF = jnp.bfloat16
F32 = jnp.float32
SCALE = 1.0 / math.sqrt(HEAD_DIM)
LOG2E = 1.4426950408889634
MIB = 1024 * 1024

NN = (((1,), (0,)), ((), ()))
NT = (((1,), (1,)), ((), ()))
TN = (((0,), (0,)), ((), ()))


def mm(a, b, dims=NN):
    return lax.dot_general(a, b, dims, preferred_element_type=F32)


def up_to(value, step):
    return -(-value // step) * step


def vmem():
    return pl.BlockSpec(memory_space=pltpu.VMEM)


def anywhere():
    return pl.BlockSpec(memory_space=pl.ANY)


def smem():
    return pl.BlockSpec(memory_space=pltpu.SMEM)


class Shape:
    def __init__(self, parts, slots, copies):
        self.parts, self.slots, self.copies = parts, slots, copies
        self.groups = parts // slots
        self.pairs = [(k, g) for k in range(slots) for g in range(self.groups)]
        self.far = [(0, g) for g in range(1, self.groups)]
        self.far += [(k, 0) for k in range(1, slots)]
        self.far += [(k, g) for k in range(1, slots) for g in range(1, self.groups)]
        self.order = [(0, 0)] + self.far
        self.bits = []
        bit = copies // 2
        while bit:
            self.bits.append(bit)
            bit //= 2

    def source(self, mine, member, k, g):
        return lax.rem(mine - k + self.slots, self.slots) * self.groups + lax.rem(
            member - g + self.groups, self.groups
        )

    def mask(self, spot):
        return sum(bit for n, bit in enumerate(self.bits) if (spot >> n) & 1)


def run_all(copies):
    for copy in copies:
        copy.start()
    for copy in copies:
        copy.wait()


def weight_copies(shape, row, own, foreign, dest, sems):
    rows = own.shape[0]
    copies = [pltpu.make_async_copy(own, dest.at[0, pl.ds(0, rows), :], sems.at[0])]
    for k in range(1, shape.slots):
        near, far = foreign[2 * (k - 1) : 2 * k]
        half, size, _ = near.shape
        for spot in range(shape.copies):
            piece = near.at[spot] if spot < half else far.at[spot - half]
            at = pl.multiple_of(jnp.bitwise_xor(row, shape.mask(spot)) * size, 16)
            copies.append(
                pltpu.make_async_copy(
                    piece,
                    dest.at[k, pl.ds(at, size), :],
                    sems.at[1 + (k - 1) * shape.copies + spot],
                )
            )
    return copies


def project_kernel(shape, seq, sc, norm_ref, down_ref, ups_ref, own_tok, own_w, *rest):
    slots, groups, parts = shape.slots, shape.groups, shape.parts
    toks = rest[: parts - 1]
    foreign = rest[parts - 1 : parts - 1 + 2 * (slots - 1)]
    rest = rest[parts - 1 + 2 * (slots - 1) :]
    qkv_ref, n1_ref, stats_ref, inner_ref, rows_ref, upx_ref = rest[:6]
    tok_ref, weights, tok_sem, weight_sem = rest[6:]
    _, width, span = tok_ref.shape
    dim = parts * width
    head_rows = upx_ref.shape[2] // 3
    heads_here = head_rows // HEAD_DIM
    block = span // groups
    mine, member, row = sc[0], sc[1], sc[3]

    tok_copies = []
    for n, (k, g) in enumerate(shape.pairs):
        source = own_tok.at[mine] if n == 0 else toks[n - 1]
        tok_copies.append(
            pltpu.make_async_copy(
                source, tok_ref.at[shape.source(mine, member, k, g)], tok_sem.at[n]
            )
        )
    weight_list = weight_copies(shape, row, own_w, foreign, weights, weight_sem)
    for copy in tok_copies + weight_list:
        copy.start()
    for copy in tok_copies:
        copy.wait()

    def norm_step(c, carry):
        cols = pl.ds(pl.multiple_of(c * LANES, LANES), LANES)
        x = tok_ref[:, :, cols].reshape(dim, LANES).astype(F32)
        mean = jnp.mean(x, 0, keepdims=True)
        center = x - mean
        rstd = lax.rsqrt(jnp.mean(center * center, 0, keepdims=True) + EPS)
        n1 = center * rstd * norm_ref[:, 0:1] + norm_ref[:, 1:2]
        n1_ref[:, cols] = n1.astype(BF)
        stats_ref[0:1, cols] = mean
        stats_ref[1:2, cols] = rstd
        return carry

    lax.fori_loop(0, span // LANES, norm_step, 0)
    stats_ref[2:8, :] = jnp.zeros((6, span), F32)
    part_of = lax.broadcasted_iota(jnp.int32, (16, 3 * head_rows), 1) // head_rows
    for k in range(slots):
        up = ups_ref[k, 0:16, 0 : 3 * head_rows]
        lines = [jnp.where(part_of == j, up, jnp.zeros_like(up)) for j in range(3)]
        upx_ref[k] = jnp.concatenate(lines + [ups_ref[k, 16:32, 0 : 3 * head_rows]], 0)
    for copy in weight_list:
        copy.wait()

    def proj_step(c, carry):
        start = pl.multiple_of(c * CHUNK, CHUNK)
        cols = pl.ds(start, CHUNK)
        n1 = n1_ref[:, cols]
        rank = down_ref.shape[0]
        inner = mm(down_ref[...], n1)
        line = lax.broadcasted_iota(jnp.int32, (rank, CHUNK), 0)
        inner_x = jnp.where(line == 48, 1.0, 0.5 * inner).astype(BF)
        inner_ref[:, cols] = inner_x
        spot = lax.broadcasted_iota(jnp.int32, (HEAD_PAD - HEAD_DIM, CHUNK), 0)
        place = start + lax.broadcasted_iota(jnp.int32, (HEAD_PAD - HEAD_DIM, CHUNK), 1)
        tails = (
            jnp.where(spot == 0, 1.0, 0.0),
            jnp.where((spot == 0) & (place >= seq), -1e30, 0.0),
            jnp.zeros((HEAD_PAD - HEAD_DIM, CHUNK), F32),
        )
        for k in range(slots):
            proj = mm(weights[k, 0 : 3 * head_rows, :], n1) + mm(upx_ref[k], inner_x, TN)
            for j in range(3):
                for h in range(heads_here):
                    at = j * head_rows + h * HEAD_DIM
                    piece = jnp.concatenate([proj[at : at + HEAD_DIM, :], tails[j]], 0)
                    qkv_ref[j, k * heads_here + h, :, cols] = piece.astype(BF)
        return carry

    lax.fori_loop(0, span // CHUNK, proj_step, 0)

    for g in range(groups):
        rows_ref[g] = tok_ref[:, :, g * block : (g + 1) * block].reshape(dim, block)


def project(shape, seq, scalars, norm, down, ups, own_tok, toks, own_w, foreign):
    slots, groups, parts = shape.slots, shape.groups, shape.parts
    _, width, span = own_tok.shape
    head_rows = own_w.shape[0] // 3
    heads = slots * head_rows // HEAD_DIM
    dim = parts * width
    weight_rows = max([own_w.shape[0]] + [w.shape[1] * shape.copies for w in foreign])
    out = (
        jax.ShapeDtypeStruct((3, heads, HEAD_PAD, span), BF),
        jax.ShapeDtypeStruct((dim, span), BF),
        jax.ShapeDtypeStruct((8, span), F32),
        jax.ShapeDtypeStruct((down.shape[0], span), BF),
        jax.ShapeDtypeStruct((groups, dim, span // groups), BF),
        jax.ShapeDtypeStruct((slots, 64, 3 * head_rows), BF),
    )
    return pl.pallas_call(
        partial(project_kernel, shape, seq),
        out_shape=out,
        in_specs=[smem()] + [vmem()] * 3 + [anywhere()] * (2 + len(toks) + len(foreign)),
        out_specs=tuple(vmem() for _ in out),
        scratch_shapes=[
            pltpu.VMEM((parts, width, span), BF),
            pltpu.VMEM((slots, weight_rows, dim), BF),
            pltpu.SemaphoreType.DMA((parts,)),
            pltpu.SemaphoreType.DMA((1 + (slots - 1) * shape.copies,)),
        ],
        compiler_params=pltpu.CompilerParams(vmem_limit_bytes=48 * MIB),
        cost_estimate=pl.CostEstimate(flops=4 * 10**9, bytes_accessed=40 * 10**6, transcendentals=10**6),
        name="project",
    )(scalars, norm, down, ups, own_tok, own_w, *toks, *foreign)


def attend_kernel(slots, sc, qkv_ref, lse_ref, heads_ref, scr):
    span = scr.shape[1]
    head_rows = scr.shape[0] // slots
    h = pl.program_id(0)
    keys = qkv_ref[1, 0].T
    vals = qkv_ref[2, 0]
    at = pl.multiple_of(h * HEAD_DIM, 8)
    for c in range(span // CHUNK):
        cols = slice(c * CHUNK, (c + 1) * CHUNK)
        scores = mm(keys, qkv_ref[0, 0, :, cols]) * (SCALE * LOG2E)
        top = jnp.max(scores, 0, keepdims=True)
        raised = jnp.exp2(scores - top)
        total = jnp.sum(raised, 0, keepdims=True)
        out = mm(vals, raised.astype(BF)) / total
        scr[pl.ds(at, HEAD_DIM), cols] = out[0:HEAD_DIM, :]
        lse_ref[0, 0:1, cols] = top + jnp.log2(total)

    @pl.when(h == pl.num_programs(0) - 1)
    def _():
        for k in range(slots):
            heads_ref[k] = scr[k * head_rows : (k + 1) * head_rows, :].astype(BF)


def attend(shape, scalars, qkv):
    slots = shape.slots
    _, heads, _, span = qkv.shape
    head_rows = heads * HEAD_DIM // slots
    out = (
        jax.ShapeDtypeStruct((heads, 1, span), F32),
        jax.ShapeDtypeStruct((slots, head_rows, span), BF),
    )
    return pl.pallas_call(
        partial(attend_kernel, slots),
        grid=(heads,),
        out_shape=out,
        in_specs=[smem(), pl.BlockSpec((3, 1, HEAD_PAD, span), lambda h: (0, h, 0, 0))],
        out_specs=(
            pl.BlockSpec((1, 1, span), lambda h: (h, 0, 0)),
            pl.BlockSpec(out[1].shape, lambda h: (0, 0, 0)),
        ),
        scratch_shapes=[pltpu.VMEM((slots * head_rows, span), F32)],
        compiler_params=pltpu.CompilerParams(vmem_limit_bytes=40 * MIB),
        cost_estimate=pl.CostEstimate(flops=4 * 10**9, bytes_accessed=60 * 10**6, transcendentals=5 * 10**6),
        name="attend",
    )(scalars, qkv)


def load_factors(fac, both, base, hidden_rows, tail):
    blank = jnp.zeros((LANES - 32, hidden_rows), BF)
    both[0, base : base + hidden_rows, tail] = jnp.concatenate([fac[0:32, :], blank], 0).T
    spread = jnp.concatenate([fac[32:48, :], jnp.zeros((16, hidden_rows), BF), blank], 0)
    both[1, base : base + hidden_rows, tail] = spread.T


def hidden_units(both, n2x, gx, acc_out, acc_back, eug, rdg, tail):
    rows = both.shape[1]
    inner_t = n2x[:, tail].T
    thr_t = gx[:, tail].T

    def units(at):
        we_c = both[0, at, :]
        wr_c = both[1, at, :]
        pre = mm(n2x[...], we_c, NT)
        grad_act = mm(gx[...], wr_c, NT)
        square = pre * pre
        th = jnp.tanh(pre * (0.7978845608028654 + 0.035677408136300125 * square))
        half = 0.5 * (1.0 + th)
        act = (pre * half).astype(BF)
        slope = half + pre * (0.5 * (1.0 - th * th)) * (
            0.7978845608028654 + 0.10703222440890037 * square
        )
        grad_pre = (grad_act * slope).astype(BF)
        acc_out[...] += mm(act, wr_c)
        acc_back[...] += mm(grad_pre, we_c)
        eug[:, at] = mm(inner_t[0:16, :], grad_pre)
        rdg[:, at] = mm(thr_t[0:16, :], act)

    def step(c, carry):
        units(pl.ds(pl.multiple_of(c * UNITS, UNITS), UNITS))
        return carry

    lax.fori_loop(0, rows // UNITS, step, 0)
    if rows % UNITS:
        units(slice(rows // UNITS * UNITS, rows))


def normalise(hidden):
    mean = jnp.mean(hidden, 1, keepdims=True)
    center = hidden - mean
    rstd = lax.rsqrt(jnp.mean(center * center, 1, keepdims=True) + EPS)
    return center * rstd, rstd


def merge_copies(parts, merge_hbm, wm, dim, sems):
    rows = dim // parts
    return [
        pltpu.make_async_copy(
            merge_hbm.at[t, pl.ds(0, rows), :], wm.at[pl.ds(t * rows, rows), pl.ds(0, dim)], sems.at[t]
        )
        for t in range(parts)
    ]


def pick_block(parts, which):
    out = parts[0]
    for n in range(1, len(parts)):
        out = jnp.where(which == n, parts[n], out)
    return out


def hidden_kernel(
    shape, turn, sc, vec_ref, tab_ref, fac_ref, rows_ref, own_expand, own_reduce, merge_hbm, own_cot, own_heads, *rest
):
    slots, groups, parts = shape.slots, shape.groups, shape.parts
    cots, rest = rest[: parts - 1], rest[parts - 1 :]
    heads_hbm, rest = (own_heads,) + rest[: groups - 1], rest[groups - 1 :]
    pieces, rest = rest[: slots - 1], rest[slots - 1 :]
    layer_ref, back_ref, gm_ref, gw_ref = rest[:4]
    kept, rest = (rest[4:9], rest[9:]) if turn == 0 else (None, rest[4:])
    both, wm, heads_in, cot_in, n2x, gx, acc_out, acc_back, eug, rdg = rest[:10]
    heads_sem, cot_sem, own_sem, merge_sem, w_sem = rest[10:]
    _, head_rows, span = heads_in.shape
    block = span // groups
    dim = parts * head_rows
    hidden_rows = both.shape[1] // slots
    size = 2 * hidden_rows // shape.copies
    half = shape.copies // 2
    tail = slice(dim, dim + LANES)
    cols = pl.ds(0, dim)
    mine, member, valid, ident = sc[0], sc[1], sc[2], sc[4]

    small = []
    for n, (k, g) in enumerate(shape.pairs):
        source = own_cot.at[mine] if n == 0 else cots[n - 1]
        spot = shape.source(mine, member, k, g)
        small.append(pltpu.make_async_copy(source, cot_in.at[spot], cot_sem.at[n]))
    for g in range(groups):
        for k in range(slots):
            spot = lax.rem(member - g + groups, groups) + groups * lax.rem(mine + k, slots)
            small.append(
                pltpu.make_async_copy(heads_hbm[g].at[k], heads_in.at[spot], heads_sem.at[g, k])
            )
    merges = merge_copies(parts, merge_hbm, wm, dim, merge_sem)
    mlps = [
        pltpu.make_async_copy(source, both.at[n, pl.ds(0, hidden_rows), cols], own_sem.at[n])
        for n, source in enumerate((own_expand, own_reduce))
    ]
    for k in range(1, slots):
        for d in range(shape.copies):
            start = k * hidden_rows + d % half * size
            mlps.append(
                pltpu.make_async_copy(
                    pieces[k - 1].at[d],
                    both.at[d // half, pl.ds(start, size), cols],
                    w_sem.at[k, d],
                )
            )
    for copy in small + merges + mlps:
        copy.start()
    for k in range(slots):
        load_factors(fac_ref[k], both, k * hidden_rows, hidden_rows, tail)
    acc_out[...] = jnp.zeros_like(acc_out)
    acc_back[...] = jnp.zeros_like(acc_back)
    for copy in small:
        copy.wait()
    for t in range(parts):
        lines = cot_in[t, head_rows : head_rows + 16, 0:head_rows]
        lines = jnp.concatenate([lines, jnp.zeros((LANES - 16, head_rows), BF)], 0).T
        wm[t * head_rows : (t + 1) * head_rows, tail] = lines
    which = lax.rem(member + turn, groups)
    blocks = [slice(g * block, (g + 1) * block) for g in range(groups)]
    cot = pick_block([cot_in[:, 0:head_rows, at] for at in blocks], which)
    grads = cot.reshape(dim, block).T * valid.astype(F32).astype(BF)
    gx[:, 0:dim] = grads
    gx[:, tail] = (0.5 * mm(grads, tab_ref[2], NT)).astype(BF)
    heads = pick_block([heads_in[:, :, at] for at in blocks], which).reshape(dim, block).T
    for copy in merges:
        copy.wait()
    lane = lax.broadcasted_iota(jnp.int32, (block, LANES), 1)
    merged = mm(heads, wm[...])
    inner_m = (0.5 * merged[:, tail]).astype(BF)
    hidden = rows_ref[which].T.astype(F32) + merged[:, :dim] + mm(inner_m, tab_ref[0]) + vec_ref[0:1, :]
    unit, _ = normalise(hidden)
    n2 = (unit * vec_ref[2:3, :] + vec_ref[3:4, :]).astype(BF)
    n2x[:, 0:dim] = n2
    n2x[:, tail] = jnp.where(lane == 16, 1.0, 0.5 * mm(n2, tab_ref[1], NT)).astype(BF)
    if kept:
        for ref, value in zip(kept, (hidden, heads, inner_m, grads, wm[:, tail]), strict=True):
            ref[...] = value
    for copy in mlps:
        copy.wait()
    hidden_units(both, n2x, gx, acc_out, acc_back, eug, rdg, tail)

    inner_r = (0.5 * acc_out[:, tail]).astype(BF)
    thr_e = (0.5 * acc_back[:, tail]).astype(BF)
    layer = acc_out[:, 0:dim] + mm(inner_r, tab_ref[2])
    if kept:
        layer = layer + kept[0][...] + vec_ref[1:2, :]
    layer = layer.T.astype(BF)
    for t in range(parts):
        layer_ref[t] = layer[t * head_rows : (t + 1) * head_rows, :]
    back_ref[...] = (acc_back[:, 0:dim] + mm(thr_e, tab_ref[1])).astype(back_ref.dtype)
    whole = (
        mm(thr_e, n2x[:, 0:dim], TN)[0:16, :],
        mm(inner_r, gx[:, 0:dim], TN)[0:16, :],
    )
    ids = jnp.full((32, LANES), ident, jnp.int32).astype(F32)
    if turn:
        ids = jnp.zeros_like(ids)
    gw_ref[...] = jnp.concatenate([jnp.concatenate(whole, 0), ids], 1).astype(BF)
    blank = jnp.zeros((16, 2 * (dim + LANES) - 2 * hidden_rows), F32)
    for k in range(slots):
        at = slice(k * hidden_rows, (k + 1) * hidden_rows)
        line = jnp.concatenate([eug[:, at], rdg[:, at], blank], 1)
        gm_ref[k, 0:16, :] = line[:, 0 : dim + LANES].astype(BF)
        gm_ref[k, 16:32, :] = line[:, dim + LANES :].astype(BF)


def hidden_part(shape, turn, scalars, vec, tab, fac, rows, own_w, merge, own_cot, cots, heads, pieces):
    slots, groups, parts = shape.slots, shape.groups, shape.parts
    own_heads, others = heads
    _, head_rows, span = own_heads.shape
    block = span // groups
    dim = parts * head_rows
    hidden_rows = fac.shape[2]
    count = slots * hidden_rows
    out = (
        jax.ShapeDtypeStruct((parts, head_rows, block), BF),
        jax.ShapeDtypeStruct((block, dim), BF if turn else F32),
        jax.ShapeDtypeStruct((slots, 32, dim + LANES), BF),
        jax.ShapeDtypeStruct((32, dim + LANES), BF),
    )
    if turn == 0:
        out += (
            jax.ShapeDtypeStruct((block, dim), F32),
            jax.ShapeDtypeStruct((block, dim), BF),
            jax.ShapeDtypeStruct((block, LANES), BF),
            jax.ShapeDtypeStruct((block, dim), BF),
            jax.ShapeDtypeStruct((dim, LANES), BF),
        )
    inputs = 5 + len(cots) + len(others) + len(pieces)
    return pl.pallas_call(
        partial(hidden_kernel, shape, turn),
        out_shape=out,
        in_specs=[smem()] + [vmem()] * 4 + [anywhere()] * inputs,
        out_specs=tuple(vmem() for _ in out),
        scratch_shapes=[
            pltpu.VMEM((2, count, dim + LANES), BF),
            pltpu.VMEM((dim, dim + LANES), BF),
            pltpu.VMEM((parts, head_rows, span), BF),
            pltpu.VMEM((parts,) + own_cot.shape[1:], BF),
            pltpu.VMEM((block, dim + LANES), BF),
            pltpu.VMEM((block, dim + LANES), BF),
            pltpu.VMEM((block, dim + LANES), F32),
            pltpu.VMEM((block, dim + LANES), F32),
            pltpu.VMEM((16, count), F32),
            pltpu.VMEM((16, count), F32),
            pltpu.SemaphoreType.DMA((groups, slots)),
            pltpu.SemaphoreType.DMA((parts,)),
            pltpu.SemaphoreType.DMA((2,)),
            pltpu.SemaphoreType.DMA((parts,)),
            pltpu.SemaphoreType.DMA((slots, shape.copies)),
        ],
        compiler_params=pltpu.CompilerParams(vmem_limit_bytes=62 * MIB),
        cost_estimate=pl.CostEstimate(flops=10 * 10**9, bytes_accessed=60 * 10**6, transcendentals=10**6),
        name="hidden_part",
    )(scalars, vec, tab, fac, rows, *own_w, merge, own_cot, own_heads, *cots, *others, *pieces)


def branch_kernel(shape, sc, vec_ref, tab_ref, merge_hbm, *rest):
    slots, groups, parts = shape.slots, shape.groups, shape.parts
    inputs, rest = rest[: groups + 5], rest[groups + 5 :]
    resid_ref, back_ref, gw_ref, wm, sem, in_sem = rest[:6]
    held = rest[6:]
    own_back, hidden_ref, heads_ref, inner_ref, grads_ref, tails_ref = held[:6]
    others = held[6:]
    _, dim = hidden_ref.shape
    head_rows = dim // parts
    mine, ident = sc[0], sc[4]
    merges = merge_copies(parts, merge_hbm, wm, dim, sem)
    loads = [
        pltpu.make_async_copy(source, dest, in_sem.at[n])
        for n, (source, dest) in enumerate(zip(inputs, held, strict=True))
    ]
    for copy in loads + merges:
        copy.start()
    for copy in loads:
        copy.wait()
    total = own_back[...]
    for other in others:
        total = total + other[...].astype(F32)
    scaled = total * vec_ref[2:3, :]
    unit, rstd = normalise(hidden_ref[...])
    first = jnp.mean(scaled, 1, keepdims=True)
    second = jnp.mean(scaled * unit, 1, keepdims=True)
    grad_hidden = grads_ref[...].astype(F32) + rstd * (scaled - first - unit * second)
    branch = grad_hidden.astype(BF)
    thr_m = (0.5 * mm(branch, tab_ref[0], NT)).astype(BF)
    resid_ref[...] = grad_hidden.T
    whole = (
        mm(inner_ref[...], branch, TN)[0:16, :],
        mm(thr_m, heads_ref[...], TN)[0:16, :],
    )
    ids = jnp.full((32, LANES), ident, jnp.int32).astype(F32)
    gw_ref[...] = jnp.concatenate([jnp.concatenate(whole, 0), ids], 1).astype(BF)
    for copy in merges:
        copy.wait()
    grad_heads = (mm(branch, wm[...], NT) + mm(thr_m, tails_ref[...], NT)).T.astype(BF)
    for t in range(parts):
        at = slice(t * head_rows, (t + 1) * head_rows)
        back_ref[t % groups, lax.rem(t // groups - mine + slots, slots)] = grad_heads[at, :]


def branch_part(shape, scalars, vec, tab, kept, merge, others):
    slots, groups, parts = shape.slots, shape.groups, shape.parts
    block, dim = kept[0].shape
    out = (
        jax.ShapeDtypeStruct((dim, block), F32),
        jax.ShapeDtypeStruct((groups, slots, dim // parts, block), BF),
        jax.ShapeDtypeStruct((32, dim + LANES), BF),
    )
    return pl.pallas_call(
        partial(branch_kernel, shape),
        out_shape=out,
        in_specs=[smem()] + [vmem()] * 2 + [anywhere()] * (1 + len(kept) + len(others)),
        out_specs=tuple(vmem() for _ in out),
        scratch_shapes=[
            pltpu.VMEM((dim, dim), BF),
            pltpu.SemaphoreType.DMA((parts,)),
            pltpu.SemaphoreType.DMA((len(kept) + len(others),)),
        ]
        + [pltpu.VMEM(x.shape, x.dtype) for x in (*kept, *others)],
        compiler_params=pltpu.CompilerParams(vmem_limit_bytes=48 * MIB),
        cost_estimate=pl.CostEstimate(flops=2 * 10**9, bytes_accessed=10**7, transcendentals=0),
        name="branch_part",
    )(scalars, vec, tab, merge, *kept, *others)


def heads_back_kernel(shape, slot, sc, qkv_ref, lse_ref, own_dout, *rest):
    groups = shape.groups
    douts = (own_dout,) + rest[: groups - 1]
    out_ref, dout_rel, dot_scr, grad_scr, sem = rest[groups - 1 :]
    _, head_rows, block = dout_rel.shape
    span = groups * block
    heads_here = head_rows // HEAD_DIM
    member = sc[1]
    h = pl.program_id(0)

    @pl.when(h == 0)
    def _():
        copies = []
        for g in range(groups):
            source = own_dout.at[member, slot] if g == 0 else douts[g].at[slot]
            spot = lax.rem(member - g + groups, groups)
            copies.append(pltpu.make_async_copy(source, dout_rel.at[spot], sem.at[g]))
        run_all(copies)
        pad = jnp.zeros((HEAD_PAD - HEAD_DIM, block), F32)
        for g in range(groups):
            piece = dout_rel[g].astype(F32)
            for n in range(heads_here):
                one = jnp.concatenate([piece[n * HEAD_DIM : (n + 1) * HEAD_DIM, :], pad], 0)
                dot_scr[n, :, g * block : (g + 1) * block] = one.astype(BF)

    query_t = qkv_ref[0, 0]
    keys_t = qkv_ref[1, 0]
    query = query_t.T
    keys = keys_t.T
    vals = qkv_ref[2, 0].T
    dout_t = dot_scr[h]
    dout = dout_t.T
    dvals = jnp.zeros((span, HEAD_PAD), F32)
    dkeys = jnp.zeros((span, HEAD_PAD), F32)
    row = pl.multiple_of(h * HEAD_DIM, 8)
    for c in range(span // CHUNK):
        cols = slice(c * CHUNK, (c + 1) * CHUNK)
        scores = mm(keys, query_t[:, cols]) * (SCALE * LOG2E)
        probs = jnp.exp2(scores - lse_ref[0, 0:1, cols])
        dprobs = mm(vals, dout_t[:, cols])
        delta = jnp.sum(probs * dprobs, 0, keepdims=True)
        dscores = (probs * (dprobs - delta)).astype(BF)
        dvals += mm(probs.astype(BF), dout[cols, :])
        dkeys += mm(dscores, query[cols, :])
        dquery = mm(keys_t, dscores) * SCALE
        grad_scr[pl.ds(row, HEAD_DIM), cols] = dquery[0:HEAD_DIM, :]
    row = pl.multiple_of(row + head_rows, 8)
    grad_scr[pl.ds(row, HEAD_DIM), :] = (dkeys * SCALE).T[0:HEAD_DIM, :]
    row = pl.multiple_of(row + head_rows, 8)
    grad_scr[pl.ds(row, HEAD_DIM), :] = dvals.T[0:HEAD_DIM, :]

    @pl.when(h == heads_here - 1)
    def _():
        out_ref[...] = grad_scr[...].astype(BF)


def heads_back(shape, slot, scalars, qkv, lse, dout):
    own, others = dout
    groups, _, head_rows, block = own.shape
    span = groups * block
    heads_here = head_rows // HEAD_DIM
    return pl.pallas_call(
        partial(heads_back_kernel, shape, slot),
        grid=(heads_here,),
        out_shape=jax.ShapeDtypeStruct((3 * head_rows, span), BF),
        in_specs=[
            smem(),
            pl.BlockSpec((3, 1, HEAD_PAD, span), lambda h: (0, slot * heads_here + h, 0, 0)),
            pl.BlockSpec((1, 1, span), lambda h: (slot * heads_here + h, 0, 0)),
            anywhere(),
        ]
        + [anywhere()] * len(others),
        out_specs=pl.BlockSpec((3 * head_rows, span), lambda h: (0, 0)),
        scratch_shapes=[
            pltpu.VMEM((groups, head_rows, block), BF),
            pltpu.VMEM((heads_here, HEAD_PAD, span), BF),
            pltpu.VMEM((3 * head_rows, span), F32),
            pltpu.SemaphoreType.DMA((groups,)),
        ],
        compiler_params=pltpu.CompilerParams(vmem_limit_bytes=40 * MIB),
        cost_estimate=pl.CostEstimate(flops=10**9, bytes_accessed=40 * 10**6, transcendentals=0),
        name="heads_back",
    )(scalars, qkv, lse, own, *others)


def rank_back_kernel(shape, sc, down_ref, upx_ref, n1_ref, inner_ref, *rest):
    slots = shape.slots
    grads = rest[:slots]
    td_ref, tu_ref, thr_ref = rest[slots:]
    dim, span = n1_ref.shape
    head_rows = upx_ref.shape[2] // 3
    ident = sc[4]
    rank = down_ref.shape[0]
    spread = 3 * head_rows
    thr = jnp.zeros((rank, span), F32)
    row_of = lax.broadcasted_iota(jnp.int32, (rank, spread), 0) // 16
    part_of = lax.broadcasted_iota(jnp.int32, (rank, spread), 1) // head_rows
    for k in range(slots):
        thr = thr + mm(upx_ref[k], grads[k][...])
        ups = mm(inner_ref[...], grads[k][...], NT)
        ups = jnp.where(row_of == part_of, ups, 0.0)
        ups = ups[0:16, :] + ups[16:32, :] + ups[32:48, :]
        blank = jnp.zeros((16, dim + LANES - spread), F32)
        tu_ref[k] = jnp.concatenate([ups, blank], 1).astype(BF)
    line = lax.broadcasted_iota(jnp.int32, (rank, span), 0)
    thr_b = jnp.where(line < 48, 0.5 * thr, 0.0).astype(BF)
    thr_ref[...] = thr_b
    downs = mm(thr_b, n1_ref[...], NT)
    ids = jnp.full((48, LANES), ident, jnp.int32).astype(F32)
    td_ref[...] = jnp.concatenate([downs[0:48, :], ids], 1).astype(BF)


def rank_back(shape, scalars, down, upx, n1, inner, grads):
    slots = shape.slots
    dim, span = n1.shape
    out = (
        jax.ShapeDtypeStruct((48, dim + LANES), BF),
        jax.ShapeDtypeStruct((slots, 16, dim + LANES), BF),
        jax.ShapeDtypeStruct((down.shape[0], span), BF),
    )
    return pl.pallas_call(
        partial(rank_back_kernel, shape),
        out_shape=out,
        in_specs=[smem()] + [vmem()] * (4 + slots),
        out_specs=(vmem(), vmem(), vmem()),
        compiler_params=pltpu.CompilerParams(vmem_limit_bytes=40 * MIB),
        cost_estimate=pl.CostEstimate(flops=10**9, bytes_accessed=40 * 10**6, transcendentals=0),
        name="rank_back",
    )(scalars, down, upx, n1, inner, *grads)


def norm_back_kernel(shape, sc, norm_ref, down_ref, thr_ref, stats_ref, rows_ref, resid_ref, own_w, *rest):
    slots, groups, parts = shape.slots, shape.groups, shape.parts
    foreign = rest[: 2 * (slots - 1)]
    rest = rest[2 * (slots - 1) :]
    grads = rest[:slots]
    out_ref, weights, e1_scr, sem = rest[slots:]
    _, dim, block = rows_ref.shape
    span = groups * block
    width = dim // parts
    spread = own_w.shape[0]
    member, row = sc[1], sc[3]
    run_all(weight_copies(shape, row, own_w, foreign, weights, sem))

    def final_step(c, carry):
        cols = pl.ds(pl.multiple_of(c * CHUNK, CHUNK), CHUNK)
        total = mm(down_ref[...], thr_ref[:, cols], TN)
        for k in range(slots):
            total = total + mm(weights[k, 0:spread, :], grads[k][:, cols], TN)
        e1_scr[:, cols] = total * norm_ref[:, 0:1]
        return carry

    lax.fori_loop(0, span // CHUNK, final_step, 0)
    for g in range(groups):
        cols = slice(g * block, (g + 1) * block)
        e1 = e1_scr[:, cols]
        first = jnp.sum(e1, 0, keepdims=True)
        mean, rstd = stats_ref[0:1, cols], stats_ref[1:2, cols]
        unit = (rows_ref[g].astype(F32) - mean) * rstd
        second = jnp.sum(e1 * unit, 0, keepdims=True)
        lines = []
        for value in (first, second, mean, rstd):
            high = value.astype(BF).astype(F32)
            lines += [high, value - high]
        lines = jnp.concatenate(lines + [jnp.zeros((8, block), F32)], 0).astype(BF)
        e1 = e1 + resid_ref[...] * (jnp.where(member == g, 1.0, 0.0) / rstd)
        for t in range(parts):
            out_ref[t, 0:width, cols] = e1[t * width : (t + 1) * width, :].astype(BF)
            out_ref[t, width : width + 16, cols] = lines


def norm_back(shape, scalars, norm, down, thr, stats, rows, resid, own_w, foreign, grads):
    slots, parts = shape.slots, shape.parts
    groups, dim, block = rows.shape
    span = groups * block
    weight_rows = max([own_w.shape[0]] + [w.shape[1] * shape.copies for w in foreign])
    return pl.pallas_call(
        partial(norm_back_kernel, shape),
        out_shape=jax.ShapeDtypeStruct((parts, dim // parts + 16, span), BF),
        in_specs=[smem()] + [vmem()] * 6 + [anywhere()] * (1 + len(foreign)) + [vmem()] * slots,
        out_specs=vmem(),
        scratch_shapes=[
            pltpu.VMEM((slots, weight_rows, dim), BF),
            pltpu.VMEM((dim, span), F32),
            pltpu.SemaphoreType.DMA((1 + (slots - 1) * shape.copies,)),
        ],
        compiler_params=pltpu.CompilerParams(vmem_limit_bytes=48 * MIB),
        cost_estimate=pl.CostEstimate(flops=10**9, bytes_accessed=40 * 10**6, transcendentals=0),
        name="norm_back",
    )(scalars, norm, down, thr, stats, rows, resid, own_w, *foreign, *grads)


def tokens_kernel(shape, seq, img_ref, held, out_ref):
    slots, groups, parts = shape.slots, shape.groups, shape.parts
    _, width, span = img_ref.shape
    dim = parts * width
    for n in range(slots):
        total = held[n * groups].astype(F32)
        lines = total[width : width + 16, :]
        mean = lines[4:5, :] + lines[5:6, :]
        rstd = lines[6:7, :] + lines[7:8, :]
        for g in range(1, groups):
            total = total + held[n * groups + g].astype(F32)
        first = (total[width : width + 1, :] + total[width + 1 : width + 2, :]) / dim
        second = (total[width + 2 : width + 3, :] + total[width + 3 : width + 4, :]) / dim
        unit = (img_ref[n].astype(F32) - mean) * rstd
        grad = rstd * (total[0:width, :] - first - unit * second)
        out_ref[:, n * seq : (n + 1) * seq] = grad[:, 0:seq]


def tokens_result(shape, seq, images, last):
    _, width, _ = images.shape
    return pl.pallas_call(
        partial(tokens_kernel, shape, seq),
        out_shape=jax.ShapeDtypeStruct((width, shape.slots * seq), F32),
        in_specs=[vmem(), vmem()],
        out_specs=vmem(),
        compiler_params=pltpu.CompilerParams(vmem_limit_bytes=40 * MIB),
        cost_estimate=pl.CostEstimate(flops=10**5, bytes_accessed=10**5, transcendentals=0),
        name="tokens_result",
    )(images, last)


def layer_kernel(shape, seq, sc, *rest):
    groups = shape.groups
    turns, out_ref = rest[:groups], rest[groups]
    for n in range(shape.slots):
        blocks = []
        for at in range(groups):
            total = turns[0][n * groups + at].astype(F32)
            for g in range(1, groups):
                total = total + turns[g][n * groups + (at - g) % groups].astype(F32)
            blocks.append(total)
        image = jnp.concatenate(blocks, 1)
        out_ref[:, n * seq : (n + 1) * seq] = image[:, 0:seq].astype(BF)


def layer_result(shape, seq, scalars, layers):
    _, width, _ = layers[0].shape
    return pl.pallas_call(
        partial(layer_kernel, shape, seq),
        out_shape=jax.ShapeDtypeStruct((width, shape.slots * seq), BF),
        in_specs=[smem()] + [vmem()] * len(layers),
        out_specs=vmem(),
        compiler_params=pltpu.CompilerParams(vmem_limit_bytes=40 * MIB),
        cost_estimate=pl.CostEstimate(flops=10**5, bytes_accessed=10**5, transcendentals=0),
        name="layer_result",
    )(scalars, *layers)


def summed(terms_ref, first, rows, adapter, count):
    images, _, cols = terms_ref.shape
    lines = slice(first, first + rows)
    total = jnp.zeros((rows, cols), F32)
    for e in range(images):
        which = terms_ref[e, 0:1, cols - 1 : cols].astype(F32)
        chosen = jnp.where(jnp.abs(which - adapter * count) < 0.5, 1.0, 0.0)
        total = total + terms_ref[e, lines, :].astype(F32) * chosen
    return total


def block_terms_kernel(count, padded, terms_ref, merge_ref, expand_ref, reduce_ref, eu_ref, rd_ref, md_ref):
    adapters, _, dim = merge_ref.shape
    hidden = eu_ref.shape[2]
    for a in range(adapters):
        whole = summed(terms_ref, 0, 64, a, count)
        for n, ref in enumerate((merge_ref, expand_ref, reduce_ref, md_ref)):
            ref[a] = whole[16 * n : 16 * n + 16, 0:dim]
        parts = summed(terms_ref, 64, 32, a, count)
        parts = jnp.concatenate([parts[0:16, :], parts[16:32, :]], 1)
        eu_ref[a] = parts[:, 0:hidden]
        rd_ref[a] = parts[:, padded : padded + hidden]


def triple_terms_kernel(count, terms_ref, down_ref, up_ref):
    _, adapters, _, dim = down_ref.shape
    rows = up_ref.shape[3]
    for a in range(adapters):
        downs = summed(terms_ref, 0, 48, a, count)
        ups = summed(terms_ref, 48, 16, a, count)
        for j in range(3):
            down_ref[j, a] = downs[16 * j : 16 * j + 16, 0:dim]
            up_ref[j, a] = ups[:, j * rows : (j + 1) * rows]


def by_adapter(kernel, terms, shapes, name):
    out = tuple(jax.ShapeDtypeStruct(one, F32) for one in shapes)
    return pl.pallas_call(
        kernel,
        out_shape=out,
        in_specs=[vmem()],
        out_specs=tuple(vmem() for _ in out),
        compiler_params=pltpu.CompilerParams(vmem_limit_bytes=40 * MIB),
        cost_estimate=pl.CostEstimate(flops=10**5, bytes_accessed=10**5, transcendentals=0),
        name=name,
    )(terms)


def shards(
    tokens,
    cotangent,
    adapter_index,
    valid_image,
    first_gain,
    first_shift,
    triple_weight,
    triple_bias,
    triple_down,
    triple_up,
    merge_weight,
    merge_bias,
    merge_down,
    merge_up,
    second_gain,
    second_shift,
    expand_weight,
    expand_bias,
    expand_down,
    expand_up,
    reduce_weight,
    reduce_bias,
    reduce_down,
    reduce_up,
    *,
    parts,
    copies,
):
    slots = adapter_index.shape[0]
    shape = Shape(parts, slots, copies)
    groups = shape.groups
    seq = tokens.shape[0] // slots
    width = tokens.shape[1]
    dim = width * parts
    head_rows = triple_weight.shape[2]
    adapters = triple_down.shape[1]
    span = up_to(seq, CHUNK)
    block = span // groups
    place = lax.axis_index("tensor")
    row = lax.axis_index("dp")
    mine, member = place // groups, place % groups

    def at(x, n, axis=0):
        return lax.dynamic_index_in_dim(x, n, axis, False)

    def jump(x, k, g):
        perm = [
            (s, ((s // groups + k) % slots) * groups + (s % groups + g) % groups)
            for s in range(parts)
        ]
        return lax.ppermute(x, "tensor", perm)

    def swap(x):
        return lax.all_to_all(x, "tensor", 0, 0)

    def spread_images(x):
        first = [at(x, mine)] + [jump(at(x, (mine + k) % slots), k, 0) for k in range(1, slots)]
        out = []
        for x_k in first:
            out.append(x_k)
            out += [jump(x_k, 0, g) for g in range(1, groups)]
        return out

    def cross(x, bit):
        return lax.ppermute(x, "dp", [(d, d ^ bit) for d in range(copies)])

    def widen(near, bits):
        for bit in bits:
            near = jnp.concatenate([near, cross(near, bit)], 0)
        return near

    def hyper(near, order):
        near = widen(near, order[:-1])
        return [near, cross(near, order[-1])]

    def after(x, *others):
        return lax.optimization_barrier((x, *others))[0]

    def images_of(x):
        flat = x.T
        return jnp.stack(
            [
                jnp.pad(flat[:, n * seq : (n + 1) * seq], ((0, 0), (0, span - seq)))
                for n in range(slots)
            ]
        )

    images = images_of(tokens)
    tok_first = [at(images, (mine + k) % slots) for k in range(slots)]
    tok_first, adapter_index, triple_weight, valid_image, expand_weight, reduce_weight = (
        lax.optimization_barrier(
            (tok_first, adapter_index, triple_weight, valid_image, expand_weight, reduce_weight)
        )
    )
    toks = [tok_first[0]] + [jump(tok_first[k], k, 0) for k in range(1, slots)]
    ready = toks[slots - 1]
    toks = [x if g == 0 else jump(x, 0, g) for x in toks for g in range(groups)][1:]

    index = at(adapter_index, mine)
    valid = at(valid_image, mine)
    scalars = jnp.stack([mine, member, valid, row, index, place]).astype(jnp.int32)

    flat_triple = triple_weight.transpose(0, 2, 1).reshape(3 * head_rows, dim)
    piece_rows = up_to(3 * head_rows, 16 * copies) // copies
    padded = jnp.pad(flat_triple, ((0, piece_rows * copies - 3 * head_rows), (0, 0)))
    my_piece = lax.dynamic_slice_in_dim(padded, row * piece_rows, piece_rows, 0)

    def up_pack(which):
        table = at(triple_up, which, 1).transpose(1, 0, 2).reshape(16, 3 * head_rows)
        bias = jnp.pad(triple_bias.reshape(1, 3 * head_rows), ((0, 15), (0, 0)))
        return jnp.pad(jnp.concatenate([table, bias], 0), ((0, 0), (0, dim - 3 * head_rows)))

    foreign, ups, arrived = [], [up_pack(index)], [ready]
    for k in range(1, slots):
        packed = up_pack(at(adapter_index, (mine - k) % slots))
        got = jump(jnp.concatenate([my_piece, packed], 0), -k, 0)
        arrived.append(got)
        ups.append(got[piece_rows:])
        foreign += hyper(got[None, :piece_rows], shape.bits)
    ups = jnp.stack(ups)
    ready = after(*arrived, toks[-1])

    merge_rows = up_to(width, 16 * copies) // copies
    merge_piece = lax.dynamic_slice_in_dim(
        jnp.pad(merge_weight, ((0, merge_rows * copies - width), (0, 0))), row * merge_rows, merge_rows, 0
    )
    hidden_here = reduce_weight.shape[0]
    hidden_rows = up_to(hidden_here, 8 * copies)
    extra = ((0, hidden_rows - hidden_here), (0, 0))
    mlp_rows = 2 * hidden_rows // copies
    half = copies // 2

    def mlp_part(x):
        return lax.dynamic_slice_in_dim(jnp.pad(x, extra), (row % half) * mlp_rows, mlp_rows, 0)

    my_w = jnp.where(row < half, mlp_part(expand_weight.T), mlp_part(reduce_weight))
    natural = ((1, 0, None),)
    near_masks = list(range(0, copies, 2))
    merge_all = lax.all_gather(merge_piece, ("tensor", "dp")).reshape(parts, merge_rows * copies, dim)
    late_w = after(my_w, ready)
    pieces = [jump(late_w, -k, 0) for k in range(1, slots)]
    own_expand = jnp.pad(expand_weight.T, extra)
    own_reduce = jnp.pad(reduce_weight, extra)

    down = jnp.pad(at(triple_down, index, 1).transpose(0, 2, 1).reshape(48, dim), ((0, 16), (0, 0)))
    norm = jnp.pad(jnp.stack([first_gain, first_shift], 1).astype(F32), ((0, 0), (0, 6)))

    late_index = adapter_index

    def factor_pack(which):
        def lanes(x):
            return jnp.pad(x, ((0, 16 - x.shape[0]), (0, hidden_rows - x.shape[1])))

        return jnp.concatenate(
            [lanes(at(expand_up, which)), lanes(expand_bias[None, :]), lanes(at(reduce_down, which).T)], 0
        )

    packs = [factor_pack(at(late_index, (mine - k) % slots)) for k in range(slots)]
    late = index
    tab = jnp.stack(
        [
            jnp.pad(x, ((0, LANES - 16), (0, 0)))
            for x in (at(merge_up, late), at(expand_down, late).T, at(reduce_up, late))
        ]
    )
    vec = jnp.pad(
        jnp.stack([merge_bias, reduce_bias, second_gain, second_shift]).astype(F32), ((0, 4), (0, 0))
    )

    merge_lines = [at(merge_down, late_index[n]).T for n in range(slots)]
    merge_lines = jnp.pad(jnp.stack(merge_lines), ((0, 0), (0, 0), (0, span - width)))
    cot_parts = jnp.concatenate([images_of(after(cotangent, adapter_index)), merge_lines], 1)

    def trade(x):
        return x, [jump(at(x, (member + g) % groups), 0, g) for g in range(1, groups)]

    begin = after(scalars, own_expand, own_reduce, tab, vec, cot_parts, *packs)
    qkv, n1, stats, inner, rows, upx = project(
        shape, seq, begin, norm, down, ups, images, toks, flat_triple, foreign
    )
    own_cot = after(at(cot_parts, mine), ready)
    cots = {(0, g): jump(own_cot, 0, g) for g in range(1, groups)}
    pieces, cot_parts, packs = lax.optimization_barrier((pieces, cot_parts, packs, stats))[:3]
    begin = after(scalars, cot_parts, *pieces)
    cots.update({(k, 0): jump(at(cot_parts, (mine + k) % slots), k, 0) for k in range(1, slots)})
    fac = [packs[0]] + [jump(packs[k], -k, 0) for k in range(1, slots)]
    pieces = [lax.all_gather(x, "dp") for x in pieces]
    lse, heads = attend(shape, begin, qkv)
    cots, fac = lax.optimization_barrier((cots, fac, lse))[:2]
    heads = (heads, [jump(heads, 0, g) for g in range(1, groups)])
    fac = jnp.stack(fac)
    cots.update({(k, g): jump(cots[k, 0], 0, g) for k in range(1, slots) for g in range(1, groups)})
    cots = [cots[pair] for pair in shape.pairs[1:]]
    layers, near, gms, gws = [None] * groups, [], [], []
    for turn in list(range(1, groups)) + [0]:
        begin = scalars
        layers[turn], back, gm, gw, *kept = hidden_part(
            shape,
            turn,
            begin,
            vec,
            tab,
            fac,
            rows,
            (own_expand, own_reduce),
            merge_all,
            cot_parts,
            cots,
            heads,
            pieces,
        )
        gms.append(gm)
        gws.append(gw)
        if turn:
            near.append(jump(back, 0, turn))
            scalars = after(scalars, back)
    near, layers[1:], kept = lax.optimization_barrier((near, layers[1:], kept))
    layers[1:] = [swap(x) for x in layers[1:]]
    resid, back, gw_branch = branch_part(
        shape, scalars, vec, tab, [back] + kept, merge_all, near
    )
    dout = trade(back)

    def spread_rows(x):
        share = x.shape[0] // copies
        own = lax.dynamic_slice_in_dim(x, row * share, share, 0)
        return jnp.stack([own] + [jump(own, k, g) for k, g in shape.pairs[1:]])

    def members_sum(x, beside):
        out, rows = [], x.shape[0]
        for k in range(slots):
            both = jnp.concatenate([x, beside[k]], 0)
            both = jump(both, k, 0) if k else both
            total = both[:rows].astype(F32)
            for g in range(1, groups):
                total = total + jump(x, k, g).astype(F32)
            out.append(jnp.concatenate([total.astype(BF), both[rows:]], 0))
        return jnp.stack(out)

    layers[0] = swap(layers[0])
    grads = [heads_back(shape, 0, after(scalars, *layers[1:]), qkv, lse, dout)]
    gms, gws, gw_branch, begin = lax.optimization_barrier((gms, gws, gw_branch, scalars, grads[0]))[:4]
    gm = sum(x.astype(F32) for x in gms).astype(BF)
    gw = sum(x.astype(F32) for x in gws).astype(BF)
    gm = members_sum(jnp.concatenate([gw_branch[0:16], gw, gw_branch[16:32]], 0), gm)
    for k in range(1, slots):
        grads.append(heads_back(shape, k, after(begin, layers[0]), qkv, lse, dout))
    gm = after(gm, grads[-1])
    td, tu, thr = rank_back(shape, after(scalars, gm), down, upx, n1, inner, grads)
    td = members_sum(td, tu)
    last = norm_back(shape, scalars, norm, down, thr, stats, rows, resid, flat_triple, foreign, grads)
    last, td = lax.optimization_barrier((last, td))
    last = swap(last)
    gm = lax.all_gather(gm, "dp", tiled=True)
    near = jnp.concatenate([td] + [cross(td, mask) for mask in near_masks[1:]], 0)
    merge_up_grad, expand_down_grad, reduce_up_grad, expand_up_grad, reduce_down_grad, merge_down_grad = by_adapter(
        partial(block_terms_kernel, groups, hidden_rows),
        gm,
        ((adapters, 16, dim),) * 3 + ((adapters, 16, hidden_here),) * 2 + ((adapters, 16, dim),),
        "block_terms",
    )
    merge_down_grad = lax.dynamic_slice_in_dim(merge_down_grad, place * width, width, 2)
    td = jnp.concatenate([near, cross(near, 1)], 0)
    layer_out = layer_result(shape, seq, after(scalars, gm), layers).T
    downs, triple_up_grad = by_adapter(
        partial(triple_terms_kernel, groups),
        td,
        ((3, adapters, 16, dim), (3, adapters, 16, head_rows)),
        "triple_terms",
    )
    tokens_grad = tokens_result(shape, seq, after(images, downs, merge_up_grad, layer_out), last).T

    return (
        layer_out,
        tokens_grad,
        downs.transpose(0, 1, 3, 2),
        triple_up_grad,
        merge_down_grad.transpose(0, 2, 1),
        merge_up_grad,
        expand_down_grad.transpose(0, 2, 1),
        expand_up_grad,
        reduce_down_grad.transpose(0, 2, 1),
        reduce_up_grad,
    )


def solution(mesh):
    in_specs = (
        P("dp", "tensor"),
        P("dp", "tensor"),
        P("dp"),
        P("dp"),
        P(),
        P(),
        P(None, None, "tensor"),
        P(None, "tensor"),
        P(),
        P(None, None, None, "tensor"),
        P("tensor", None),
        P(),
        P(None, "tensor", None),
        P(),
        P(),
        P(),
        P(None, "tensor"),
        P("tensor"),
        P(),
        P(None, None, "tensor"),
        P("tensor", None),
        P(),
        P(None, "tensor", None),
        P(),
    )
    out_specs = (
        P("dp", "tensor"),
        P("dp", "tensor"),
        P(),
        P(None, None, None, "tensor"),
        P(None, "tensor", None),
        P(),
        P(),
        P(None, None, "tensor"),
        P(None, "tensor", None),
        P(),
    )
    return jax.shard_map(
        partial(shards, parts=mesh.shape["tensor"], copies=mesh.shape["dp"]),
        mesh=mesh,
        in_specs=in_specs,
        out_specs=out_specs,
        check_vma=False,
    )
```
